256 devices in a mesh: dp: 16 (over z, y_hi), shard: 16 (over y_lo, x, core).
Axes of the slice: x: 4, y: 4 (y_hi: 2, y_lo: 2; y = y_hi * 2 + y_lo), z: 8, core: 2. Of those that a mesh axis runs over, the one named last changes fastest.
Arguments:
- hid_teacher: bfloat16 [8192, 2048], P(('dp', 'shard')), may hold values from -40 to 40
- hid_student: bfloat16 [8192, 2048], P(('dp', 'shard')), may hold values from -40 to 40
- proj_teacher: bfloat16 [2048, 384], P('shard'), may hold values from -0.176776695 to 0.176776695
- proj_student: bfloat16 [2048, 384], P('shard'), may hold values from -0.125 to 0.125
- proto_teacher: bfloat16 [384, 65536], P(None, 'shard'), may hold values from -0.61237244 to 0.61237244
- proto_student: bfloat16 [384, 65536], P(None, 'shard'), may hold values from -0.61237244 to 0.61237244
Outputs:
- loss: float32 [], replicated
- grad_proj: float32 [2048, 384], P('shard')
- grad_proto: float32 [384, 65536], P('dp', 'shard')
The draws below stay inside these ranges and needn't reach their ends.
All inputs are finite; a program needn't handle non-finite values.
Results may differ from the reference program's by a relative error of at most 0.003.
The reference program's roundings to bfloat16 on the way (of `z_t`, `z_s`, `v_t`, `v_s`, `grad_logits` and `dy`) count: a program that leaves them out, or rounds other values in their place, can miss the bound.
Values may be sent and summed in bfloat16 or wider, within the bound.
No kernel may reach another device: no remote copies, remote signals or barrier semaphores. Data moves between devices by JAX's collectives and lax.ppermute only.
A program may use at most 128 MiB of HBM per device.

```python
import math
import jax
import jax.numpy as jnp
from jax import lax

HID = 2048
BOT = 384
PROTO = 65536
ITERS = 3
ROWS = 8192
GRAD_SCALE = 256
N_SHARD = 16


def activations(key):
    key_scale, key_base = jax.random.split(key, 2)
    scales = jnp.exp(jax.random.uniform(key_scale, (ROWS, 1), jnp.float32, 0.0, math.log(10.0)))
    base = jnp.clip(jax.random.normal(key_base, (ROWS, HID), jnp.float32), -4.0, 4.0)
    return base * scales


def prototypes(key):
    key_scale, key_base = jax.random.split(key, 2)
    scales = jnp.exp(jax.random.uniform(key_scale, (1, PROTO), jnp.float32, math.log(0.3), math.log(3.0)))
    base = jnp.clip(jax.random.normal(key_base, (BOT, PROTO), jnp.float32), -4.0, 4.0)
    limit = 11.9 / math.sqrt(BOT)
    return jnp.clip(base * scales / math.sqrt(BOT), -limit, limit)


def teacher_basis(key):
    key_hid, key_bot = jax.random.split(key)
    hid_dirs = jnp.clip(jax.random.normal(key_hid, (8, HID), jnp.float32), -3.0, 3.0)
    bot_dirs = jnp.clip(jax.random.normal(key_bot, (8, BOT), jnp.float32), -3.0, 3.0)
    return (hid_dirs, bot_dirs)


def bumps(key, count, lowest, highest):
    key_center, key_sharp, key_height = jax.random.split(key, 3)
    centers = jax.random.uniform(key_center, (1, 8), jnp.float32, 0.0, 1.0)
    sharpness = jnp.exp(jax.random.uniform(key_sharp, (1, 8), jnp.float32, math.log(2.5), math.log(25.0)))
    heights = jnp.exp(jax.random.uniform(key_height, (1, 8), jnp.float32, math.log(lowest), math.log(highest)))
    position = jnp.arange(count, dtype=jnp.float32)[:, None] / count
    return heights * jnp.exp((jnp.cos(2.0 * math.pi * (position - centers)) - 1.0) * sharpness)


def draw_hid_teacher(key, part):
    hid_dirs, bot_dirs = teacher_basis(jax.random.fold_in(key, 97))
    key = jax.random.fold_in(key, 11)
    key_mix, key_jitter, key_first = jax.random.split(key, 3)
    struct_scale = jnp.exp(jax.random.uniform(key_first, (ROWS, 1), jnp.float32, 0.0, math.log(8.0)))
    weights = bumps(key_mix, ROWS, 0.5, 2.0)
    jitter = jnp.clip(jax.random.normal(key_jitter, (ROWS, HID), jnp.float32), -3.0, 3.0)
    jitter_scale = struct_scale
    shared = jnp.zeros((ROWS, HID), jnp.float32)
    for member in range(8):
        shared = shared + weights[:, member:member + 1] * hid_dirs[member][None, :]
    return jnp.clip(shared * struct_scale + jitter * jitter_scale, -39.0, 39.0).astype(jnp.bfloat16)


def draw_hid_student(key, part):
    key = jax.random.fold_in(key, 23)
    return activations(key).astype(jnp.bfloat16)


def draw_proj_teacher(key, part):
    hid_dirs, bot_dirs = teacher_basis(jax.random.fold_in(key, 97))
    key = jax.random.fold_in(key, 53)
    jitter = jnp.clip(jax.random.normal(key, (HID, BOT), jnp.float32), -4.0, 4.0) / math.sqrt(HID)
    shared = jnp.zeros((HID, BOT), jnp.float32)
    for member in range(8):
        shared = shared + hid_dirs[member][:, None] * bot_dirs[member][None, :]
    limit = 8.0 / math.sqrt(HID)
    return jnp.clip(jitter + shared * (3.0 / HID), -limit, limit).astype(jnp.bfloat16)


def draw_proto_teacher(key, part):
    hid_dirs, bot_dirs = teacher_basis(jax.random.fold_in(key, 97))
    key = jax.random.fold_in(key, 37)
    key_mix, key_jitter, key_scale = jax.random.split(key, 3)
    mixing = bumps(key_mix, PROTO, 0.5, 2.0)
    jitter = jnp.clip(jax.random.normal(key_jitter, (BOT, PROTO), jnp.float32), -3.0, 3.0)
    col_scale = jnp.exp(jax.random.uniform(key_scale, (1, PROTO), jnp.float32, math.log(0.4), math.log(2.0)))
    shared = jnp.zeros((BOT, PROTO), jnp.float32)
    for member in range(8):
        shared = shared + bot_dirs[member][:, None] * mixing[:, member][None, :]
    limit = 11.9 / math.sqrt(BOT)
    return jnp.clip((shared * 0.6 + jitter) * col_scale / math.sqrt(BOT), -limit, limit).astype(jnp.bfloat16)


def draw_proto_student(key, part):
    key = jax.random.fold_in(key, 41)
    return prototypes(key).astype(jnp.bfloat16)


def levels(key, shape, cuts, low, high):
    factor_of, own = 1.0, jax.random.fold_in(key, 6)
    for dim, parts in cuts:
        draws = jnp.exp(jax.random.uniform(jax.random.fold_in(own, dim), (parts,), jnp.float32, low / len(cuts), high / len(cuts)))
        factor_of = factor_of * jnp.repeat(draws, shape[dim] // parts).reshape([-1 if axis == dim else 1 for axis in range(len(shape))])
    return factor_of


def gaussian(stream_key, dims, scale, most, cuts=(), held_as=jnp.bfloat16):
    entries = jax.random.normal(stream_key, dims, jnp.float32) * scale
    if len(cuts) > 0:
        entries = levels(stream_key, dims, cuts, -0.22, 0.18) * entries
    return jnp.clip(entries, min=-most, max=most).astype(held_as)


def setup_inputs(seed: int = 0) -> dict:
    seeds = jax.random.split(jax.random.key(seed), 7)
    return {
        "hid_teacher": draw_hid_teacher(jax.random.fold_in(seeds[6], 71), 0),
        "hid_student": draw_hid_student(jax.random.fold_in(seeds[6], 71), 0),
        "proj_teacher": draw_proj_teacher(jax.random.fold_in(seeds[6], 71), 0),
        "proj_student": gaussian(seeds[3], (HID, BOT), HID ** -0.5, 0.125, ((0, 16),)),
        "proto_teacher": draw_proto_teacher(jax.random.fold_in(seeds[6], 71), 0),
        "proto_student": draw_proto_student(jax.random.fold_in(seeds[6], 71), 0),
    }


TAU_T = 0.04
TAU_S = 0.1
EPS = 1e-06
ROW_DIMS = (((0,), (0,)), ((), ()))
COL_DIMS = (((1,), (1,)), ((), ()))

def unit_rows(proj_out):
    norm = jnp.sqrt(lax.optimization_barrier(jnp.sum(proj_out * proj_out, axis=1, keepdims=True)) + EPS)
    return (proj_out / norm, norm)

def unit_columns(weight):
    wide = weight.astype(jnp.float32)
    norm = jnp.sqrt(lax.optimization_barrier(jnp.sum(wide * wide, axis=0)) + EPS)
    return ((wide / norm).astype(jnp.bfloat16), norm)

def reference(hid_teacher, hid_student, proj_teacher, proj_student, proto_teacher, proto_student):
    y_t = jnp.dot(hid_teacher, proj_teacher, preferred_element_type=jnp.float32)
    z_t = unit_rows(y_t)[0].astype(jnp.bfloat16)
    y_s = jnp.dot(hid_student, proj_student, preferred_element_type=jnp.float32)
    u_s, norm_s = unit_rows(y_s)
    z_s = u_s.astype(jnp.bfloat16)
    v_t, _ = unit_columns(proto_teacher)
    v_s, col_norm = unit_columns(proto_student)
    blocks = N_SHARD
    width = PROTO // blocks
    vt_blocks = v_t.reshape(BOT, blocks, width).transpose(1, 0, 2)
    vs_blocks = v_s.reshape(BOT, blocks, width).transpose(1, 0, 2)
    norm_blocks = col_norm.reshape(blocks, width)

    def teacher_exp(vblock):
        return jnp.exp(jnp.dot(z_t, vblock, preferred_element_type=jnp.float32) / TAU_T)
    row_scale = jnp.ones((ROWS,), jnp.float32)
    col_scale = jnp.ones((blocks, width), jnp.float32)
    for step in range(ITERS):
        scale_now = row_scale

        def column_block(vblock):
            return 1.0 / lax.optimization_barrier(jnp.sum(scale_now[:, None] * teacher_exp(vblock), axis=0))
        col_scale = lax.map(column_block, vt_blocks)

        def add_rows(total, pair):
            return (total + lax.optimization_barrier(jnp.sum(teacher_exp(pair[0]) * pair[1][None, :], axis=1)), None)
        mass, _ = lax.scan(add_rows, jnp.zeros((ROWS,), jnp.float32), (vt_blocks, col_scale))
        row_scale = 1.0 / mass

    def add_exp(total, vblock):
        scores = jnp.dot(z_s, vblock, preferred_element_type=jnp.float32)
        return (total + lax.optimization_barrier(jnp.sum(jnp.exp(scores / TAU_S), axis=1)), None)
    expsum, _ = lax.scan(add_exp, jnp.zeros((ROWS,), jnp.float32), vs_blocks)

    def finish(carry, pieces):
        cross, dzhat = carry
        vt_block, vs_block, cs_block, norm_block = pieces
        target = row_scale[:, None] * teacher_exp(vt_block) * cs_block[None, :]
        scores = jnp.dot(z_s, vs_block, preferred_element_type=jnp.float32)
        prob = jnp.exp(scores / TAU_S) / expsum[:, None]
        grad_logits = (GRAD_SCALE / TAU_S * (prob - target)).astype(jnp.bfloat16)
        cross = cross + lax.optimization_barrier(jnp.sum(target * scores, axis=1))
        dzhat = dzhat + lax.dot_general(grad_logits, vs_block, COL_DIMS, preferred_element_type=jnp.float32)
        dproto = lax.dot_general(z_s, grad_logits, ROW_DIMS, preferred_element_type=jnp.float32)
        wide_v = vs_block.astype(jnp.float32)
        dots = lax.optimization_barrier(jnp.sum(wide_v * dproto, axis=0))
        grad_block = (dproto - wide_v * dots[None, :]) / norm_block[None, :]
        return ((cross, dzhat), grad_block)
    start = (jnp.zeros((ROWS,), jnp.float32), jnp.zeros((ROWS, BOT), jnp.float32))
    (cross, dzhat), grad_blocks = lax.scan(finish, start, (vt_blocks, vs_blocks, col_scale, norm_blocks))
    loss = jnp.mean(jnp.log(expsum) - cross / TAU_S)
    dy = ((dzhat - u_s * lax.optimization_barrier(jnp.sum(u_s * dzhat, axis=1, keepdims=True))) / norm_s).astype(jnp.bfloat16)
    grad_proj = lax.dot_general(hid_student, dy, ROW_DIMS, preferred_element_type=jnp.float32)
    grad_proto = grad_blocks.transpose(1, 0, 2).reshape(BOT, PROTO)
    return (loss, grad_proj, grad_proto)
```

```python
import jax
import jax.numpy as jnp
from jax import lax
from jax.sharding import Mesh, PartitionSpec as P

ITERS = 3
GRAD_SCALE = 256
TAU_T = 0.04
TAU_S = 0.1
EPS = 1e-06
LANES = 128
ROW_DIMS = (((0,), (0,)), ((), ()))
COL_DIMS = (((1,), (1,)), ((), ()))

DP = ("z", "yh")
SHARD = ("yl", "x", "c")
PLANE = ("yh", "yl", "x", "c")


def unit_rows(proj_out):
    norm = jnp.sqrt(jnp.sum(proj_out * proj_out, axis=1, keepdims=True) + EPS)
    return (proj_out / norm, norm)


def unit_columns(weight):
    wide = weight.astype(jnp.float32)
    norm = jnp.sqrt(jnp.sum(wide * wide, axis=0) + EPS)
    return ((wide / norm).astype(jnp.bfloat16), norm)


def spread(block, axes):
    count = lax.axis_size(axes)
    return lax.all_to_all(
        jnp.broadcast_to(block[None], (count,) + block.shape), axes, 0, 0, tiled=True
    )


def total(vector, axes):
    return jnp.sum(spread(vector.reshape(-1, LANES), axes), axis=0).reshape(vector.shape)


def scatter_sum(parts, axes):
    count = lax.axis_size(axes)
    own = parts.shape[0] // count
    blocks = parts.reshape((count, own) + parts.shape[1:])
    return jnp.sum(lax.all_to_all(blocks, axes, 0, 0, tiled=True), axis=0)


def norm_backward(dzhat, unit_s, norm_s):
    inner = jnp.sum(unit_s * dzhat, axis=1, keepdims=True)
    return ((dzhat - unit_s * inner) / norm_s).astype(jnp.bfloat16)


def local(hid_teacher, hid_student, proj_teacher, proj_student, proto_teacher, proto_student):
    rows, bot = hid_teacher.shape[0], proj_teacher.shape[1]
    half = proto_teacher.shape[1] // lax.axis_size("yh")
    side = lax.axis_index("yh")
    first = side * half
    v_t, _ = unit_columns(lax.dynamic_slice_in_dim(proto_teacher, first, half, 1))
    v_s, col_norm = unit_columns(lax.dynamic_slice_in_dim(proto_student, first, half, 1))

    y_t = jnp.dot(
        hid_teacher,
        lax.all_gather(proj_teacher, SHARD, axis=0, tiled=True),
        preferred_element_type=jnp.float32,
    )
    y_s = jnp.dot(
        hid_student,
        lax.all_gather(proj_student, SHARD, axis=0, tiled=True),
        preferred_element_type=jnp.float32,
    )
    unit_s, norm_s = unit_rows(y_s)
    z_t = spread(unit_rows(y_t)[0].astype(jnp.bfloat16), PLANE).reshape(-1, bot)
    wide_s = lax.all_gather(y_s, PLANE, axis=0, tiled=True)
    z_s = unit_rows(wide_s)[0].astype(jnp.bfloat16)
    hid_group = lax.all_gather(hid_student, SHARD, axis=0, tiled=True)

    teacher_exp = jnp.exp(jnp.dot(z_t, v_t, preferred_element_type=jnp.float32) / TAU_T)
    row_scale = jnp.ones((teacher_exp.shape[0],), jnp.float32)
    col_scale = 1.0 / total(jnp.sum(row_scale[:, None] * teacher_exp, axis=0), "z")
    for step in range(ITERS - 1):
        row_scale = 1.0 / total(jnp.sum(teacher_exp * col_scale[None, :], axis=1), PLANE)
        col_scale = 1.0 / total(jnp.sum(row_scale[:, None] * teacher_exp, axis=0), "z")
    scores = jnp.dot(z_s, v_s, preferred_element_type=jnp.float32)
    student_exp = jnp.exp(scores / TAU_S)
    weighted = teacher_exp * col_scale[None, :]
    sums = total(
        jnp.stack(
            [
                jnp.sum(weighted, axis=1),
                jnp.sum(student_exp, axis=1),
                jnp.sum(weighted * scores, axis=1),
            ]
        ),
        PLANE,
    )
    row_scale, expsum, cross = 1.0 / sums[0], sums[1], sums[2]
    row_scale, expsum, cross = lax.optimization_barrier((row_scale, expsum, cross))
    row_loss = jnp.sum(jnp.log(expsum) - row_scale * cross / TAU_S)
    target = weighted * row_scale[:, None]
    prob = student_exp / expsum[:, None]
    grad_logits = (GRAD_SCALE / TAU_S * (prob - target)).astype(jnp.bfloat16)

    dproto = lax.psum_scatter(
        lax.dot_general(z_s, grad_logits, ROW_DIMS, preferred_element_type=jnp.float32),
        "z",
        scatter_dimension=0,
        tiled=True,
    )
    dzhat = scatter_sum(
        lax.dot_general(grad_logits, v_s, COL_DIMS, preferred_element_type=jnp.float32), PLANE
    )
    dy = norm_backward(dzhat, unit_s, norm_s)
    dy_group = spread(dy, SHARD).reshape(-1, bot)
    depth = proj_student.shape[0]
    hid_block = lax.dynamic_slice_in_dim(
        hid_group, lax.axis_index(SHARD) * depth, depth, 1
    )
    proj_term = lax.dot_general(hid_block, dy_group, ROW_DIMS, preferred_element_type=jnp.float32)
    proj_part = scatter_sum(proj_term, DP)

    own = dproto.shape[0]
    v_own = lax.dynamic_slice_in_dim(v_s, lax.axis_index("z") * own, own, 0).astype(jnp.float32)
    dots = jnp.sum(v_own * dproto, axis=0)
    flat = jnp.concatenate(
        [proj_part.reshape(-1, LANES), dots.reshape(-1, LANES), jnp.full((8, LANES), row_loss)]
    )
    parts = spread(flat, DP)
    cut = proj_part.size // LANES
    grad_proj = parts[:, :cut].reshape(-1, bot)
    sides = parts[:, cut:].reshape(lax.axis_size("z"), lax.axis_size("yh"), -1)
    sums = jnp.sum(lax.dynamic_index_in_dim(sides, side, 1, keepdims=False), axis=0)
    dots = sums[:half]
    row_count = hid_teacher.shape[0] * lax.axis_size(DP + SHARD)
    loss = sums[half] / row_count
    grad = (dproto - v_own * dots[None, :]) / col_norm[None, :]
    grad = grad.reshape(lax.axis_size("yh"), -1, half)
    grad = lax.all_to_all(grad, "yh", 0, 0, tiled=True)
    grad_proto = jnp.concatenate([grad[0], grad[1]], axis=1)
    return (loss, grad_proj, grad_proto)


def solution(mesh):
    fine = Mesh(mesh.devices.reshape(8, 2, 2, 4, 2), DP + SHARD)
    everything = DP + SHARD
    placed = (
        P(everything, None),
        P(everything, None),
        P(SHARD, None),
        P(SHARD, None),
        P(None, SHARD),
        P(None, SHARD),
    )
    return jax.shard_map(
        local,
        mesh=fine,
        in_specs=placed,
        out_specs=(P(), P(SHARD, None), P(DP, SHARD)),
        check_vma=False,
    )
```

```python
import jax
import jax.numpy as jnp
from jax import lax
from jax.sharding import Mesh, PartitionSpec as P

ITERS = 3
GRAD_SCALE = 256
TAU_T = 0.04
TAU_S = 0.1
EPS = 1e-06
LANES = 128
ROW_DIMS = (((0,), (0,)), ((), ()))
COL_DIMS = (((1,), (1,)), ((), ()))

DP = ("z", "yh")
SHARD = ("yl", "x", "c")
PLANE = ("yh", "yl", "x", "c")


def unit_rows(proj_out):
    norm = jnp.sqrt(jnp.sum(proj_out * proj_out, axis=1, keepdims=True) + EPS)
    return (proj_out / norm, norm)


def unit_columns(weight):
    wide = weight.astype(jnp.float32)
    norm = jnp.sqrt(jnp.sum(wide * wide, axis=0) + EPS)
    return ((wide / norm).astype(jnp.bfloat16), norm)


def spread(block, axes):
    count = lax.axis_size(axes)
    return lax.all_to_all(
        jnp.broadcast_to(block[None], (count,) + block.shape), axes, 0, 0, tiled=True
    )


def total(vector, axes):
    return jnp.sum(spread(vector.reshape(-1, LANES), axes), axis=0).reshape(vector.shape)


def scatter_sum(parts, axes):
    count = lax.axis_size(axes)
    own = parts.shape[0] // count
    blocks = parts.reshape((count, own) + parts.shape[1:])
    return jnp.sum(lax.all_to_all(blocks, axes, 0, 0, tiled=True), axis=0)


def project_split(hidden, weight):
    rows, depth = hidden.shape[0], weight.shape[0]
    yl, x, c = (lax.axis_size(axis) for axis in SHARD)
    share = spread(weight, ("yl", "c")).reshape(yl * c * depth, -1)
    pieces = hidden.reshape(rows, yl, x, c, depth).transpose(2, 0, 1, 3, 4)
    pieces = lax.all_to_all(pieces.reshape(x, rows, -1), "x", 0, 0, tiled=True)
    part = jnp.dot(pieces.reshape(x * rows, -1), share, preferred_element_type=jnp.float32)
    return scatter_sum(part, "x")


def swap(block):
    count = lax.axis_size("yh")
    parts = block.reshape((count, -1, block.shape[1]))
    parts = lax.all_to_all(parts, "yh", 0, 0, tiled=True)
    return jnp.concatenate([parts[i] for i in range(count)], axis=1)


def norm_backward(dzhat, unit_s, norm_s):
    inner = jnp.sum(unit_s * dzhat, axis=1, keepdims=True)
    return ((dzhat - unit_s * inner) / norm_s).astype(jnp.bfloat16)


def local(hid_teacher, hid_student, proj_teacher, proj_student, proto_teacher, proto_student):
    rows, bot = hid_teacher.shape[0], proj_teacher.shape[1]
    half = proto_teacher.shape[1] // lax.axis_size("yh")
    side = lax.axis_index("yh")
    first = side * half
    v_t, _ = unit_columns(lax.dynamic_slice_in_dim(proto_teacher, first, half, 1))
    v_all, norm_all = unit_columns(proto_student)
    v_s = lax.dynamic_slice_in_dim(v_all, first, half, 1)
    v_t, v_s = lax.optimization_barrier((v_t, v_s))

    y_t = project_split(hid_teacher, proj_teacher)
    z_t = spread(unit_rows(y_t)[0].astype(jnp.bfloat16), PLANE).reshape(-1, bot)
    gathered = lax.all_gather(proj_student, SHARD, axis=0, tiled=True)
    gathered, z_t = lax.optimization_barrier((gathered, z_t))
    y_s = jnp.dot(hid_student, gathered, preferred_element_type=jnp.float32)
    unit_s, norm_s = unit_rows(y_s)
    wide_s = lax.all_gather(y_s, PLANE, axis=0, tiled=True)
    z_s = unit_rows(wide_s)[0].astype(jnp.bfloat16)
    hid_group = lax.all_gather(hid_student, SHARD, axis=0, tiled=True)

    teacher_exp = jnp.exp(jnp.dot(z_t, v_t, preferred_element_type=jnp.float32) / TAU_T)
    row_scale = jnp.ones((teacher_exp.shape[0],), jnp.float32)
    col_scale = 1.0 / total(jnp.sum(row_scale[:, None] * teacher_exp, axis=0), "z")
    for step in range(ITERS - 1):
        row_scale = 1.0 / total(jnp.sum(teacher_exp * col_scale[None, :], axis=1), PLANE)
        col_scale = 1.0 / total(jnp.sum(row_scale[:, None] * teacher_exp, axis=0), "z")
    scores = jnp.dot(z_s, v_s, preferred_element_type=jnp.float32)
    student_exp = jnp.exp(scores / TAU_S)
    weighted = teacher_exp * col_scale[None, :]
    sums = total(
        jnp.stack(
            [
                jnp.sum(weighted, axis=1),
                jnp.sum(student_exp, axis=1),
                jnp.sum(weighted * scores, axis=1),
            ]
        ),
        PLANE,
    )
    row_scale, expsum, cross = 1.0 / sums[0], sums[1], sums[2]
    row_scale, expsum, cross = lax.optimization_barrier((row_scale, expsum, cross))
    row_loss = jnp.sum(jnp.log(expsum) - row_scale * cross / TAU_S)
    target = weighted * row_scale[:, None]
    prob = student_exp / expsum[:, None]
    grad_logits = (GRAD_SCALE / TAU_S * (prob - target)).astype(jnp.bfloat16)

    dzhat_part = lax.dot_general(
        grad_logits, v_s, COL_DIMS, preferred_element_type=jnp.float32
    )
    grad_logits, dzhat_part = lax.optimization_barrier((grad_logits, dzhat_part))
    dproto = lax.psum_scatter(
        lax.dot_general(z_s, grad_logits, ROW_DIMS, preferred_element_type=jnp.float32),
        "z",
        scatter_dimension=0,
        tiled=True,
    )
    dzhat = scatter_sum(dzhat_part, PLANE)
    dy = norm_backward(dzhat, unit_s, norm_s)
    dy_group = spread(dy, SHARD).reshape(-1, bot)
    depth = proj_student.shape[0]
    hid_block = lax.dynamic_slice_in_dim(
        hid_group, lax.axis_index(SHARD) * depth, depth, 1
    )
    proj_term = lax.dot_general(hid_block, dy_group, ROW_DIMS, preferred_element_type=jnp.float32)
    proj_part = scatter_sum(proj_term, DP)

    own = dproto.shape[0]
    v_own = lax.dynamic_slice_in_dim(v_s, lax.axis_index("z") * own, own, 0).astype(jnp.float32)
    dots = jnp.sum(v_own * dproto, axis=0)
    swapped = swap(dproto)
    last = own // lax.axis_size("yh")
    v_swapped = lax.dynamic_slice_in_dim(v_all, lax.axis_index(DP) * last, last, 0).astype(
        jnp.float32
    )
    flat = jnp.concatenate(
        [proj_part.reshape(-1, LANES), dots.reshape(-1, LANES), jnp.full((8, LANES), row_loss)]
    )
    parts = spread(flat, DP)
    cut = proj_part.size // LANES
    grad_proj = parts[:, :cut].reshape(-1, bot)
    sides = jnp.sum(
        parts[:, cut:].reshape(lax.axis_size("z"), lax.axis_size("yh"), -1), axis=0
    )
    dots = sides[:, :half].reshape(-1)
    row_count = hid_teacher.shape[0] * lax.axis_size(DP + SHARD)
    loss = sides[0, half] / row_count
    grad_proto = (swapped - v_swapped * dots[None, :]) / norm_all[None, :]
    return (loss, grad_proj, grad_proto)


def solution(mesh):
    fine = Mesh(mesh.devices.reshape(8, 2, 2, 4, 2), DP + SHARD)
    everything = DP + SHARD
    placed = (
        P(everything, None),
        P(everything, None),
        P(SHARD, None),
        P(SHARD, None),
        P(None, SHARD),
        P(None, SHARD),
    )
    return jax.shard_map(
        local,
        mesh=fine,
        in_specs=placed,
        out_specs=(P(), P(SHARD, None), P(DP, SHARD)),
        check_vma=False,
    )
```

```python
import functools

import jax
import jax.numpy as jnp
from jax import lax
from jax.experimental import pallas as pl
from jax.experimental.pallas import tpu as pltpu
from jax.sharding import Mesh, PartitionSpec as P

ITERS = 3
GRAD_SCALE = 256
TAU_T = 0.04
TAU_S = 0.1
EPS = 1e-06
LANES = 128
ROWS_BLOCK = 256
CHUNK = 512
VMEM_LIMIT = 32 * 1024 * 1024
ROW_DIMS = (((0,), (0,)), ((), ()))
COL_DIMS = (((1,), (1,)), ((), ()))

DP = ("z", "yh")
SHARD = ("yl", "x", "c")
PLANE = ("yh", "yl", "x", "c")


def unit_rows(proj_out):
    norm = jnp.sqrt(jnp.sum(proj_out * proj_out, axis=1, keepdims=True) + EPS)
    return (proj_out / norm, norm)


def unit_columns(weight):
    wide = weight.astype(jnp.float32)
    norm = jnp.sqrt(jnp.sum(wide * wide, axis=0) + EPS)
    return ((wide / norm).astype(jnp.bfloat16), norm)


def exchange(blocks, axes):
    return lax.all_to_all(blocks, axes, 0, 0, tiled=True)


def spread(block, axes):
    count = lax.axis_size(axes)
    return lax.all_to_all(
        jnp.broadcast_to(block[None], (count,) + block.shape), axes, 0, 0, tiled=True
    )


def scatter_sum(parts, axes):
    count = lax.axis_size(axes)
    own = parts.shape[0] // count
    blocks = parts.reshape((count, own) + parts.shape[1:])
    return jnp.sum(lax.all_to_all(blocks, axes, 0, 0, tiled=True), axis=0)


def project_split(hidden, weight):
    rows, depth = hidden.shape[0], weight.shape[0]
    yl, x, c = (lax.axis_size(axis) for axis in SHARD)
    share = spread(weight, ("yl", "c")).reshape(yl * c * depth, -1)
    pieces = hidden.reshape(rows, yl, x, c, depth).transpose(2, 0, 1, 3, 4)
    pieces = lax.all_to_all(pieces.reshape(x, rows, -1), "x", 0, 0, tiled=True)
    part = jnp.dot(pieces.reshape(x * rows, -1), share, preferred_element_type=jnp.float32)
    return scatter_sum(part, "x")


def swap(block):
    side, count = lax.axis_index("yh"), lax.axis_size("yh")
    rows = block.shape[0] // count
    kept = lax.dynamic_slice_in_dim(block, side * rows, rows, 0)
    sent = lax.dynamic_slice_in_dim(block, (1 - side) * rows, rows, 0)
    got = lax.ppermute(sent, "yh", [(0, 1), (1, 0)])
    return jnp.where(
        side == 0,
        jnp.concatenate([kept, got], axis=1),
        jnp.concatenate([got, kept], axis=1),
    )


def lane_rows(row):
    return jnp.concatenate(
        [row[:, i * LANES : (i + 1) * LANES] for i in range(row.shape[1] // LANES)], axis=0
    )


def one_row(block):
    return jnp.concatenate([block[i : i + 1] for i in range(block.shape[0])], axis=1)


def down(block):
    return jnp.concatenate(
        [
            jnp.broadcast_to(block[i : i + 1], (LANES, LANES)).T
            for i in range(block.shape[0])
        ],
        axis=0,
    )


def lane_sums(wide):
    ones = jnp.ones((8, LANES), jnp.float32)
    row = lax.dot_general(
        ones, wide, COL_DIMS, precision=lax.Precision.HIGHEST, preferred_element_type=jnp.float32
    )
    return lane_rows(row[0:1])


def fold_lanes(wide):
    pieces = [wide[:, i * LANES : (i + 1) * LANES] for i in range(wide.shape[1] // LANES)]
    return functools.reduce(lambda a, b: a + b, pieces)


def fold_rows(tall):
    return jnp.sum(tall.reshape(-1, 8, tall.shape[1]), axis=0)


def repeat_out(out_ref, block):
    out_ref[...] = jnp.broadcast_to(block[None], out_ref.shape)


def first_kernel(z_ref, v_ref, exp_ref, out_ref, acc):
    step = pl.program_id(0)

    @pl.when(step == 0)
    def _():
        acc[...] = jnp.zeros_like(acc)

    width = v_ref.shape[1]
    for start in range(0, width, CHUNK):
        cols = slice(start, start + CHUNK)
        product = jnp.dot(z_ref[...], v_ref[:, cols], preferred_element_type=jnp.float32)
        block = jnp.exp(product * (1.0 / TAU_T))
        exp_ref[:, cols] = block
        acc[:, cols] += fold_rows(block)

    @pl.when(step == pl.num_programs(0) - 1)
    def _():
        repeat_out(out_ref, lane_rows(jnp.sum(acc[...], axis=0, keepdims=True)))


def row_kernel(parts_ref, exp_ref, out_ref, scale, acc):
    step = pl.program_id(0)

    @pl.when(step == 0)
    def _():
        scale[...] = one_row(1.0 / jnp.sum(parts_ref[...], axis=0))

    rows, width = exp_ref.shape
    block = exp_ref[:, 0:LANES] * scale[:, 0:LANES]
    for start in range(LANES, width, LANES):
        cols = slice(start, start + LANES)
        block += exp_ref[:, cols] * scale[:, cols]
    acc[pl.ds(pl.multiple_of(step * rows, rows), rows), :] = block

    @pl.when(step == pl.num_programs(0) - 1)
    def _():
        repeat_out(out_ref, lane_sums(acc[...]))


def column_kernel(parts_ref, exp_ref, out_ref, scale, acc):
    step = pl.program_id(0)

    @pl.when(step == 0)
    def _():
        scale[...] = down(1.0 / jnp.sum(parts_ref[...], axis=0))
        acc[...] = jnp.zeros_like(acc)

    rows, width = exp_ref.shape
    factor = scale[pl.ds(pl.multiple_of(step * rows, rows), rows), :]
    for start in range(0, width, LANES):
        cols = slice(start, start + LANES)
        acc[:, cols] += fold_rows(exp_ref[:, cols] * factor)

    @pl.when(step == pl.num_programs(0) - 1)
    def _():
        repeat_out(out_ref, lane_rows(jnp.sum(acc[...], axis=0, keepdims=True)))


def student_kernel(parts_ref, exp_ref, z_ref, v_ref, out_ref, scale, acc):
    step = pl.program_id(0)

    @pl.when(step == 0)
    def _():
        scale[...] = one_row(1.0 / jnp.sum(parts_ref[...], axis=0))

    rows, width = exp_ref.shape
    here = pl.ds(pl.multiple_of(step * rows, rows), rows)
    mass = jnp.zeros((rows, LANES), jnp.float32)
    exps = jnp.zeros((rows, LANES), jnp.float32)
    cross = jnp.zeros((rows, LANES), jnp.float32)
    for start in range(0, width, CHUNK):
        cols = slice(start, start + CHUNK)
        scores = jnp.dot(z_ref[...], v_ref[:, cols], preferred_element_type=jnp.float32)
        weighted = exp_ref[:, cols] * scale[:, cols]
        mass += fold_lanes(weighted)
        exps += fold_lanes(jnp.exp(scores * (1.0 / TAU_S)))
        cross += fold_lanes(weighted * scores)
    acc[0, here, :] = mass
    acc[1, here, :] = exps
    acc[2, here, :] = cross

    @pl.when(step == pl.num_programs(0) - 1)
    def _():
        sums = [lane_sums(acc[i]) for i in range(3)]
        repeat_out(out_ref, jnp.concatenate(sums, axis=0))


def gradient_kernel(
    row_parts_ref, col_parts_ref, exp_ref, z_ref, zt_ref, v_ref, dz_ref, dp_ref,
    scale, teacher, student, grad,
):
    step = pl.program_id(0)
    rows, width = exp_ref.shape
    tall = rows // LANES

    @pl.when(step == 0)
    def _():
        sums = jnp.sum(row_parts_ref[...], axis=0)
        factor = GRAD_SCALE / TAU_S
        teacher[...] = down(factor / sums[0:tall])
        student[...] = down(factor / sums[tall : 2 * tall])
        scale[...] = 1.0 / jnp.sum(col_parts_ref[...], axis=0)
        dz_ref[...] = jnp.zeros_like(dz_ref)

    groups = width // LANES
    col = one_row(scale[pl.ds(pl.multiple_of(step * groups, groups), groups), :])
    for start in range(0, rows, ROWS_BLOCK):
        here = slice(start, start + ROWS_BLOCK)
        scores = jnp.dot(z_ref[here, :], v_ref[...], preferred_element_type=jnp.float32)
        prob = jnp.exp(scores * (1.0 / TAU_S))
        for piece in range(0, width, LANES):
            cols = slice(piece, piece + LANES)
            target = exp_ref[here, cols] * col[:, cols] * teacher[here, :]
            grad[here, cols] = (prob[:, cols] * student[here, :] - target).astype(jnp.bfloat16)
        dz_ref[here, :] += lax.dot_general(
            grad[here, :], v_ref[...], COL_DIMS, preferred_element_type=jnp.float32
        )
    dp_ref[...] = jnp.dot(zt_ref[...], grad[...], preferred_element_type=jnp.float32)


def params():
    return pltpu.CompilerParams(
        dimension_semantics=("arbitrary",), vmem_limit_bytes=VMEM_LIMIT
    )


def cost(flops, size, exps=0):
    return pl.CostEstimate(flops=flops, bytes_accessed=size, transcendentals=exps)


def whole(shape):
    return pl.BlockSpec(shape, lambda i: (0,) * len(shape))


def f32(*shape):
    return jax.ShapeDtypeStruct(shape, jnp.float32)


def first_pass(z, v, copies):
    rows, width = z.shape[0], v.shape[1]
    spread_shape = (copies, width // LANES, LANES)
    return pl.pallas_call(
        first_kernel,
        grid=(rows // ROWS_BLOCK,),
        in_specs=[pl.BlockSpec((ROWS_BLOCK, z.shape[1]), lambda i: (i, 0)), whole(v.shape)],
        out_specs=[pl.BlockSpec((ROWS_BLOCK, width), lambda i: (i, 0)), whole(spread_shape)],
        out_shape=[f32(rows, width), f32(*spread_shape)],
        scratch_shapes=[pltpu.VMEM((8, width), jnp.float32)],
        compiler_params=params(),
        cost_estimate=cost(2 * z.size * width, rows * width * 4, rows * width),
    )(z, v)


def row_pass(parts, exp, copies):
    rows, width = exp.shape
    out = (copies, rows // LANES, LANES)
    return pl.pallas_call(
        row_kernel,
        grid=(rows // ROWS_BLOCK,),
        in_specs=[whole(parts.shape), pl.BlockSpec((ROWS_BLOCK, width), lambda i: (i, 0))],
        out_specs=whole(out),
        out_shape=f32(*out),
        scratch_shapes=[pltpu.VMEM((1, width), jnp.float32), pltpu.VMEM((rows, LANES), jnp.float32)],
        compiler_params=params(),
        cost_estimate=cost(2 * exp.size, exp.size * 4),
    )(parts, exp)


def column_pass(parts, exp, copies):
    rows, width = exp.shape
    out = (copies, width // LANES, LANES)
    return pl.pallas_call(
        column_kernel,
        grid=(rows // ROWS_BLOCK,),
        in_specs=[whole(parts.shape), pl.BlockSpec((ROWS_BLOCK, width), lambda i: (i, 0))],
        out_specs=whole(out),
        out_shape=f32(*out),
        scratch_shapes=[pltpu.VMEM((rows, LANES), jnp.float32), pltpu.VMEM((8, width), jnp.float32)],
        compiler_params=params(),
        cost_estimate=cost(2 * exp.size, exp.size * 4),
    )(parts, exp)


def student_pass(parts, exp, z, v, copies):
    rows, width = exp.shape
    out = (copies, 3 * rows // LANES, LANES)
    return pl.pallas_call(
        student_kernel,
        grid=(rows // ROWS_BLOCK,),
        in_specs=[
            whole(parts.shape),
            pl.BlockSpec((ROWS_BLOCK, width), lambda i: (i, 0)),
            pl.BlockSpec((ROWS_BLOCK, z.shape[1]), lambda i: (i, 0)),
            whole(v.shape),
        ],
        out_specs=whole(out),
        out_shape=f32(*out),
        scratch_shapes=[
            pltpu.VMEM((1, width), jnp.float32),
            pltpu.VMEM((3, rows, LANES), jnp.float32),
        ],
        compiler_params=params(),
        cost_estimate=cost(2 * z.size * width, exp.size * 4, exp.size),
    )(parts, exp, z, v)


def gradient_pass(row_parts, col_parts, exp, z, zt, v):
    rows, width = exp.shape
    bot = z.shape[1]
    return pl.pallas_call(
        gradient_kernel,
        grid=(width // CHUNK,),
        in_specs=[
            whole(row_parts.shape),
            whole(col_parts.shape),
            pl.BlockSpec((rows, CHUNK), lambda i: (0, i)),
            whole(z.shape),
            whole(zt.shape),
            pl.BlockSpec((bot, CHUNK), lambda i: (0, i)),
        ],
        out_specs=[whole((rows, bot)), pl.BlockSpec((bot, CHUNK), lambda i: (0, i))],
        out_shape=[f32(rows, bot), f32(bot, width)],
        scratch_shapes=[
            pltpu.VMEM((width // LANES, LANES), jnp.float32),
            pltpu.VMEM((rows, LANES), jnp.float32),
            pltpu.VMEM((rows, LANES), jnp.float32),
            pltpu.VMEM((rows, CHUNK), jnp.bfloat16),
        ],
        compiler_params=params(),
        cost_estimate=cost(6 * z.size * width, exp.size * 4, exp.size),
    )(row_parts, col_parts, exp, z, zt, v)


def norm_backward(dzhat, unit_s, norm_s):
    inner = jnp.sum(unit_s * dzhat, axis=1, keepdims=True)
    return ((dzhat - unit_s * inner) / norm_s).astype(jnp.bfloat16)


def local(hid_teacher, hid_student, proj_teacher, proj_student, proto_teacher, proto_student):
    rows, bot = hid_teacher.shape[0], proj_teacher.shape[1]
    half = proto_teacher.shape[1] // lax.axis_size("yh")
    side = lax.axis_index("yh")
    first = side * half
    v_t, _ = unit_columns(lax.dynamic_slice_in_dim(proto_teacher, first, half, 1))
    v_all, norm_all = unit_columns(proto_student)
    v_s = lax.dynamic_slice_in_dim(v_all, first, half, 1)
    v_t, v_s = lax.optimization_barrier((v_t, v_s))

    y_t = project_split(hid_teacher, proj_teacher)
    z_t = spread(unit_rows(y_t)[0].astype(jnp.bfloat16), PLANE).reshape(-1, bot)
    gathered = lax.all_gather(proj_student, SHARD, axis=0, tiled=True)
    gathered, z_t = lax.optimization_barrier((gathered, z_t))
    y_s = jnp.dot(hid_student, gathered, preferred_element_type=jnp.float32)
    unit_s, norm_s = unit_rows(y_s)
    wide_s = lax.all_gather(y_s, PLANE, axis=0, tiled=True)
    z_s = unit_rows(wide_s)[0].astype(jnp.bfloat16)
    hid_group = lax.all_gather(hid_student, SHARD, axis=0, tiled=True)

    columns, planes = lax.axis_size("z"), lax.axis_size(PLANE)
    teacher_exp, mass = first_pass(z_t, v_t, columns)
    col_parts = exchange(mass, "z")
    for step in range(ITERS - 1):
        row_parts = exchange(row_pass(col_parts, teacher_exp, planes), PLANE)
        col_parts = exchange(column_pass(row_parts, teacher_exp, columns), "z")
    sums = exchange(student_pass(col_parts, teacher_exp, z_s, v_s, planes), PLANE)
    dzhat_part, dproto_part = gradient_pass(sums, col_parts, teacher_exp, z_s, z_s.T, v_s)
    row_mass, expsum, cross = jnp.split(jnp.sum(sums, axis=0), 3, axis=0)
    row_loss = jnp.sum(jnp.log(expsum) - cross / row_mass / TAU_S)
    dproto = lax.psum_scatter(dproto_part, "z", scatter_dimension=0, tiled=True)
    dzhat = scatter_sum(dzhat_part, PLANE)
    dy = norm_backward(dzhat, unit_s, norm_s)
    dy_group = spread(dy, SHARD).reshape(-1, bot)
    depth = proj_student.shape[0]
    hid_block = lax.dynamic_slice_in_dim(
        hid_group, lax.axis_index(SHARD) * depth, depth, 1
    )
    proj_term = lax.dot_general(hid_block, dy_group, ROW_DIMS, preferred_element_type=jnp.float32)
    proj_part = scatter_sum(proj_term, DP)

    own = dproto.shape[0]
    v_own = lax.dynamic_slice_in_dim(v_s, lax.axis_index("z") * own, own, 0).astype(jnp.float32)
    dots = jnp.sum(v_own * dproto, axis=0)
    swapped = swap(dproto)
    last = own // lax.axis_size("yh")
    v_swapped = lax.dynamic_slice_in_dim(v_all, lax.axis_index(DP) * last, last, 0).astype(
        jnp.float32
    )
    flat = jnp.concatenate(
        [proj_part.reshape(-1, LANES), dots.reshape(-1, LANES), jnp.full((8, LANES), row_loss)]
    )
    parts = spread(flat, DP)
    cut = proj_part.size // LANES
    grad_proj = parts[:, :cut].reshape(-1, bot)
    sides = jnp.sum(
        parts[:, cut:].reshape(lax.axis_size("z"), lax.axis_size("yh"), -1), axis=0
    )
    dots = sides[:, :half].reshape(-1)
    row_count = hid_teacher.shape[0] * lax.axis_size(DP + SHARD)
    loss = sides[0, half] / row_count
    grad_proto = (swapped - v_swapped * dots[None, :]) / norm_all[None, :]
    return (loss, grad_proj, grad_proto)


def solution(mesh):
    fine = Mesh(mesh.devices.reshape(8, 2, 2, 4, 2), DP + SHARD)
    everything = DP + SHARD
    placed = (
        P(everything, None),
        P(everything, None),
        P(SHARD, None),
        P(SHARD, None),
        P(None, SHARD),
        P(None, SHARD),
    )
    return jax.shard_map(
        local,
        mesh=fine,
        in_specs=placed,
        out_specs=(P(), P(SHARD, None), P(DP, SHARD)),
        check_vma=False,
    )
```

```python
import functools

import jax
import jax.numpy as jnp
from jax import lax
from jax.experimental import pallas as pl
from jax.experimental.pallas import tpu as pltpu
from jax.sharding import Mesh, PartitionSpec as P

ITERS = 3
GRAD_SCALE = 256
TAU_T = 0.04
TAU_S = 0.1
EPS = 1e-06
LANES = 128
ROWS_BLOCK = 256
CHUNK = 512
MIB = 1024 * 1024
ROW_DIMS = (((0,), (0,)), ((), ()))
COL_DIMS = (((1,), (1,)), ((), ()))

DP = ("z", "yh")
SHARD = ("yl", "x", "c")
PLANE = ("yh", "yl", "x", "c")


def unit_rows(proj_out):
    norm = jnp.sqrt(jnp.sum(proj_out * proj_out, axis=1, keepdims=True) + EPS)
    return (proj_out / norm, norm)


def exchange(blocks, axes):
    return lax.all_to_all(blocks, axes, 0, 0, tiled=True)


def spread(block, axes):
    count = lax.axis_size(axes)
    return lax.all_to_all(
        jnp.broadcast_to(block[None], (count,) + block.shape), axes, 0, 0, tiled=True
    )


def over_cores(blocks):
    return lax.ppermute(blocks, "c", [(0, 1), (1, 0)])


def scatter_sum(parts, axes):
    count = lax.axis_size(axes)
    own = parts.shape[0] // count
    blocks = parts.reshape((count, own) + parts.shape[1:])
    blocks = lax.all_to_all(blocks, axes, 0, 0, tiled=True)
    return jnp.sum(blocks.astype(jnp.float32), axis=0)


def project_split(hidden, weight):
    rows = hidden.shape[0]
    kept, sent = depth_halves(hidden)
    both = jnp.concatenate([kept, over_cores(sent)], axis=0)
    share = spread(weight, ("yl", "x")).reshape(-1, weight.shape[1])
    part = jnp.dot(both, share, preferred_element_type=jnp.float32)
    return part[:rows] + over_cores(part[rows:])


def swap(block):
    side, count = lax.axis_index("yh"), lax.axis_size("yh")
    rows = block.shape[0] // count
    kept = lax.dynamic_slice_in_dim(block, side * rows, rows, 0)
    sent = lax.dynamic_slice_in_dim(block, (1 - side) * rows, rows, 0)
    got = lax.ppermute(sent, "yh", [(0, 1), (1, 0)])
    return jnp.where(
        side == 0,
        jnp.concatenate([kept, got], axis=1),
        jnp.concatenate([got, kept], axis=1),
    )


def lane_rows(row):
    return jnp.concatenate(
        [row[:, i * LANES : (i + 1) * LANES] for i in range(row.shape[1] // LANES)], axis=0
    )


def one_row(block):
    return jnp.concatenate([block[i : i + 1] for i in range(block.shape[0])], axis=1)


def down(block):
    return jnp.concatenate(
        [
            jnp.broadcast_to(block[i : i + 1], (LANES, LANES)).T
            for i in range(block.shape[0])
        ],
        axis=0,
    )


def lane_sums(wide):
    ones = jnp.ones((8, LANES), jnp.float32)
    row = lax.dot_general(
        ones, wide, COL_DIMS, precision=lax.Precision.HIGHEST, preferred_element_type=jnp.float32
    )
    return lane_rows(row[0:1])


def fold_lanes(wide):
    pieces = [wide[:, i * LANES : (i + 1) * LANES] for i in range(wide.shape[1] // LANES)]
    return functools.reduce(lambda a, b: a + b, pieces)


def fold_rows(tall):
    return jnp.sum(tall.reshape(-1, 8, tall.shape[1]), axis=0)


def repeat_out(out_ref, block):
    out_ref[...] = jnp.broadcast_to(block[None], out_ref.shape)


def unit_kernel(teacher_ref, student_ref, vt_ref, vs_ref, norm_ref):
    def unit(ref, out_ref):
        wide = ref[...].astype(jnp.float32)
        norm = jnp.sqrt(jnp.sum(wide * wide, axis=0, keepdims=True) + EPS)
        out_ref[...] = (wide / norm).astype(jnp.bfloat16)
        return norm

    unit(teacher_ref, vt_ref)
    norm_ref[...] = unit(student_ref, vs_ref)


def halves_kernel(core_ref, hidden_ref, kept_ref, sent_ref):
    width = kept_ref.shape[1]

    def split(even_ref, odd_ref):
        for start in range(0, width, LANES):
            cols = slice(start, start + LANES)
            even_ref[:, cols] = hidden_ref[:, 2 * start : 2 * start + LANES]
            odd_ref[:, cols] = hidden_ref[:, 2 * start + LANES : 2 * start + 2 * LANES]

    @pl.when(core_ref[0] == 0)
    def _():
        split(kept_ref, sent_ref)

    @pl.when(core_ref[0] != 0)
    def _():
        split(sent_ref, kept_ref)


def project_kernel(hidden_ref, weight_ref, out_ref):
    @pl.when(pl.program_id(0) == 0)
    def _():
        out_ref[...] = jnp.zeros_like(out_ref)

    out_ref[...] += jnp.dot(hidden_ref[...], weight_ref[...], preferred_element_type=jnp.float32)


def first_kernel(z_ref, v_ref, exp_ref, out_ref, acc):
    step = pl.program_id(0)
    width = v_ref.shape[1]

    @pl.when(step == 0)
    def _():
        acc[...] = jnp.zeros_like(acc)

    for start in range(0, width, CHUNK):
        cols = slice(start, start + CHUNK)
        product = jnp.dot(z_ref[...], v_ref[:, cols], preferred_element_type=jnp.float32)
        block = jnp.exp(product * (1.0 / TAU_T))
        exp_ref[:, cols] = block
        acc[:, cols] += fold_rows(block)

    @pl.when(step == pl.num_programs(0) - 1)
    def _():
        repeat_out(out_ref, lane_rows(jnp.sum(acc[...], axis=0, keepdims=True)))


def row_kernel(parts_ref, exp_ref, out_ref, scale, acc):
    step = pl.program_id(0)

    @pl.when(step == 0)
    def _():
        scale[...] = one_row(1.0 / jnp.sum(parts_ref[...], axis=0))

    rows, width = exp_ref.shape
    block = exp_ref[:, 0:LANES] * scale[:, 0:LANES]
    for start in range(LANES, width, LANES):
        cols = slice(start, start + LANES)
        block += exp_ref[:, cols] * scale[:, cols]
    acc[pl.ds(pl.multiple_of(step * rows, rows), rows), :] = block

    @pl.when(step == pl.num_programs(0) - 1)
    def _():
        repeat_out(out_ref, lane_sums(acc[...]))


def column_kernel(parts_ref, exp_ref, out_ref, scale, acc):
    step = pl.program_id(0)

    @pl.when(step == 0)
    def _():
        scale[...] = down(1.0 / jnp.sum(parts_ref[...], axis=0))
        acc[...] = jnp.zeros_like(acc)

    rows, width = exp_ref.shape
    factor = scale[pl.ds(pl.multiple_of(step * rows, rows), rows), :]
    for start in range(0, width, LANES):
        cols = slice(start, start + LANES)
        acc[:, cols] += fold_rows(exp_ref[:, cols] * factor)

    @pl.when(step == pl.num_programs(0) - 1)
    def _():
        repeat_out(out_ref, lane_rows(jnp.sum(acc[...], axis=0, keepdims=True)))


def student_kernel(parts_ref, exp_ref, y_ref, v_ref, out_ref, z_ref, zt_ref, scale, acc):
    step = pl.program_id(0)

    @pl.when(step == 0)
    def _():
        scale[...] = one_row(1.0 / jnp.sum(parts_ref[...], axis=0))

    rows, width = exp_ref.shape
    here = pl.ds(pl.multiple_of(step * rows, rows), rows)
    y = y_ref[...]
    z = y / jnp.sqrt(jnp.sum(y * y, axis=1, keepdims=True) + EPS)
    z_ref[...] = z.astype(jnp.bfloat16)
    zt_ref[...] = z.T.astype(jnp.bfloat16)
    mass = jnp.zeros((rows, LANES), jnp.float32)
    exps = jnp.zeros((rows, LANES), jnp.float32)
    cross = jnp.zeros((rows, LANES), jnp.float32)
    for start in range(0, width, CHUNK):
        cols = slice(start, start + CHUNK)
        scores = jnp.dot(z_ref[...], v_ref[:, cols], preferred_element_type=jnp.float32)
        weighted = exp_ref[:, cols] * scale[:, cols]
        mass += fold_lanes(weighted)
        exps += fold_lanes(jnp.exp(scores * (1.0 / TAU_S)))
        cross += fold_lanes(weighted * scores)
    acc[0, here, :] = mass
    acc[1, here, :] = exps
    acc[2, here, :] = cross

    @pl.when(step == pl.num_programs(0) - 1)
    def _():
        sums = [lane_sums(acc[i]) for i in range(3)]
        repeat_out(out_ref, jnp.concatenate(sums, axis=0))


def gradient_kernel(
    row_parts_ref, col_parts_ref, exp_ref, z_ref, zt_ref, v_ref, dz_ref, dp_ref, dots_ref,
    scale, teacher, student, grad,
):
    step = pl.program_id(0)
    rows, width = exp_ref.shape
    tall = rows // LANES

    @pl.when(step == 0)
    def _():
        sums = jnp.sum(row_parts_ref[...], axis=0)
        factor = GRAD_SCALE / TAU_S
        teacher[...] = down(factor / sums[0:tall])
        student[...] = down(factor / sums[tall : 2 * tall])
        scale[...] = 1.0 / jnp.sum(col_parts_ref[...], axis=0)
        dz_ref[...] = jnp.zeros_like(dz_ref)

    groups = width // LANES
    col = one_row(scale[pl.ds(pl.multiple_of(step * groups, groups), groups), :])
    for start in range(0, rows, ROWS_BLOCK):
        here = slice(start, start + ROWS_BLOCK)
        scores = jnp.dot(z_ref[here, :], v_ref[...], preferred_element_type=jnp.float32)
        prob = jnp.exp(scores * (1.0 / TAU_S))
        for piece in range(0, width, LANES):
            cols = slice(piece, piece + LANES)
            target = exp_ref[here, cols] * col[:, cols] * teacher[here, :]
            grad[here, cols] = (prob[:, cols] * student[here, :] - target).astype(jnp.bfloat16)
        dz_ref[here, :] += lax.dot_general(
            grad[here, :], v_ref[...], COL_DIMS, preferred_element_type=jnp.float32
        )
    dproto = jnp.dot(zt_ref[...], grad[...], preferred_element_type=jnp.float32)
    dp_ref[...] = dproto
    dots_ref[...] = jnp.sum(v_ref[...].astype(jnp.float32) * dproto, axis=0, keepdims=True)


def collect_kernel(proj_ref, dots_ref, loss_ref, out_ref):
    own, bot = proj_ref.shape[1:]
    proj = jnp.sum(proj_ref[...], axis=0)
    dots = dots_ref[...]
    width = dots.shape[1]
    rows = -(-(width + LANES) // bot)
    loss = jnp.broadcast_to(loss_ref[...], (1, rows * bot - width))
    row = jnp.concatenate([dots, loss], axis=1)
    pieces = [row[:, i * bot : (i + 1) * bot] for i in range(rows)]
    pieces.append(jnp.zeros((out_ref.shape[1] - own - rows, bot), jnp.float32))
    repeat_out(out_ref, jnp.concatenate([proj] + pieces, axis=0))


def finish_kernel(parts_ref, dproto_ref, v_ref, norm_ref, proj_ref, grad_ref, loss_ref):
    copies, height, bot = parts_ref.shape
    own = proj_ref.shape[0] // copies
    width = dproto_ref.shape[1] // 2
    rows = -(-(width + LANES) // bot)
    for i in range(copies):
        proj_ref[i * own : (i + 1) * own, :] = parts_ref[i, 0:own, :]
    lines = []
    for side in range(2):
        block = parts_ref[side, own:height, :]
        for i in range(2 + side, copies, 2):
            block = block + parts_ref[i, own:height, :]
        lines.append(jnp.concatenate([block[i : i + 1] for i in range(rows)], axis=1))
    loss_ref[...] = lines[0][:, width : width + LANES]
    for side in range(2):
        cols = slice(side * width, (side + 1) * width)
        dots = lines[side][:, 0:width]
        grad_ref[:, cols] = (dproto_ref[:, cols] - v_ref[:, cols] * dots) / norm_ref[:, cols]


def params(mib):
    return pltpu.CompilerParams(
        dimension_semantics=("arbitrary",), vmem_limit_bytes=mib * MIB
    )


def cost(flops, size, exps=0):
    return pl.CostEstimate(flops=flops, bytes_accessed=size, transcendentals=exps)


def whole(shape):
    return pl.BlockSpec(shape, lambda i: (0,) * len(shape))


def f32(*shape):
    return jax.ShapeDtypeStruct(shape, jnp.float32)


def unit_columns(teacher, student):
    bot, width = teacher.shape
    step = width // CHUNK
    wide = student.shape[1] // step
    return pl.pallas_call(
        unit_kernel,
        grid=(step,),
        in_specs=[
            pl.BlockSpec((bot, CHUNK), lambda i: (0, i)),
            pl.BlockSpec((bot, wide), lambda i: (0, i)),
        ],
        out_specs=[
            pl.BlockSpec((bot, CHUNK), lambda i: (0, i)),
            pl.BlockSpec((bot, wide), lambda i: (0, i)),
            pl.BlockSpec((1, wide), lambda i: (0, i)),
        ],
        out_shape=[
            jax.ShapeDtypeStruct(teacher.shape, jnp.bfloat16),
            jax.ShapeDtypeStruct(student.shape, jnp.bfloat16),
            f32(1, student.shape[1]),
        ],
        compiler_params=params(16),
        cost_estimate=cost(4 * (teacher.size + student.size), 4 * (teacher.size + student.size)),
    )(teacher, student)


def depth_halves(hidden):
    half = jax.ShapeDtypeStruct((hidden.shape[0], hidden.shape[1] // 2), hidden.dtype)
    return pl.pallas_call(
        halves_kernel,
        in_specs=[pl.BlockSpec(memory_space=pltpu.SMEM), pl.BlockSpec(memory_space=pltpu.VMEM)],
        out_shape=[half, half],
        cost_estimate=cost(0, 4 * hidden.size),
    )(lax.axis_index("c").reshape(1), hidden)


def project(hidden, weight):
    rows, depth = hidden.shape
    bot = weight.shape[1]
    return pl.pallas_call(
        project_kernel,
        grid=(depth // CHUNK,),
        in_specs=[
            pl.BlockSpec((rows, CHUNK), lambda i: (0, i)),
            pl.BlockSpec((CHUNK, bot), lambda i: (i, 0)),
        ],
        out_specs=whole((rows, bot)),
        out_shape=f32(rows, bot),
        compiler_params=params(8),
        cost_estimate=cost(2 * rows * weight.size, 2 * (hidden.size + weight.size)),
    )(hidden, weight)


def first_pass(z, v, copies):
    rows, bot = z.shape
    width = v.shape[1]
    out = (copies, width // LANES, LANES)
    return pl.pallas_call(
        first_kernel,
        grid=(rows // ROWS_BLOCK,),
        in_specs=[pl.BlockSpec((ROWS_BLOCK, bot), lambda i: (i, 0)), whole(v.shape)],
        out_specs=[pl.BlockSpec((ROWS_BLOCK, width), lambda i: (i, 0)), whole(out)],
        out_shape=[f32(rows, width), f32(*out)],
        scratch_shapes=[pltpu.VMEM((8, width), jnp.float32)],
        compiler_params=params(16),
        cost_estimate=cost(2 * z.size * width, rows * width * 4, rows * width),
    )(z, v)


def row_pass(parts, exp, copies):
    rows, width = exp.shape
    out = (copies, rows // LANES, LANES)
    return pl.pallas_call(
        row_kernel,
        grid=(rows // ROWS_BLOCK,),
        in_specs=[whole(parts.shape), pl.BlockSpec((ROWS_BLOCK, width), lambda i: (i, 0))],
        out_specs=whole(out),
        out_shape=f32(*out),
        scratch_shapes=[pltpu.VMEM((1, width), jnp.float32), pltpu.VMEM((rows, LANES), jnp.float32)],
        compiler_params=params(12),
        cost_estimate=cost(2 * exp.size, exp.size * 4),
    )(parts, exp)


def column_pass(parts, exp, copies):
    rows, width = exp.shape
    out = (copies, width // LANES, LANES)
    return pl.pallas_call(
        column_kernel,
        grid=(rows // ROWS_BLOCK,),
        in_specs=[whole(parts.shape), pl.BlockSpec((ROWS_BLOCK, width), lambda i: (i, 0))],
        out_specs=whole(out),
        out_shape=f32(*out),
        scratch_shapes=[pltpu.VMEM((rows, LANES), jnp.float32), pltpu.VMEM((8, width), jnp.float32)],
        compiler_params=params(12),
        cost_estimate=cost(2 * exp.size, exp.size * 4),
    )(parts, exp)


def student_pass(parts, exp, y, v, copies):
    rows, width = exp.shape
    bot = y.shape[1]
    out = (copies, 3 * rows // LANES, LANES)
    return pl.pallas_call(
        student_kernel,
        grid=(rows // ROWS_BLOCK,),
        in_specs=[
            whole(parts.shape),
            pl.BlockSpec((ROWS_BLOCK, width), lambda i: (i, 0)),
            pl.BlockSpec((ROWS_BLOCK, bot), lambda i: (i, 0)),
            whole(v.shape),
        ],
        out_specs=[
            whole(out),
            pl.BlockSpec((ROWS_BLOCK, bot), lambda i: (i, 0)),
            pl.BlockSpec((bot, ROWS_BLOCK), lambda i: (0, i)),
        ],
        out_shape=[
            f32(*out),
            jax.ShapeDtypeStruct((rows, bot), jnp.bfloat16),
            jax.ShapeDtypeStruct((bot, rows), jnp.bfloat16),
        ],
        scratch_shapes=[
            pltpu.VMEM((1, width), jnp.float32),
            pltpu.VMEM((3, rows, LANES), jnp.float32),
        ],
        compiler_params=params(16),
        cost_estimate=cost(2 * y.size * width, exp.size * 4, exp.size),
    )(parts, exp, y, v)


def gradient_pass(row_parts, col_parts, exp, z, zt, v):
    rows, width = exp.shape
    bot = z.shape[1]
    return pl.pallas_call(
        gradient_kernel,
        grid=(width // CHUNK,),
        in_specs=[
            whole(row_parts.shape),
            whole(col_parts.shape),
            pl.BlockSpec((rows, CHUNK), lambda i: (0, i)),
            whole(z.shape),
            whole(zt.shape),
            pl.BlockSpec((bot, CHUNK), lambda i: (0, i)),
        ],
        out_specs=[
            whole((rows, bot)),
            pl.BlockSpec((bot, CHUNK), lambda i: (0, i)),
            pl.BlockSpec((1, CHUNK), lambda i: (0, i)),
        ],
        out_shape=[f32(rows, bot), f32(bot, width), f32(1, width)],
        scratch_shapes=[
            pltpu.VMEM((width // LANES, LANES), jnp.float32),
            pltpu.VMEM((rows, LANES), jnp.float32),
            pltpu.VMEM((rows, LANES), jnp.float32),
            pltpu.VMEM((rows, CHUNK), jnp.bfloat16),
        ],
        compiler_params=params(24),
        cost_estimate=cost(6 * z.size * width, exp.size * 4, exp.size),
    )(row_parts, col_parts, exp, z, zt, v)


def norm_backward(dzhat, unit_s, norm_s):
    inner = jnp.sum(unit_s * dzhat, axis=1, keepdims=True)
    return ((dzhat - unit_s * inner) / norm_s).astype(jnp.bfloat16)


def local(hid_teacher, hid_student, proj_teacher, proj_student, proto_teacher, proto_student):
    bot = proj_teacher.shape[1]
    half = proto_teacher.shape[1] // lax.axis_size("yh")
    first = lax.axis_index("yh") * half
    columns, planes = lax.axis_size("z"), lax.axis_size(PLANE)

    gathered = lax.all_gather(proj_student, SHARD, axis=0, tiled=True)
    z_own = unit_rows(project_split(hid_teacher, proj_teacher))[0].astype(jnp.bfloat16)
    z_own, proto_teacher, proto_student = lax.optimization_barrier(
        (z_own, proto_teacher, proto_student)
    )
    z_t = spread(z_own, PLANE).reshape(-1, bot)
    v_t, v_all, norm_all = unit_columns(
        lax.dynamic_slice_in_dim(proto_teacher, first, half, 1), proto_student
    )
    v_s = lax.dynamic_slice_in_dim(v_all, first, half, 1)
    z_t, v_t, v_s = lax.optimization_barrier((z_t, v_t, v_s))
    y_s = project(hid_student, gathered)
    z_t, y_s, hid_student = lax.optimization_barrier((z_t, y_s, hid_student))
    wide_s = lax.all_gather(y_s, PLANE, axis=0, tiled=True)
    hid_group = lax.all_gather(hid_student, SHARD, axis=0, tiled=True)

    teacher_exp, mass = first_pass(z_t, v_t, columns)
    col_parts = exchange(mass, "z")
    for step in range(ITERS - 1):
        row_parts = exchange(row_pass(col_parts, teacher_exp, planes), PLANE)
        col_parts = exchange(column_pass(row_parts, teacher_exp, columns), "z")
    sums, z_s, z_s_t = student_pass(col_parts, teacher_exp, wide_s, v_s, planes)
    sums = exchange(sums, PLANE)
    dzhat_part, dproto_part, dots = gradient_pass(sums, col_parts, teacher_exp, z_s, z_s_t, v_s)

    dzhat_part, y_s, hid_group, v_all, sums = lax.optimization_barrier(
        (dzhat_part, y_s, hid_group, v_all, sums)
    )
    unit_s, norm_s = unit_rows(y_s)
    row_mass, expsum, cross = jnp.split(jnp.sum(sums, axis=0), 3, axis=0)
    row_count = unit_s.shape[0] * lax.axis_size(DP + SHARD)
    loss_part = jnp.sum(jnp.log(expsum) - cross / row_mass / TAU_S) / row_count
    dproto = lax.psum_scatter(dproto_part, "z", scatter_dimension=0, tiled=True)
    last = dproto.shape[0] // lax.axis_size("yh")
    v_last = lax.dynamic_slice_in_dim(v_all, lax.axis_index(DP) * last, last, 0).astype(jnp.float32)
    swapped = swap(dproto)

    dzhat = scatter_sum(dzhat_part, PLANE)
    dy = norm_backward(dzhat, unit_s, norm_s)
    dy_group = spread(dy, SHARD).reshape(-1, bot)
    depth = proj_student.shape[0]
    hid_block = lax.dynamic_slice_in_dim(
        hid_group, lax.axis_index(SHARD) * depth, depth, 1
    )
    proj_term = lax.dot_general(hid_block, dy_group, ROW_DIMS, preferred_element_type=jnp.float32)
    proj_parts = exchange(proj_term.reshape(lax.axis_size(DP), -1, bot), DP)
    height = proj_parts.shape[1] + 8 * -(-(half + LANES) // (8 * bot))
    collected = pl.pallas_call(
        collect_kernel,
        out_shape=f32(proj_parts.shape[0], height, bot),
        compiler_params=pltpu.CompilerParams(vmem_limit_bytes=8 * MIB),
    )(proj_parts, dots, loss_part.reshape(1, 1))
    grad_proj, grad_proto, loss = pl.pallas_call(
        finish_kernel,
        out_shape=[f32(depth, bot), f32(last, 2 * half), f32(1, LANES)],
        compiler_params=pltpu.CompilerParams(vmem_limit_bytes=12 * MIB),
    )(exchange(collected, DP), swapped, v_last, norm_all)
    return (loss[0, 0], grad_proj, grad_proto)


def solution(mesh):
    fine = Mesh(mesh.devices.reshape(8, 2, 2, 4, 2), DP + SHARD)
    everything = DP + SHARD
    placed = (
        P(everything, None),
        P(everything, None),
        P(SHARD, None),
        P(SHARD, None),
        P(None, SHARD),
        P(None, SHARD),
    )
    return jax.shard_map(
        local,
        mesh=fine,
        in_specs=placed,
        out_specs=(P(), P(SHARD, None), P(DP, SHARD)),
        check_vma=False,
    )
```

```python
import functools

import jax
import jax.numpy as jnp
from jax import lax
from jax.experimental import pallas as pl
from jax.experimental.pallas import tpu as pltpu
from jax.sharding import Mesh, PartitionSpec as P

ITERS = 3
GRAD_SCALE = 256
TAU_T = 0.04
TAU_S = 0.1
EPS = 1e-06
LANES = 128
ROWS_BLOCK = 256
CHUNK = 512
MIB = 1024 * 1024
ROW_DIMS = (((0,), (0,)), ((), ()))
COL_DIMS = (((1,), (1,)), ((), ()))

DP = ("z", "yh")
SHARD = ("yl", "x", "c")
PLANE = ("yh", "yl", "x", "c")


def exchange(blocks, axes):
    return lax.all_to_all(blocks, axes, 0, 0, tiled=True)


def over_cores(blocks):
    return lax.ppermute(blocks, "c", [(0, 1), (1, 0)])


def features_kernel(part_ref, got_ref, out_ref):
    y = part_ref[0 : got_ref.shape[0], :] + got_ref[...]
    unit = y / jnp.sqrt(jnp.sum(y * y, axis=1, keepdims=True) + EPS)
    repeat_out(out_ref, unit.astype(jnp.bfloat16))


def unit_split(hidden, weight, copies):
    rows, bot = hidden.shape[0], weight.shape[1]
    kept, sent, repeated = depth_halves(hidden, weight, lax.axis_size(("yl", "x")))
    share = exchange(repeated, ("yl", "x")).reshape(-1, bot)
    both = jnp.concatenate([kept, over_cores(sent)], axis=0)
    part = jnp.dot(both, share, preferred_element_type=jnp.float32)
    return pl.pallas_call(
        features_kernel,
        out_shape=pltpu.HBM((copies, rows, bot), jnp.bfloat16),
        compiler_params=pltpu.CompilerParams(vmem_limit_bytes=8 * MIB),
    )(part, over_cores(part[rows:]))


def swap(block):
    side, count = lax.axis_index("yh"), lax.axis_size("yh")
    rows = block.shape[0] // count
    kept = lax.dynamic_slice_in_dim(block, side * rows, rows, 0)
    sent = lax.dynamic_slice_in_dim(block, (1 - side) * rows, rows, 0)
    got = lax.ppermute(sent, "yh", [(0, 1), (1, 0)])
    return jnp.where(
        side == 0,
        jnp.concatenate([kept, got], axis=1),
        jnp.concatenate([got, kept], axis=1),
    )


def lane_rows(row):
    return jnp.concatenate(
        [row[:, i * LANES : (i + 1) * LANES] for i in range(row.shape[1] // LANES)], axis=0
    )


def one_row(block):
    return jnp.concatenate([block[i : i + 1] for i in range(block.shape[0])], axis=1)


def down(block):
    return jnp.concatenate(
        [
            jnp.broadcast_to(block[i : i + 1], (LANES, LANES)).T
            for i in range(block.shape[0])
        ],
        axis=0,
    )


def lane_sums(wide):
    ones = jnp.ones((8, LANES), jnp.float32)
    row = lax.dot_general(
        ones, wide, COL_DIMS, precision=lax.Precision.HIGHEST, preferred_element_type=jnp.float32
    )
    return lane_rows(row[0:1])


def fold_lanes(wide):
    pieces = [wide[:, i * LANES : (i + 1) * LANES] for i in range(wide.shape[1] // LANES)]
    return functools.reduce(lambda a, b: a + b, pieces)


def fold_rows(tall):
    return jnp.sum(tall.reshape(-1, 8, tall.shape[1]), axis=0)


def repeat_out(out_ref, block):
    out_ref[...] = jnp.broadcast_to(block[None], out_ref.shape)


def unit_kernel(teacher_ref, student_ref, vt_ref, vs_ref, norm_ref):
    def unit(ref, out_ref):
        wide = ref[...].astype(jnp.float32)
        norm = jnp.sqrt(jnp.sum(wide * wide, axis=0, keepdims=True) + EPS)
        out_ref[...] = (wide / norm).astype(jnp.bfloat16)
        return norm

    unit(teacher_ref, vt_ref)
    norm_ref[...] = unit(student_ref, vs_ref)


def halves_kernel(core_ref, hidden_ref, weight_ref, kept_ref, sent_ref, out_ref):
    width = kept_ref.shape[1]
    repeat_out(out_ref, weight_ref[...])

    def split(even_ref, odd_ref):
        for start in range(0, width, LANES):
            cols = slice(start, start + LANES)
            even_ref[:, cols] = hidden_ref[:, 2 * start : 2 * start + LANES]
            odd_ref[:, cols] = hidden_ref[:, 2 * start + LANES : 2 * start + 2 * LANES]

    @pl.when(core_ref[0] == 0)
    def _():
        split(kept_ref, sent_ref)

    @pl.when(core_ref[0] != 0)
    def _():
        split(sent_ref, kept_ref)


def project_kernel(hidden_ref, weight_ref, out_ref):
    @pl.when(pl.program_id(0) == 0)
    def _():
        out_ref[...] = jnp.zeros_like(out_ref)

    out_ref[...] += jnp.dot(hidden_ref[...], weight_ref[...], preferred_element_type=jnp.float32)


def first_kernel(z_ref, v_ref, exp_ref, out_ref, acc):
    step = pl.program_id(0)
    width = v_ref.shape[1]

    @pl.when(step == 0)
    def _():
        acc[...] = jnp.zeros_like(acc)

    for start in range(0, width, CHUNK):
        cols = slice(start, start + CHUNK)
        product = jnp.dot(z_ref[...], v_ref[:, cols], preferred_element_type=jnp.float32)
        block = jnp.exp(product * (1.0 / TAU_T))
        exp_ref[:, cols] = block
        acc[:, cols] += fold_rows(block)

    @pl.when(step == pl.num_programs(0) - 1)
    def _():
        repeat_out(out_ref, lane_rows(jnp.sum(acc[...], axis=0, keepdims=True)))


def row_kernel(parts_ref, exp_ref, out_ref, scale, acc):
    step = pl.program_id(0)

    @pl.when(step == 0)
    def _():
        scale[...] = one_row(1.0 / jnp.sum(parts_ref[...], axis=0))

    rows, width = exp_ref.shape
    block = exp_ref[:, 0:LANES] * scale[:, 0:LANES]
    for start in range(LANES, width, LANES):
        cols = slice(start, start + LANES)
        block += exp_ref[:, cols] * scale[:, cols]
    acc[pl.ds(pl.multiple_of(step * rows, rows), rows), :] = block

    @pl.when(step == pl.num_programs(0) - 1)
    def _():
        repeat_out(out_ref, lane_sums(acc[...]))


def column_kernel(parts_ref, exp_ref, out_ref, scale, acc):
    step = pl.program_id(0)

    @pl.when(step == 0)
    def _():
        scale[...] = down(1.0 / jnp.sum(parts_ref[...], axis=0))
        acc[...] = jnp.zeros_like(acc)

    rows, width = exp_ref.shape
    factor = scale[pl.ds(pl.multiple_of(step * rows, rows), rows), :]
    for start in range(0, width, LANES):
        cols = slice(start, start + LANES)
        acc[:, cols] += fold_rows(exp_ref[:, cols] * factor)

    @pl.when(step == pl.num_programs(0) - 1)
    def _():
        repeat_out(out_ref, lane_rows(jnp.sum(acc[...], axis=0, keepdims=True)))


def student_kernel(parts_ref, exp_ref, y_ref, v_ref, out_ref, z_ref, zt_ref, scale, acc):
    step = pl.program_id(0)

    @pl.when(step == 0)
    def _():
        scale[...] = one_row(1.0 / jnp.sum(parts_ref[...], axis=0))

    rows, width = exp_ref.shape
    here = pl.ds(pl.multiple_of(step * rows, rows), rows)
    y = y_ref[...]
    z = y / jnp.sqrt(jnp.sum(y * y, axis=1, keepdims=True) + EPS)
    z_ref[...] = z.astype(jnp.bfloat16)
    zt_ref[...] = z.T.astype(jnp.bfloat16)
    mass = jnp.zeros((rows, LANES), jnp.float32)
    exps = jnp.zeros((rows, LANES), jnp.float32)
    cross = jnp.zeros((rows, LANES), jnp.float32)
    for start in range(0, width, CHUNK):
        cols = slice(start, start + CHUNK)
        scores = jnp.dot(z_ref[...], v_ref[:, cols], preferred_element_type=jnp.float32)
        weighted = exp_ref[:, cols] * scale[:, cols]
        mass += fold_lanes(weighted)
        exps += fold_lanes(jnp.exp(scores * (1.0 / TAU_S)))
        cross += fold_lanes(weighted * scores)
    acc[0, here, :] = mass
    acc[1, here, :] = exps
    acc[2, here, :] = cross

    @pl.when(step == pl.num_programs(0) - 1)
    def _():
        sums = [lane_sums(acc[i]) for i in range(3)]
        repeat_out(out_ref, jnp.concatenate(sums, axis=0))


def gradient_kernel(
    row_parts_ref, col_parts_ref, exp_ref, z_ref, zt_ref, v_ref, dz_ref, dp_ref, dots_ref,
    scale, teacher, student, grad,
):
    step = pl.program_id(0)
    rows, width = exp_ref.shape
    tall = rows // LANES

    @pl.when(step == 0)
    def _():
        sums = jnp.sum(row_parts_ref[...], axis=0)
        factor = GRAD_SCALE / TAU_S
        teacher[...] = down(factor / sums[0:tall])
        student[...] = down(factor / sums[tall : 2 * tall])
        scale[...] = 1.0 / jnp.sum(col_parts_ref[...], axis=0)
        dz_ref[...] = jnp.zeros_like(dz_ref)

    groups = width // LANES
    col = one_row(scale[pl.ds(pl.multiple_of(step * groups, groups), groups), :])
    for start in range(0, rows, ROWS_BLOCK):
        here = slice(start, start + ROWS_BLOCK)
        scores = jnp.dot(z_ref[here, :], v_ref[...], preferred_element_type=jnp.float32)
        prob = jnp.exp(scores * (1.0 / TAU_S))
        for piece in range(0, width, LANES):
            cols = slice(piece, piece + LANES)
            target = exp_ref[here, cols] * col[:, cols] * teacher[here, :]
            grad[here, cols] = (prob[:, cols] * student[here, :] - target).astype(jnp.bfloat16)
        dz_ref[here, :] += lax.dot_general(
            grad[here, :], v_ref[...], COL_DIMS, preferred_element_type=jnp.float32
        )
    dproto = jnp.dot(zt_ref[...], grad[...], preferred_element_type=jnp.float32)
    dp_ref[...] = dproto
    dots_ref[...] = jnp.sum(v_ref[...].astype(jnp.float32) * dproto, axis=0, keepdims=True)


def collect_kernel(proj_ref, dots_ref, loss_ref, out_ref):
    own, bot = proj_ref.shape[1:]
    proj = jnp.sum(proj_ref[...], axis=0)
    dots = dots_ref[...]
    width = dots.shape[1]
    rows = -(-(width + LANES) // bot)
    loss = jnp.broadcast_to(loss_ref[...], (1, rows * bot - width))
    row = jnp.concatenate([dots, loss], axis=1)
    pieces = [row[:, i * bot : (i + 1) * bot] for i in range(rows)]
    pieces.append(jnp.zeros((out_ref.shape[1] - own - rows, bot), jnp.float32))
    repeat_out(out_ref, jnp.concatenate([proj] + pieces, axis=0))


def finish_kernel(parts_ref, dproto_ref, v_ref, norm_ref, proj_ref, grad_ref, loss_ref):
    copies, height, bot = parts_ref.shape
    own = proj_ref.shape[0] // copies
    width = dproto_ref.shape[1] // 2
    rows = -(-(width + LANES) // bot)
    for i in range(copies):
        proj_ref[i * own : (i + 1) * own, :] = parts_ref[i, 0:own, :]
    lines = []
    for side in range(2):
        block = parts_ref[side, own:height, :]
        for i in range(2 + side, copies, 2):
            block = block + parts_ref[i, own:height, :]
        lines.append(jnp.concatenate([block[i : i + 1] for i in range(rows)], axis=1))
    loss_ref[...] = lines[0][:, width : width + LANES]
    for side in range(2):
        cols = slice(side * width, (side + 1) * width)
        dots = lines[side][:, 0:width]
        grad_ref[:, cols] = (dproto_ref[:, cols] - v_ref[:, cols] * dots) / norm_ref[:, cols]


def params(mib):
    return pltpu.CompilerParams(
        dimension_semantics=("arbitrary",), vmem_limit_bytes=mib * MIB
    )


def cost(flops, size, exps=0):
    return pl.CostEstimate(flops=flops, bytes_accessed=size, transcendentals=exps)


def whole(shape):
    return pl.BlockSpec(shape, lambda i: (0,) * len(shape))


def f32(*shape):
    return jax.ShapeDtypeStruct(shape, jnp.float32)


def hbm(array):
    return pltpu.with_memory_space_constraint(array, pltpu.HBM)


def unit_columns(teacher, student):
    bot, width = teacher.shape
    step = width // CHUNK
    wide = student.shape[1] // step
    return pl.pallas_call(
        unit_kernel,
        grid=(step,),
        in_specs=[
            pl.BlockSpec((bot, CHUNK), lambda i: (0, i)),
            pl.BlockSpec((bot, wide), lambda i: (0, i)),
        ],
        out_specs=[
            pl.BlockSpec((bot, CHUNK), lambda i: (0, i)),
            pl.BlockSpec((bot, wide), lambda i: (0, i)),
            pl.BlockSpec((1, wide), lambda i: (0, i)),
        ],
        out_shape=[
            jax.ShapeDtypeStruct(teacher.shape, jnp.bfloat16),
            jax.ShapeDtypeStruct(student.shape, jnp.bfloat16),
            f32(1, student.shape[1]),
        ],
        compiler_params=params(16),
        cost_estimate=cost(4 * (teacher.size + student.size), 4 * (teacher.size + student.size)),
    )(teacher, student)


def depth_halves(hidden, weight, copies):
    half = jax.ShapeDtypeStruct((hidden.shape[0], hidden.shape[1] // 2), hidden.dtype)
    return pl.pallas_call(
        halves_kernel,
        in_specs=[pl.BlockSpec(memory_space=pltpu.SMEM)]
        + [pl.BlockSpec(memory_space=pltpu.VMEM)] * 2,
        out_shape=[half, half, pltpu.HBM((copies,) + weight.shape, weight.dtype)],
        compiler_params=pltpu.CompilerParams(vmem_limit_bytes=8 * MIB),
        cost_estimate=cost(0, 4 * hidden.size + 2 * copies * weight.size),
    )(lax.axis_index("c").reshape(1), hbm(hidden), hbm(weight))


def project(hidden, weight):
    rows, depth = hidden.shape
    bot = weight.shape[1]
    return pl.pallas_call(
        project_kernel,
        grid=(depth // CHUNK,),
        in_specs=[
            pl.BlockSpec((rows, CHUNK), lambda i: (0, i)),
            pl.BlockSpec((CHUNK, bot), lambda i: (i, 0)),
        ],
        out_specs=whole((rows, bot)),
        out_shape=f32(rows, bot),
        compiler_params=params(8),
        cost_estimate=cost(2 * rows * weight.size, 2 * (hidden.size + weight.size)),
    )(hidden, hbm(weight))


def first_pass(z, v, copies):
    rows, bot = z.shape
    width = v.shape[1]
    out = (copies, width // LANES, LANES)
    return pl.pallas_call(
        first_kernel,
        grid=(rows // ROWS_BLOCK,),
        in_specs=[pl.BlockSpec((ROWS_BLOCK, bot), lambda i: (i, 0)), whole(v.shape)],
        out_specs=[pl.BlockSpec((ROWS_BLOCK, width), lambda i: (i, 0)), whole(out)],
        out_shape=[f32(rows, width), f32(*out)],
        scratch_shapes=[pltpu.VMEM((8, width), jnp.float32)],
        compiler_params=params(16),
        cost_estimate=cost(2 * z.size * width, rows * width * 4, rows * width),
    )(z, hbm(v))


def row_pass(parts, exp, copies):
    rows, width = exp.shape
    out = (copies, rows // LANES, LANES)
    return pl.pallas_call(
        row_kernel,
        grid=(rows // ROWS_BLOCK,),
        in_specs=[whole(parts.shape), pl.BlockSpec((ROWS_BLOCK, width), lambda i: (i, 0))],
        out_specs=whole(out),
        out_shape=f32(*out),
        scratch_shapes=[pltpu.VMEM((1, width), jnp.float32), pltpu.VMEM((rows, LANES), jnp.float32)],
        compiler_params=params(12),
        cost_estimate=cost(2 * exp.size, exp.size * 4),
    )(parts, exp)


def column_pass(parts, exp, copies):
    rows, width = exp.shape
    out = (copies, width // LANES, LANES)
    return pl.pallas_call(
        column_kernel,
        grid=(rows // ROWS_BLOCK,),
        in_specs=[whole(parts.shape), pl.BlockSpec((ROWS_BLOCK, width), lambda i: (i, 0))],
        out_specs=whole(out),
        out_shape=f32(*out),
        scratch_shapes=[pltpu.VMEM((rows, LANES), jnp.float32), pltpu.VMEM((8, width), jnp.float32)],
        compiler_params=params(12),
        cost_estimate=cost(2 * exp.size, exp.size * 4),
    )(parts, exp)


def student_pass(parts, exp, y, v, copies):
    rows, width = exp.shape
    bot = y.shape[1]
    out = (copies, 3 * rows // LANES, LANES)
    return pl.pallas_call(
        student_kernel,
        grid=(rows // ROWS_BLOCK,),
        in_specs=[
            whole(parts.shape),
            pl.BlockSpec((ROWS_BLOCK, width), lambda i: (i, 0)),
            pl.BlockSpec((ROWS_BLOCK, bot), lambda i: (i, 0)),
            whole(v.shape),
        ],
        out_specs=[
            whole(out),
            pl.BlockSpec((ROWS_BLOCK, bot), lambda i: (i, 0)),
            pl.BlockSpec((bot, ROWS_BLOCK), lambda i: (0, i)),
        ],
        out_shape=[
            f32(*out),
            jax.ShapeDtypeStruct((rows, bot), jnp.bfloat16),
            jax.ShapeDtypeStruct((bot, rows), jnp.bfloat16),
        ],
        scratch_shapes=[
            pltpu.VMEM((1, width), jnp.float32),
            pltpu.VMEM((3, rows, LANES), jnp.float32),
        ],
        compiler_params=params(16),
        cost_estimate=cost(2 * y.size * width, exp.size * 4, exp.size),
    )(parts, hbm(exp), hbm(y), hbm(v))


def gradient_pass(row_parts, col_parts, exp, z, zt, v):
    rows, width = exp.shape
    bot = z.shape[1]
    return pl.pallas_call(
        gradient_kernel,
        grid=(width // CHUNK,),
        in_specs=[
            whole(row_parts.shape),
            whole(col_parts.shape),
            pl.BlockSpec((rows, CHUNK), lambda i: (0, i)),
            whole(z.shape),
            whole(zt.shape),
            pl.BlockSpec((bot, CHUNK), lambda i: (0, i)),
        ],
        out_specs=[
            whole((rows, bot)),
            pl.BlockSpec((bot, CHUNK), lambda i: (0, i)),
            pl.BlockSpec((1, CHUNK), lambda i: (0, i)),
        ],
        out_shape=[
            pltpu.HBM((rows, bot), jnp.float32),
            pltpu.HBM((bot, width), jnp.float32),
            pltpu.HBM((1, width), jnp.float32),
        ],
        scratch_shapes=[
            pltpu.VMEM((width // LANES, LANES), jnp.float32),
            pltpu.VMEM((rows, LANES), jnp.float32),
            pltpu.VMEM((rows, LANES), jnp.float32),
            pltpu.VMEM((rows, CHUNK), jnp.bfloat16),
        ],
        compiler_params=params(24),
        cost_estimate=cost(6 * z.size * width, exp.size * 4, exp.size),
    )(row_parts, col_parts, hbm(exp), z, zt, hbm(v))


def backward_kernel(parts_ref, y_ref, out_ref):
    dzhat = jnp.sum(parts_ref[...], axis=0)
    y = y_ref[...]
    norm = jnp.sqrt(jnp.sum(y * y, axis=1, keepdims=True) + EPS)
    unit = y / norm
    inner = jnp.sum(unit * dzhat, axis=1, keepdims=True)
    repeat_out(out_ref, ((dzhat - unit * inner) / norm).astype(jnp.bfloat16))


def norm_backward(parts, y, copies):
    return pl.pallas_call(
        backward_kernel,
        out_shape=pltpu.HBM((copies,) + y.shape, jnp.bfloat16),
        compiler_params=pltpu.CompilerParams(vmem_limit_bytes=8 * MIB),
    )(parts, hbm(y))


def local(hid_teacher, hid_student, proj_teacher, proj_student, proto_teacher, proto_student):
    bot = proj_teacher.shape[1]
    half = proto_teacher.shape[1] // lax.axis_size("yh")
    first = lax.axis_index("yh") * half
    columns, planes = lax.axis_size("z"), lax.axis_size(PLANE)

    gathered = lax.all_gather(proj_student, SHARD, axis=0, tiled=True)
    z_own = unit_split(hid_teacher, proj_teacher, planes)
    z_own, proto_teacher, proto_student = lax.optimization_barrier(
        (z_own, proto_teacher, proto_student)
    )
    z_t = exchange(z_own, PLANE).reshape(-1, bot)
    v_t, v_all, norm_all = unit_columns(
        lax.dynamic_slice_in_dim(proto_teacher, first, half, 1), proto_student
    )
    v_s = lax.dynamic_slice_in_dim(v_all, first, half, 1)
    z_t, v_t, v_s = lax.optimization_barrier((z_t, v_t, v_s))
    y_s = project(hid_student, gathered)
    z_t, y_s, hid_student = lax.optimization_barrier((z_t, y_s, hid_student))
    wide_s = lax.all_gather(y_s, PLANE, axis=0, tiled=True)
    hid_group = lax.all_gather(hid_student, SHARD, axis=0, tiled=True)

    teacher_exp, mass = first_pass(z_t, v_t, columns)
    col_parts = exchange(mass, "z")
    for step in range(ITERS - 1):
        row_parts = exchange(row_pass(col_parts, teacher_exp, planes), PLANE)
        col_parts = exchange(column_pass(row_parts, teacher_exp, columns), "z")
    sums, z_s, z_s_t = student_pass(col_parts, teacher_exp, wide_s, v_s, planes)
    sums = exchange(sums, PLANE)
    dzhat_part, dproto_part, dots = gradient_pass(sums, col_parts, teacher_exp, z_s, z_s_t, v_s)

    dzhat_part, y_s, hid_group, v_all, sums = lax.optimization_barrier(
        (dzhat_part, y_s, hid_group, v_all, sums)
    )
    row_mass, expsum, cross = jnp.split(jnp.sum(sums, axis=0), 3, axis=0)
    row_count = y_s.shape[0] * lax.axis_size(DP + SHARD)
    loss_part = jnp.sum(jnp.log(expsum) - cross / row_mass / TAU_S) / row_count
    dproto = lax.psum_scatter(dproto_part, "z", scatter_dimension=0, tiled=True)
    last = dproto.shape[0] // lax.axis_size("yh")
    v_last = lax.dynamic_slice_in_dim(v_all, lax.axis_index(DP) * last, last, 0).astype(jnp.float32)
    swapped = swap(dproto)

    dzhat_parts = exchange(dzhat_part.reshape((planes,) + y_s.shape), PLANE)
    dy_group = exchange(
        norm_backward(dzhat_parts, y_s, lax.axis_size(SHARD)), SHARD
    ).reshape(-1, bot)
    depth = proj_student.shape[0]
    hid_block = lax.dynamic_slice_in_dim(
        hid_group, lax.axis_index(SHARD) * depth, depth, 1
    )
    proj_term = lax.dot_general(hid_block, dy_group, ROW_DIMS, preferred_element_type=jnp.float32)
    proj_parts = exchange(proj_term.reshape(lax.axis_size(DP), -1, bot), DP)
    height = proj_parts.shape[1] + 8 * -(-(half + LANES) // (8 * bot))
    collected = pl.pallas_call(
        collect_kernel,
        out_shape=pltpu.HBM((proj_parts.shape[0], height, bot), jnp.float32),
        compiler_params=pltpu.CompilerParams(vmem_limit_bytes=8 * MIB),
    )(proj_parts, hbm(dots), loss_part.reshape(1, 1))
    grad_proj, grad_proto, loss = pl.pallas_call(
        finish_kernel,
        out_shape=[f32(depth, bot), f32(last, 2 * half), f32(1, LANES)],
        compiler_params=pltpu.CompilerParams(vmem_limit_bytes=12 * MIB),
    )(exchange(collected, DP), hbm(swapped), hbm(v_last), hbm(norm_all))
    return (loss[0, 0], grad_proj, grad_proto)


def solution(mesh):
    fine = Mesh(mesh.devices.reshape(8, 2, 2, 4, 2), DP + SHARD)
    everything = DP + SHARD
    placed = (
        P(everything, None),
        P(everything, None),
        P(SHARD, None),
        P(SHARD, None),
        P(None, SHARD),
        P(None, SHARD),
    )
    return jax.shard_map(
        local,
        mesh=fine,
        in_specs=placed,
        out_specs=(P(), P(SHARD, None), P(DP, SHARD)),
        check_vma=False,
    )
```

```python
import functools

import jax
import jax.numpy as jnp
from jax import lax
from jax.experimental import pallas as pl
from jax.experimental.pallas import tpu as pltpu
from jax.sharding import Mesh, PartitionSpec as P

ITERS = 3
GRAD_SCALE = 256
TAU_T = 0.04
TAU_S = 0.1
EPS = 1e-06
LANES = 128
ROWS_BLOCK = 256
TALL_BLOCK = 512
DEPTH_BLOCK = 1024
CHUNK = 512
MIB = 1024 * 1024
WIRE_SCALE = 4.0
ROW_DIMS = (((0,), (0,)), ((), ()))
COL_DIMS = (((1,), (1,)), ((), ()))

DP = ("z", "yh")
SHARD = ("yl", "x", "c")
PLANE = ("yh", "yl", "x", "c")


def exchange(blocks, axes):
    return lax.all_to_all(blocks, axes, 0, 0, tiled=True)


def over_cores(blocks):
    return lax.ppermute(blocks, "c", [(0, 1), (1, 0)])


def features_kernel(part_ref, got_ref, out_ref):
    y = part_ref[0 : got_ref.shape[0], :] + got_ref[...]
    unit = y / jnp.sqrt(jnp.sum(y * y, axis=1, keepdims=True) + EPS)
    repeat_out(out_ref, unit.astype(jnp.bfloat16))


def unit_split(hidden, weight, copies):
    rows, bot = hidden.shape[0], weight.shape[1]
    kept, sent, repeated = depth_halves(hidden, weight, lax.axis_size(("yl", "x")))
    share = exchange(repeated, ("yl", "x")).reshape(-1, bot)
    both = jnp.concatenate([kept, over_cores(sent)], axis=0)
    part = jnp.dot(both, share, preferred_element_type=jnp.float32)
    return pl.pallas_call(
        features_kernel,
        out_shape=pltpu.HBM((copies, rows, bot), jnp.bfloat16),
        compiler_params=pltpu.CompilerParams(vmem_limit_bytes=8 * MIB),
    )(part, over_cores(part[rows:]))


def swap(block):
    side, count = lax.axis_index("yh"), lax.axis_size("yh")
    rows = block.shape[0] // count
    kept = lax.dynamic_slice_in_dim(block, side * rows, rows, 0)
    sent = lax.dynamic_slice_in_dim(block, (1 - side) * rows, rows, 0)
    got = lax.ppermute(sent, "yh", [(0, 1), (1, 0)])
    return jnp.where(
        side == 0,
        jnp.concatenate([kept, got], axis=1),
        jnp.concatenate([got, kept], axis=1),
    )


def lane_rows(row):
    return jnp.concatenate(
        [row[:, i * LANES : (i + 1) * LANES] for i in range(row.shape[1] // LANES)], axis=0
    )


def one_row(block):
    return jnp.concatenate([block[i : i + 1] for i in range(block.shape[0])], axis=1)


def down(block):
    return jnp.concatenate(
        [
            jnp.broadcast_to(block[i : i + 1], (LANES, LANES)).T
            for i in range(block.shape[0])
        ],
        axis=0,
    )


def lane_sums(wide):
    ones = jnp.ones((8, LANES), jnp.float32)
    row = lax.dot_general(
        ones, wide, COL_DIMS, precision=lax.Precision.HIGHEST, preferred_element_type=jnp.float32
    )
    return lane_rows(row[0:1])


def fold_lanes(wide):
    pieces = [wide[:, i * LANES : (i + 1) * LANES] for i in range(wide.shape[1] // LANES)]
    return functools.reduce(lambda a, b: a + b, pieces)


def fold_rows(tall):
    return jnp.sum(tall.reshape(-1, 8, tall.shape[1]), axis=0)


def repeat_out(out_ref, block):
    out_ref[...] = jnp.broadcast_to(block[None], out_ref.shape)


def unit_kernel(teacher_ref, student_ref, vt_ref, vs_ref, norm_ref):
    def unit(ref, out_ref):
        wide = ref[...].astype(jnp.float32)
        norm = jnp.sqrt(jnp.sum(wide * wide, axis=0, keepdims=True) + EPS)
        out_ref[...] = (wide / norm).astype(jnp.bfloat16)
        return norm

    unit(teacher_ref, vt_ref)
    norm_ref[...] = unit(student_ref, vs_ref)


def halves_kernel(core_ref, hidden_ref, weight_ref, kept_ref, sent_ref, out_ref):
    width = kept_ref.shape[1]
    repeat_out(out_ref, weight_ref[...])

    def split(even_ref, odd_ref):
        for start in range(0, width, LANES):
            cols = slice(start, start + LANES)
            even_ref[:, cols] = hidden_ref[:, 2 * start : 2 * start + LANES]
            odd_ref[:, cols] = hidden_ref[:, 2 * start + LANES : 2 * start + 2 * LANES]

    @pl.when(core_ref[0] == 0)
    def _():
        split(kept_ref, sent_ref)

    @pl.when(core_ref[0] != 0)
    def _():
        split(sent_ref, kept_ref)


def project_kernel(hidden_ref, weight_ref, out_ref):
    @pl.when(pl.program_id(0) == 0)
    def _():
        out_ref[...] = jnp.zeros_like(out_ref)

    out_ref[...] += jnp.dot(hidden_ref[...], weight_ref[...], preferred_element_type=jnp.float32)


def first_kernel(z_ref, v_ref, exp_ref, out_ref, acc):
    step = pl.program_id(0)
    width = v_ref.shape[1]

    @pl.when(step == 0)
    def _():
        acc[...] = jnp.zeros_like(acc)

    for start in range(0, width, CHUNK):
        cols = slice(start, start + CHUNK)
        product = jnp.dot(z_ref[...], v_ref[:, cols], preferred_element_type=jnp.float32)
        block = jnp.exp(product * (1.0 / TAU_T))
        exp_ref[:, cols] = block
        acc[:, cols] += fold_rows(block)

    @pl.when(step == pl.num_programs(0) - 1)
    def _():
        repeat_out(out_ref, lane_rows(jnp.sum(acc[...], axis=0, keepdims=True)))


def row_kernel(parts_ref, exp_ref, out_ref, scale, acc):
    step = pl.program_id(0)

    @pl.when(step == 0)
    def _():
        scale[...] = one_row(1.0 / jnp.sum(parts_ref[...], axis=0))

    rows, width = exp_ref.shape
    block = exp_ref[:, 0:LANES] * scale[:, 0:LANES]
    for start in range(LANES, width, LANES):
        cols = slice(start, start + LANES)
        block += exp_ref[:, cols] * scale[:, cols]
    acc[pl.ds(pl.multiple_of(step * rows, rows), rows), :] = block

    @pl.when(step == pl.num_programs(0) - 1)
    def _():
        repeat_out(out_ref, lane_sums(acc[...]))


def column_kernel(parts_ref, exp_ref, out_ref, scale, acc):
    step = pl.program_id(0)

    @pl.when(step == 0)
    def _():
        scale[...] = down(1.0 / jnp.sum(parts_ref[...], axis=0))
        acc[...] = jnp.zeros_like(acc)

    rows, width = exp_ref.shape
    factor = scale[pl.ds(pl.multiple_of(step * rows, rows), rows), :]
    for start in range(0, width, LANES):
        cols = slice(start, start + LANES)
        acc[:, cols] += fold_rows(exp_ref[:, cols] * factor)

    @pl.when(step == pl.num_programs(0) - 1)
    def _():
        repeat_out(out_ref, lane_rows(jnp.sum(acc[...], axis=0, keepdims=True)))


def student_kernel(parts_ref, exp_ref, y_ref, v_ref, out_ref, z_ref, zt_ref, scale, acc):
    step = pl.program_id(0)

    @pl.when(step == 0)
    def _():
        scale[...] = one_row(1.0 / jnp.sum(parts_ref[...], axis=0))

    rows, width = exp_ref.shape
    here = pl.ds(pl.multiple_of(step * rows, rows), rows)
    y = y_ref[...]
    z = y / jnp.sqrt(jnp.sum(y * y, axis=1, keepdims=True) + EPS)
    z_ref[...] = z.astype(jnp.bfloat16)
    zt_ref[...] = z.T.astype(jnp.bfloat16)
    mass = jnp.zeros((rows, LANES), jnp.float32)
    exps = jnp.zeros((rows, LANES), jnp.float32)
    cross = jnp.zeros((rows, LANES), jnp.float32)
    for start in range(0, width, CHUNK):
        cols = slice(start, start + CHUNK)
        scores = jnp.dot(z_ref[...], v_ref[:, cols], preferred_element_type=jnp.float32)
        weighted = exp_ref[:, cols] * scale[:, cols]
        mass += fold_lanes(weighted)
        exps += fold_lanes(jnp.exp(scores * (1.0 / TAU_S)))
        cross += fold_lanes(weighted * scores)
    acc[0, here, :] = mass
    acc[1, here, :] = exps
    acc[2, here, :] = cross

    @pl.when(step == pl.num_programs(0) - 1)
    def _():
        sums = [lane_sums(acc[i]) for i in range(3)]
        repeat_out(out_ref, jnp.concatenate(sums, axis=0))


def gradient_kernel(
    row_parts_ref, col_parts_ref, exp_ref, z_ref, zt_ref, v_ref, y_ref, dy_ref, dp_ref, dots_ref,
    scale, teacher, student, grad, dz,
):
    step = pl.program_id(0)
    rows, width = exp_ref.shape
    tall = rows // LANES

    @pl.when(step == 0)
    def _():
        sums = jnp.sum(row_parts_ref[...], axis=0)
        factor = GRAD_SCALE / TAU_S
        teacher[...] = down(factor / sums[0:tall])
        student[...] = down(factor / sums[tall : 2 * tall])
        scale[...] = 1.0 / jnp.sum(col_parts_ref[...], axis=0)
        dz[...] = jnp.zeros_like(dz)

    groups = width // LANES
    col = one_row(scale[pl.ds(pl.multiple_of(step * groups, groups), groups), :])
    for start in range(0, rows, ROWS_BLOCK):
        here = slice(start, start + ROWS_BLOCK)
        scores = jnp.dot(z_ref[here, :], v_ref[...], preferred_element_type=jnp.float32)
        prob = jnp.exp(scores * (1.0 / TAU_S))
        for piece in range(0, width, LANES):
            cols = slice(piece, piece + LANES)
            target = exp_ref[here, cols] * col[:, cols] * teacher[here, :]
            grad[here, cols] = (prob[:, cols] * student[here, :] - target).astype(jnp.bfloat16)
        dz[here, :] += lax.dot_general(
            grad[here, :], v_ref[...], COL_DIMS, preferred_element_type=jnp.float32
        )
    dproto = jnp.dot(zt_ref[...], grad[...], preferred_element_type=jnp.float32)
    dp_ref[...] = dproto
    dots_ref[...] = jnp.sum(v_ref[...].astype(jnp.float32) * dproto, axis=0, keepdims=True)

    @pl.when(step == pl.num_programs(0) - 1)
    def _():
        for start in range(0, rows, ROWS_BLOCK):
            here = slice(start, start + ROWS_BLOCK)
            y = y_ref[here, :]
            part = dz[here, :]
            square = jnp.sum(y * y, axis=1, keepdims=True) + EPS
            inner = jnp.sum(y * part, axis=1, keepdims=True)
            dy_ref[here, :] = part - y * (inner / square)


def collect_kernel(proj_ref, dots_ref, loss_ref, out_ref):
    own, bot = proj_ref.shape[1:]
    proj = jnp.sum(proj_ref[...], axis=0)
    dots = dots_ref[...]
    width = dots.shape[1]
    rows = -(-(width + LANES) // bot)
    loss = jnp.broadcast_to(loss_ref[...], (1, rows * bot - width))
    row = jnp.concatenate([dots, loss], axis=1)
    pieces = [row[:, i * bot : (i + 1) * bot] for i in range(rows)]
    pieces.append(jnp.zeros((out_ref.shape[1] - own - rows, bot), jnp.float32))
    repeat_out(out_ref, jnp.concatenate([proj] + pieces, axis=0))


def finish_kernel(parts_ref, dproto_ref, v_ref, norm_ref, proj_ref, grad_ref, loss_ref):
    copies, height, bot = parts_ref.shape
    own = proj_ref.shape[0] // copies
    width = dproto_ref.shape[1] // 2
    rows = -(-(width + LANES) // bot)
    for i in range(copies):
        proj_ref[i * own : (i + 1) * own, :] = parts_ref[i, 0:own, :]
    lines = []
    for side in range(2):
        block = parts_ref[side, own:height, :]
        for i in range(2 + side, copies, 2):
            block = block + parts_ref[i, own:height, :]
        lines.append(jnp.concatenate([block[i : i + 1] for i in range(rows)], axis=1))
    loss_ref[...] = lines[0][:, width : width + LANES]
    for side in range(2):
        cols = slice(side * width, (side + 1) * width)
        dots = lines[side][:, 0:width]
        grad_ref[:, cols] = (dproto_ref[:, cols] - v_ref[:, cols] * dots) / norm_ref[:, cols]


def params(mib):
    return pltpu.CompilerParams(
        dimension_semantics=("arbitrary",), vmem_limit_bytes=mib * MIB
    )


def cost(flops, size, exps=0):
    return pl.CostEstimate(flops=flops, bytes_accessed=size, transcendentals=exps)


def whole(shape):
    return pl.BlockSpec(shape, lambda i: (0,) * len(shape))


def f32(*shape):
    return jax.ShapeDtypeStruct(shape, jnp.float32)


def hbm(array):
    return pltpu.with_memory_space_constraint(array, pltpu.HBM)


def unit_columns(teacher, student):
    bot, width = teacher.shape
    step = width // CHUNK
    wide = student.shape[1] // step
    return pl.pallas_call(
        unit_kernel,
        grid=(step,),
        in_specs=[
            pl.BlockSpec((bot, CHUNK), lambda i: (0, i)),
            pl.BlockSpec((bot, wide), lambda i: (0, i)),
        ],
        out_specs=[
            pl.BlockSpec((bot, CHUNK), lambda i: (0, i)),
            pl.BlockSpec((bot, wide), lambda i: (0, i)),
            pl.BlockSpec((1, wide), lambda i: (0, i)),
        ],
        out_shape=[
            jax.ShapeDtypeStruct(teacher.shape, jnp.bfloat16),
            jax.ShapeDtypeStruct(student.shape, jnp.bfloat16),
            f32(1, student.shape[1]),
        ],
        compiler_params=params(20),
        cost_estimate=cost(4 * (teacher.size + student.size), 4 * (teacher.size + student.size)),
    )(teacher, student)


def depth_halves(hidden, weight, copies):
    half = jax.ShapeDtypeStruct((hidden.shape[0], hidden.shape[1] // 2), hidden.dtype)
    return pl.pallas_call(
        halves_kernel,
        in_specs=[pl.BlockSpec(memory_space=pltpu.SMEM)]
        + [pl.BlockSpec(memory_space=pltpu.VMEM)] * 2,
        out_shape=[half, half, pltpu.HBM((copies,) + weight.shape, weight.dtype)],
        compiler_params=pltpu.CompilerParams(vmem_limit_bytes=8 * MIB),
        cost_estimate=cost(0, 4 * hidden.size + 2 * copies * weight.size),
    )(lax.axis_index("c").reshape(1), hbm(hidden), hbm(weight))


def project(hidden, weight):
    rows, depth = hidden.shape
    bot = weight.shape[1]
    return pl.pallas_call(
        project_kernel,
        grid=(depth // DEPTH_BLOCK,),
        in_specs=[
            pl.BlockSpec((rows, DEPTH_BLOCK), lambda i: (0, i)),
            pl.BlockSpec((DEPTH_BLOCK, bot), lambda i: (i, 0)),
        ],
        out_specs=whole((rows, bot)),
        out_shape=f32(rows, bot),
        compiler_params=params(8),
        cost_estimate=cost(2 * rows * weight.size, 2 * (hidden.size + weight.size)),
    )(hidden, hbm(weight))


def first_pass(z, v, copies):
    rows, bot = z.shape
    width = v.shape[1]
    out = (copies, width // LANES, LANES)
    return pl.pallas_call(
        first_kernel,
        grid=(rows // TALL_BLOCK,),
        in_specs=[pl.BlockSpec((TALL_BLOCK, bot), lambda i: (i, 0)), whole(v.shape)],
        out_specs=[pl.BlockSpec((TALL_BLOCK, width), lambda i: (i, 0)), whole(out)],
        out_shape=[f32(rows, width), f32(*out)],
        scratch_shapes=[pltpu.VMEM((8, width), jnp.float32)],
        compiler_params=params(20),
        cost_estimate=cost(2 * z.size * width, rows * width * 4, rows * width),
    )(z, hbm(v))


def row_pass(parts, exp, copies):
    rows, width = exp.shape
    out = (copies, rows // LANES, LANES)
    return pl.pallas_call(
        row_kernel,
        grid=(rows // ROWS_BLOCK,),
        in_specs=[whole(parts.shape), pl.BlockSpec((ROWS_BLOCK, width), lambda i: (i, 0))],
        out_specs=whole(out),
        out_shape=f32(*out),
        scratch_shapes=[pltpu.VMEM((1, width), jnp.float32), pltpu.VMEM((rows, LANES), jnp.float32)],
        compiler_params=params(20),
        cost_estimate=cost(2 * exp.size, exp.size * 4),
    )(parts, exp)


def column_pass(parts, exp, copies):
    rows, width = exp.shape
    out = (copies, width // LANES, LANES)
    return pl.pallas_call(
        column_kernel,
        grid=(rows // ROWS_BLOCK,),
        in_specs=[whole(parts.shape), pl.BlockSpec((ROWS_BLOCK, width), lambda i: (i, 0))],
        out_specs=whole(out),
        out_shape=f32(*out),
        scratch_shapes=[pltpu.VMEM((rows, LANES), jnp.float32), pltpu.VMEM((8, width), jnp.float32)],
        compiler_params=params(20),
        cost_estimate=cost(2 * exp.size, exp.size * 4),
    )(parts, exp)


def student_pass(parts, exp, y, v, copies):
    rows, width = exp.shape
    bot = y.shape[1]
    out = (copies, 3 * rows // LANES, LANES)
    return pl.pallas_call(
        student_kernel,
        grid=(rows // ROWS_BLOCK,),
        in_specs=[
            whole(parts.shape),
            pl.BlockSpec((ROWS_BLOCK, width), lambda i: (i, 0)),
            pl.BlockSpec((ROWS_BLOCK, bot), lambda i: (i, 0)),
            whole(v.shape),
        ],
        out_specs=[
            whole(out),
            pl.BlockSpec((ROWS_BLOCK, bot), lambda i: (i, 0)),
            pl.BlockSpec((bot, ROWS_BLOCK), lambda i: (0, i)),
        ],
        out_shape=[
            f32(*out),
            jax.ShapeDtypeStruct((rows, bot), jnp.bfloat16),
            jax.ShapeDtypeStruct((bot, rows), jnp.bfloat16),
        ],
        scratch_shapes=[
            pltpu.VMEM((1, width), jnp.float32),
            pltpu.VMEM((3, rows, LANES), jnp.float32),
        ],
        compiler_params=params(20),
        cost_estimate=cost(2 * y.size * width, exp.size * 4, exp.size),
    )(parts, hbm(exp), hbm(y), hbm(v))


def gradient_pass(row_parts, col_parts, exp, z, zt, v, y):
    rows, width = exp.shape
    bot = z.shape[1]
    return pl.pallas_call(
        gradient_kernel,
        grid=(width // CHUNK,),
        in_specs=[
            whole(row_parts.shape),
            whole(col_parts.shape),
            pl.BlockSpec((rows, CHUNK), lambda i: (0, i)),
            whole(z.shape),
            whole(zt.shape),
            pl.BlockSpec((bot, CHUNK), lambda i: (0, i)),
            whole(y.shape),
        ],
        out_specs=[
            whole((rows, bot)),
            pl.BlockSpec((bot, CHUNK), lambda i: (0, i)),
            pl.BlockSpec((1, CHUNK), lambda i: (0, i)),
        ],
        out_shape=[
            pltpu.HBM((rows, bot), jnp.float32),
            pltpu.HBM((bot, width), jnp.float32),
            pltpu.HBM((1, width), jnp.float32),
        ],
        scratch_shapes=[
            pltpu.VMEM((width // LANES, LANES), jnp.float32),
            pltpu.VMEM((rows, LANES), jnp.float32),
            pltpu.VMEM((rows, LANES), jnp.float32),
            pltpu.VMEM((rows, CHUNK), jnp.bfloat16),
            pltpu.VMEM((rows, bot), jnp.float32),
        ],
        compiler_params=params(20),
        cost_estimate=cost(6 * z.size * width, exp.size * 4, exp.size),
    )(row_parts, col_parts, exp, z, zt, v, y)


def backward_kernel(sum_ref, y_ref, out_ref):
    y = y_ref[...]
    norm = jnp.sqrt(jnp.sum(y * y, axis=1, keepdims=True) + EPS)
    repeat_out(out_ref, (sum_ref[...] / norm).astype(jnp.bfloat16))


def norm_backward(total, y, copies):
    return pl.pallas_call(
        backward_kernel,
        out_shape=pltpu.HBM((copies,) + y.shape, jnp.bfloat16),
        compiler_params=pltpu.CompilerParams(vmem_limit_bytes=8 * MIB),
    )(total, hbm(y))


def local(hid_teacher, hid_student, proj_teacher, proj_student, proto_teacher, proto_student):
    bot = proj_teacher.shape[1]
    half = proto_teacher.shape[1] // lax.axis_size("yh")
    first = lax.axis_index("yh") * half
    columns, planes = lax.axis_size("z"), lax.axis_size(PLANE)

    gathered = lax.all_gather(proj_student, SHARD, axis=0, tiled=True)
    z_own = unit_split(hid_teacher, proj_teacher, planes)
    z_own, proto_teacher, proto_student = lax.optimization_barrier(
        (z_own, proto_teacher, proto_student)
    )
    z_t = exchange(z_own, PLANE).reshape(-1, bot)
    v_t, v_all, norm_all = unit_columns(
        lax.dynamic_slice_in_dim(proto_teacher, first, half, 1), proto_student
    )
    v_s = lax.dynamic_slice_in_dim(v_all, first, half, 1)
    z_t, v_t, v_s = lax.optimization_barrier((z_t, v_t, v_s))
    y_s = project(hid_student, gathered)
    z_t, y_s, hid_student = lax.optimization_barrier((z_t, y_s, hid_student))
    wide_s = lax.all_gather(y_s, PLANE, axis=0, tiled=True)
    hid_group = lax.all_gather(hid_student, SHARD, axis=0, tiled=True)

    teacher_exp, mass = first_pass(z_t, v_t, columns)
    col_parts = exchange(mass, "z")
    for step in range(ITERS - 1):
        row_parts = exchange(row_pass(col_parts, teacher_exp, planes), PLANE)
        mass = column_pass(row_parts, teacher_exp, columns)
        if step == ITERS - 2:
            mass, wide_s = lax.optimization_barrier((mass, wide_s))
        col_parts = exchange(mass, "z")
    sums, z_s, z_s_t = student_pass(col_parts, teacher_exp, wide_s, v_s, planes)
    sums = exchange(sums, PLANE)
    dy_part, dproto_part, dots = gradient_pass(
        sums, col_parts, teacher_exp, z_s, z_s_t, v_s, wide_s
    )

    dy_part, hid_group, v_all, sums = lax.optimization_barrier((dy_part, hid_group, v_all, sums))
    row_mass, expsum, cross = jnp.split(jnp.sum(sums, axis=0), 3, axis=0)
    row_count = y_s.shape[0] * lax.axis_size(DP + SHARD)
    loss_part = jnp.sum(jnp.log(expsum) - cross / row_mass / TAU_S) / row_count
    dproto = lax.psum_scatter(dproto_part, "z", scatter_dimension=0, tiled=True)
    last = dproto.shape[0] // lax.axis_size("yh")
    v_last = lax.dynamic_slice_in_dim(v_all, lax.axis_index(DP) * last, last, 0).astype(jnp.float32)
    swapped = swap(dproto)

    parts = (dy_part * WIRE_SCALE).astype(jnp.float16).reshape((planes,) + y_s.shape)
    tangent = jnp.sum(exchange(parts, PLANE).astype(jnp.float32), axis=0) * (1.0 / WIRE_SCALE)
    dy_group = exchange(
        norm_backward(tangent, y_s, lax.axis_size(SHARD)), SHARD
    ).reshape(-1, bot)
    depth = proj_student.shape[0]
    hid_block = lax.dynamic_slice_in_dim(
        hid_group, lax.axis_index(SHARD) * depth, depth, 1
    )
    proj_term = lax.dot_general(hid_block, dy_group, ROW_DIMS, preferred_element_type=jnp.float32)
    proj_parts = exchange(proj_term.reshape(lax.axis_size(DP), -1, bot), DP)
    height = proj_parts.shape[1] + 8 * -(-(half + LANES) // (8 * bot))
    collected = pl.pallas_call(
        collect_kernel,
        out_shape=pltpu.HBM((proj_parts.shape[0], height, bot), jnp.float32),
        compiler_params=pltpu.CompilerParams(vmem_limit_bytes=8 * MIB),
    )(proj_parts, hbm(dots), loss_part.reshape(1, 1))
    grad_proj, grad_proto, loss = pl.pallas_call(
        finish_kernel,
        out_shape=[f32(depth, bot), f32(last, 2 * half), f32(1, LANES)],
        compiler_params=pltpu.CompilerParams(vmem_limit_bytes=12 * MIB),
    )(exchange(collected, DP), hbm(swapped), hbm(v_last), hbm(norm_all))
    return (loss[0, 0], grad_proj, grad_proto)


def solution(mesh):
    fine = Mesh(mesh.devices.reshape(8, 2, 2, 4, 2), DP + SHARD)
    everything = DP + SHARD
    placed = (
        P(everything, None),
        P(everything, None),
        P(SHARD, None),
        P(SHARD, None),
        P(None, SHARD),
        P(None, SHARD),
    )
    return jax.shard_map(
        local,
        mesh=fine,
        in_specs=placed,
        out_specs=(P(), P(SHARD, None), P(DP, SHARD)),
        check_vma=False,
    )
```

```python
import functools

import jax
import jax.numpy as jnp
from jax import lax
from jax.experimental import pallas as pl
from jax.experimental.pallas import tpu as pltpu
from jax.sharding import Mesh, PartitionSpec as P

ITERS = 3
GRAD_SCALE = 256
TAU_T = 0.04
TAU_S = 0.1
EPS = 1e-06
LANES = 128
ROWS_BLOCK = 256
TALL_BLOCK = 512
DEPTH_BLOCK = 1024
CHUNK = 512
MIB = 1024 * 1024
WIRE_SCALE = 4.0
ROW_DIMS = (((0,), (0,)), ((), ()))
COL_DIMS = (((1,), (1,)), ((), ()))

DP = ("z", "yh")
SHARD = ("yl", "x", "c")
PLANE = ("yh", "yl", "x", "c")


def exchange(blocks, axes):
    return lax.all_to_all(blocks, axes, 0, 0, tiled=True)


def over_cores(blocks):
    return lax.ppermute(blocks, "c", [(0, 1), (1, 0)])


def features_kernel(part_ref, got_ref, out_ref):
    y = part_ref[0 : got_ref.shape[0], :] + got_ref[...]
    unit = y / jnp.sqrt(jnp.sum(y * y, axis=1, keepdims=True) + EPS)
    repeat_out(out_ref, unit.astype(jnp.bfloat16))


def unit_split(hidden, weight, copies):
    rows, bot = hidden.shape[0], weight.shape[1]
    kept, sent, repeated = depth_halves(hidden, weight, lax.axis_size(("yl", "x")))
    share = exchange(repeated, ("yl", "x")).reshape(-1, bot)
    both = jnp.concatenate([kept, over_cores(sent)], axis=0)
    part = jnp.dot(both, share, preferred_element_type=jnp.float32)
    return pl.pallas_call(
        features_kernel,
        out_shape=pltpu.HBM((copies, rows, bot), jnp.bfloat16),
        compiler_params=pltpu.CompilerParams(vmem_limit_bytes=8 * MIB),
    )(part, over_cores(part[rows:]))


def swap(block):
    side, count = lax.axis_index("yh"), lax.axis_size("yh")
    rows = block.shape[0] // count
    kept = lax.dynamic_slice_in_dim(block, side * rows, rows, 0)
    sent = lax.dynamic_slice_in_dim(block, (1 - side) * rows, rows, 0)
    got = lax.ppermute(sent, "yh", [(0, 1), (1, 0)])
    return jnp.where(
        side == 0,
        jnp.concatenate([kept, got], axis=1),
        jnp.concatenate([got, kept], axis=1),
    )


def lane_rows(row):
    return jnp.concatenate(
        [row[:, i * LANES : (i + 1) * LANES] for i in range(row.shape[1] // LANES)], axis=0
    )


def one_row(block):
    return jnp.concatenate([block[i : i + 1] for i in range(block.shape[0])], axis=1)


def down(block):
    return jnp.concatenate(
        [
            jnp.broadcast_to(block[i : i + 1], (LANES, LANES)).T
            for i in range(block.shape[0])
        ],
        axis=0,
    )


def lane_sums(wide):
    ones = jnp.ones((8, LANES), jnp.float32)
    row = lax.dot_general(
        ones, wide, COL_DIMS, precision=lax.Precision.HIGHEST, preferred_element_type=jnp.float32
    )
    return lane_rows(row[0:1])


def fold_lanes(wide):
    pieces = [wide[:, i * LANES : (i + 1) * LANES] for i in range(wide.shape[1] // LANES)]
    return functools.reduce(lambda a, b: a + b, pieces)


def fold_rows(tall):
    return jnp.sum(tall.reshape(-1, 8, tall.shape[1]), axis=0)


def repeat_out(out_ref, block):
    out_ref[...] = jnp.broadcast_to(block[None], out_ref.shape)


def unit_kernel(teacher_ref, student_ref, vt_ref, vs_ref, norm_ref):
    def unit(ref, out_ref):
        wide = ref[...].astype(jnp.float32)
        norm = jnp.sqrt(jnp.sum(wide * wide, axis=0, keepdims=True) + EPS)
        out_ref[...] = (wide / norm).astype(jnp.bfloat16)
        return norm

    unit(teacher_ref, vt_ref)
    norm_ref[...] = unit(student_ref, vs_ref)


def halves_kernel(core_ref, hidden_ref, weight_ref, kept_ref, sent_ref, out_ref):
    width = kept_ref.shape[1]
    repeat_out(out_ref, weight_ref[...])

    def split(even_ref, odd_ref):
        for start in range(0, width, LANES):
            cols = slice(start, start + LANES)
            even_ref[:, cols] = hidden_ref[:, 2 * start : 2 * start + LANES]
            odd_ref[:, cols] = hidden_ref[:, 2 * start + LANES : 2 * start + 2 * LANES]

    @pl.when(core_ref[0] == 0)
    def _():
        split(kept_ref, sent_ref)

    @pl.when(core_ref[0] != 0)
    def _():
        split(sent_ref, kept_ref)


def project_kernel(hidden_ref, weight_ref, out_ref):
    @pl.when(pl.program_id(0) == 0)
    def _():
        out_ref[...] = jnp.zeros_like(out_ref)

    out_ref[...] += jnp.dot(hidden_ref[...], weight_ref[...], preferred_element_type=jnp.float32)


def first_kernel(z_ref, v_ref, exp_ref, out_ref, acc):
    step = pl.program_id(0)
    width = v_ref.shape[1]

    @pl.when(step == 0)
    def _():
        acc[...] = jnp.zeros_like(acc)

    for start in range(0, width, CHUNK):
        cols = slice(start, start + CHUNK)
        product = jnp.dot(z_ref[...], v_ref[:, cols], preferred_element_type=jnp.float32)
        block = jnp.exp(product * (1.0 / TAU_T))
        exp_ref[:, cols] = block
        acc[:, cols] += fold_rows(block)

    @pl.when(step == pl.num_programs(0) - 1)
    def _():
        repeat_out(out_ref, lane_rows(jnp.sum(acc[...], axis=0, keepdims=True)))


def row_kernel(parts_ref, exp_ref, out_ref, scale, acc):
    step = pl.program_id(0)

    @pl.when(step == 0)
    def _():
        scale[...] = one_row(1.0 / jnp.sum(parts_ref[...], axis=0))

    rows, width = exp_ref.shape
    block = exp_ref[:, 0:LANES] * scale[:, 0:LANES]
    for start in range(LANES, width, LANES):
        cols = slice(start, start + LANES)
        block += exp_ref[:, cols] * scale[:, cols]
    acc[pl.ds(pl.multiple_of(step * rows, rows), rows), :] = block

    @pl.when(step == pl.num_programs(0) - 1)
    def _():
        repeat_out(out_ref, lane_sums(acc[...]))


def column_kernel(parts_ref, exp_ref, out_ref, scale, acc):
    step = pl.program_id(0)

    @pl.when(step == 0)
    def _():
        scale[...] = down(1.0 / jnp.sum(parts_ref[...], axis=0))
        acc[...] = jnp.zeros_like(acc)

    rows, width = exp_ref.shape
    factor = scale[pl.ds(pl.multiple_of(step * rows, rows), rows), :]
    for start in range(0, width, LANES):
        cols = slice(start, start + LANES)
        acc[:, cols] += fold_rows(exp_ref[:, cols] * factor)

    @pl.when(step == pl.num_programs(0) - 1)
    def _():
        repeat_out(out_ref, lane_rows(jnp.sum(acc[...], axis=0, keepdims=True)))


def student_kernel(y_ref, v_ref, z_ref, zt_ref, scores_ref, out_ref, acc):
    step = pl.program_id(0)
    rows, width = scores_ref.shape
    y = y_ref[...]
    z = y / jnp.sqrt(jnp.sum(y * y, axis=1, keepdims=True) + EPS)
    z_ref[...] = z.astype(jnp.bfloat16)
    zt_ref[...] = z.T.astype(jnp.bfloat16)
    exps = jnp.zeros((rows, LANES), jnp.float32)
    for start in range(0, width, CHUNK):
        cols = slice(start, start + CHUNK)
        scores = jnp.dot(z_ref[...], v_ref[:, cols], preferred_element_type=jnp.float32)
        scores_ref[:, cols] = scores.astype(jnp.bfloat16)
        exps += fold_lanes(jnp.exp(scores * (1.0 / TAU_S)))
    acc[pl.ds(pl.multiple_of(step * rows, rows), rows), :] = exps

    @pl.when(step == pl.num_programs(0) - 1)
    def _():
        out_ref[...] = lane_sums(acc[...])


def last_kernel(parts_ref, exps_ref, exp_ref, scores_ref, out_ref, scale, acc):
    step = pl.program_id(0)

    @pl.when(step == 0)
    def _():
        scale[...] = one_row(1.0 / jnp.sum(parts_ref[...], axis=0))

    rows, width = exp_ref.shape
    here = pl.ds(pl.multiple_of(step * rows, rows), rows)
    mass = jnp.zeros((rows, LANES), jnp.float32)
    cross = jnp.zeros((rows, LANES), jnp.float32)
    for start in range(0, width, LANES):
        cols = slice(start, start + LANES)
        weighted = exp_ref[:, cols] * scale[:, cols]
        mass += weighted
        cross += weighted * scores_ref[:, cols].astype(jnp.float32)
    acc[0, here, :] = mass
    acc[1, here, :] = cross

    @pl.when(step == pl.num_programs(0) - 1)
    def _():
        sums = [lane_sums(acc[0]), exps_ref[...], lane_sums(acc[1])]
        repeat_out(out_ref, jnp.concatenate(sums, axis=0))


def gradient_kernel(
    row_parts_ref, col_parts_ref, exp_ref, z_ref, zt_ref, v_ref, y_ref, dy_ref, dp_ref, dots_ref,
    scale, teacher, student, grad, dz,
):
    step = pl.program_id(0)
    rows, width = exp_ref.shape
    tall = rows // LANES

    @pl.when(step == 0)
    def _():
        sums = jnp.sum(row_parts_ref[...], axis=0)
        factor = GRAD_SCALE / TAU_S
        teacher[...] = down(factor / sums[0:tall])
        student[...] = down(factor / sums[tall : 2 * tall])
        scale[...] = 1.0 / jnp.sum(col_parts_ref[...], axis=0)
        dz[...] = jnp.zeros_like(dz)

    groups = width // LANES
    col = one_row(scale[pl.ds(pl.multiple_of(step * groups, groups), groups), :])
    for start in range(0, rows, ROWS_BLOCK):
        here = slice(start, start + ROWS_BLOCK)
        scores = jnp.dot(z_ref[here, :], v_ref[...], preferred_element_type=jnp.float32)
        prob = jnp.exp(scores * (1.0 / TAU_S))
        for piece in range(0, width, LANES):
            cols = slice(piece, piece + LANES)
            target = exp_ref[here, cols] * col[:, cols] * teacher[here, :]
            grad[here, cols] = (prob[:, cols] * student[here, :] - target).astype(jnp.bfloat16)
        dz[here, :] += lax.dot_general(
            grad[here, :], v_ref[...], COL_DIMS, preferred_element_type=jnp.float32
        )
    dproto = jnp.dot(zt_ref[...], grad[...], preferred_element_type=jnp.float32)
    dp_ref[...] = dproto
    dots_ref[...] = jnp.sum(v_ref[...].astype(jnp.float32) * dproto, axis=0, keepdims=True)

    @pl.when(step == pl.num_programs(0) - 1)
    def _():
        for start in range(0, rows, ROWS_BLOCK):
            here = slice(start, start + ROWS_BLOCK)
            y = y_ref[here, :]
            part = dz[here, :]
            square = jnp.sum(y * y, axis=1, keepdims=True) + EPS
            inner = jnp.sum(y * part, axis=1, keepdims=True)
            dy_ref[here, :] = part - y * (inner / square)


def collect_kernel(proj_ref, dots_ref, loss_ref, out_ref):
    own, bot = proj_ref.shape[1:]
    proj = jnp.sum(proj_ref[...], axis=0)
    dots = dots_ref[...]
    width = dots.shape[1]
    rows = -(-(width + LANES) // bot)
    loss = jnp.broadcast_to(loss_ref[...], (1, rows * bot - width))
    row = jnp.concatenate([dots, loss], axis=1)
    pieces = [row[:, i * bot : (i + 1) * bot] for i in range(rows)]
    pieces.append(jnp.zeros((out_ref.shape[1] - own - rows, bot), jnp.float32))
    repeat_out(out_ref, jnp.concatenate([proj] + pieces, axis=0))


def finish_kernel(parts_ref, dproto_ref, v_ref, norm_ref, proj_ref, grad_ref, loss_ref):
    copies, height, bot = parts_ref.shape
    own = proj_ref.shape[0] // copies
    width = dproto_ref.shape[1] // 2
    rows = -(-(width + LANES) // bot)
    for i in range(copies):
        proj_ref[i * own : (i + 1) * own, :] = parts_ref[i, 0:own, :]
    lines = []
    for side in range(2):
        block = parts_ref[side, own:height, :]
        for i in range(2 + side, copies, 2):
            block = block + parts_ref[i, own:height, :]
        lines.append(jnp.concatenate([block[i : i + 1] for i in range(rows)], axis=1))
    loss_ref[...] = lines[0][:, width : width + LANES]
    for side in range(2):
        cols = slice(side * width, (side + 1) * width)
        dots = lines[side][:, 0:width]
        grad_ref[:, cols] = (dproto_ref[:, cols] - v_ref[:, cols] * dots) / norm_ref[:, cols]


def params(mib):
    return pltpu.CompilerParams(
        dimension_semantics=("arbitrary",), vmem_limit_bytes=mib * MIB
    )


def cost(flops, size, exps=0):
    return pl.CostEstimate(flops=flops, bytes_accessed=size, transcendentals=exps)


def whole(shape):
    return pl.BlockSpec(shape, lambda i: (0,) * len(shape))


def f32(*shape):
    return jax.ShapeDtypeStruct(shape, jnp.float32)


def hbm(array):
    return pltpu.with_memory_space_constraint(array, pltpu.HBM)


def unit_columns(teacher, student):
    bot, width = teacher.shape
    step = width // CHUNK
    wide = student.shape[1] // step
    return pl.pallas_call(
        unit_kernel,
        grid=(step,),
        in_specs=[
            pl.BlockSpec((bot, CHUNK), lambda i: (0, i)),
            pl.BlockSpec((bot, wide), lambda i: (0, i)),
        ],
        out_specs=[
            pl.BlockSpec((bot, CHUNK), lambda i: (0, i)),
            pl.BlockSpec((bot, wide), lambda i: (0, i)),
            pl.BlockSpec((1, wide), lambda i: (0, i)),
        ],
        out_shape=[
            jax.ShapeDtypeStruct(teacher.shape, jnp.bfloat16),
            jax.ShapeDtypeStruct(student.shape, jnp.bfloat16),
            f32(1, student.shape[1]),
        ],
        compiler_params=params(20),
        cost_estimate=cost(4 * (teacher.size + student.size), 4 * (teacher.size + student.size)),
    )(teacher, student)


def depth_halves(hidden, weight, copies):
    half = jax.ShapeDtypeStruct((hidden.shape[0], hidden.shape[1] // 2), hidden.dtype)
    return pl.pallas_call(
        halves_kernel,
        in_specs=[pl.BlockSpec(memory_space=pltpu.SMEM)]
        + [pl.BlockSpec(memory_space=pltpu.VMEM)] * 2,
        out_shape=[half, half, pltpu.HBM((copies,) + weight.shape, weight.dtype)],
        compiler_params=pltpu.CompilerParams(vmem_limit_bytes=8 * MIB),
        cost_estimate=cost(0, 4 * hidden.size + 2 * copies * weight.size),
    )(lax.axis_index("c").reshape(1), hbm(hidden), hbm(weight))


def project(hidden, weight):
    rows, depth = hidden.shape
    bot = weight.shape[1]
    return pl.pallas_call(
        project_kernel,
        grid=(depth // DEPTH_BLOCK,),
        in_specs=[
            pl.BlockSpec((rows, DEPTH_BLOCK), lambda i: (0, i)),
            pl.BlockSpec((DEPTH_BLOCK, bot), lambda i: (i, 0)),
        ],
        out_specs=whole((rows, bot)),
        out_shape=f32(rows, bot),
        compiler_params=params(8),
        cost_estimate=cost(2 * rows * weight.size, 2 * (hidden.size + weight.size)),
    )(hidden, hbm(weight))


def first_pass(z, v, copies):
    rows, bot = z.shape
    width = v.shape[1]
    out = (copies, width // LANES, LANES)
    return pl.pallas_call(
        first_kernel,
        grid=(rows // TALL_BLOCK,),
        in_specs=[pl.BlockSpec((TALL_BLOCK, bot), lambda i: (i, 0)), whole(v.shape)],
        out_specs=[pl.BlockSpec((TALL_BLOCK, width), lambda i: (i, 0)), whole(out)],
        out_shape=[f32(rows, width), f32(*out)],
        scratch_shapes=[pltpu.VMEM((8, width), jnp.float32)],
        compiler_params=params(20),
        cost_estimate=cost(2 * z.size * width, rows * width * 4, rows * width),
    )(z, hbm(v))


def row_pass(parts, exp, copies):
    rows, width = exp.shape
    out = (copies, rows // LANES, LANES)
    return pl.pallas_call(
        row_kernel,
        grid=(rows // ROWS_BLOCK,),
        in_specs=[whole(parts.shape), pl.BlockSpec((ROWS_BLOCK, width), lambda i: (i, 0))],
        out_specs=whole(out),
        out_shape=f32(*out),
        scratch_shapes=[pltpu.VMEM((1, width), jnp.float32), pltpu.VMEM((rows, LANES), jnp.float32)],
        compiler_params=params(20),
        cost_estimate=cost(2 * exp.size, exp.size * 4),
    )(parts, exp)


def column_pass(parts, exp, copies):
    rows, width = exp.shape
    out = (copies, width // LANES, LANES)
    return pl.pallas_call(
        column_kernel,
        grid=(rows // ROWS_BLOCK,),
        in_specs=[whole(parts.shape), pl.BlockSpec((ROWS_BLOCK, width), lambda i: (i, 0))],
        out_specs=whole(out),
        out_shape=f32(*out),
        scratch_shapes=[pltpu.VMEM((rows, LANES), jnp.float32), pltpu.VMEM((8, width), jnp.float32)],
        compiler_params=params(20),
        cost_estimate=cost(2 * exp.size, exp.size * 4),
    )(parts, exp)


def student_pass(y, v):
    rows, bot = y.shape
    width = v.shape[1]
    return pl.pallas_call(
        student_kernel,
        grid=(rows // ROWS_BLOCK,),
        in_specs=[pl.BlockSpec((ROWS_BLOCK, bot), lambda i: (i, 0)), whole(v.shape)],
        out_specs=[
            pl.BlockSpec((ROWS_BLOCK, bot), lambda i: (i, 0)),
            pl.BlockSpec((bot, ROWS_BLOCK), lambda i: (0, i)),
            pl.BlockSpec((ROWS_BLOCK, width), lambda i: (i, 0)),
            whole((rows // LANES, LANES)),
        ],
        out_shape=[
            jax.ShapeDtypeStruct((rows, bot), jnp.bfloat16),
            jax.ShapeDtypeStruct((bot, rows), jnp.bfloat16),
            pltpu.HBM((rows, width), jnp.bfloat16),
            f32(rows // LANES, LANES),
        ],
        scratch_shapes=[pltpu.VMEM((rows, LANES), jnp.float32)],
        compiler_params=params(20),
        cost_estimate=cost(2 * y.size * width, rows * width * 4, rows * width),
    )(hbm(y), hbm(v))


def last_pass(parts, exps, exp, scores, copies):
    rows, width = exp.shape
    out = (copies, 3 * rows // LANES, LANES)
    return pl.pallas_call(
        last_kernel,
        grid=(rows // ROWS_BLOCK,),
        in_specs=[
            whole(parts.shape),
            whole(exps.shape),
            pl.BlockSpec((ROWS_BLOCK, width), lambda i: (i, 0)),
            pl.BlockSpec((ROWS_BLOCK, width), lambda i: (i, 0)),
        ],
        out_specs=whole(out),
        out_shape=f32(*out),
        scratch_shapes=[
            pltpu.VMEM((1, width), jnp.float32),
            pltpu.VMEM((2, rows, LANES), jnp.float32),
        ],
        compiler_params=params(20),
        cost_estimate=cost(4 * exp.size, exp.size * 6),
    )(parts, exps, hbm(exp), hbm(scores))


def gradient_pass(row_parts, col_parts, exp, z, zt, v, y):
    rows, width = exp.shape
    bot = z.shape[1]
    return pl.pallas_call(
        gradient_kernel,
        grid=(width // CHUNK,),
        in_specs=[
            whole(row_parts.shape),
            whole(col_parts.shape),
            pl.BlockSpec((rows, CHUNK), lambda i: (0, i)),
            whole(z.shape),
            whole(zt.shape),
            pl.BlockSpec((bot, CHUNK), lambda i: (0, i)),
            whole(y.shape),
        ],
        out_specs=[
            whole((rows, bot)),
            pl.BlockSpec((bot, CHUNK), lambda i: (0, i)),
            pl.BlockSpec((1, CHUNK), lambda i: (0, i)),
        ],
        out_shape=[
            pltpu.HBM((rows, bot), jnp.float32),
            pltpu.HBM((bot, width), jnp.float32),
            pltpu.HBM((1, width), jnp.float32),
        ],
        scratch_shapes=[
            pltpu.VMEM((width // LANES, LANES), jnp.float32),
            pltpu.VMEM((rows, LANES), jnp.float32),
            pltpu.VMEM((rows, LANES), jnp.float32),
            pltpu.VMEM((rows, CHUNK), jnp.bfloat16),
            pltpu.VMEM((rows, bot), jnp.float32),
        ],
        compiler_params=params(20),
        cost_estimate=cost(6 * z.size * width, exp.size * 4, exp.size),
    )(row_parts, col_parts, exp, z, zt, v, y)


def backward_kernel(sum_ref, y_ref, out_ref):
    y = y_ref[...]
    norm = jnp.sqrt(jnp.sum(y * y, axis=1, keepdims=True) + EPS)
    repeat_out(out_ref, (sum_ref[...] / norm).astype(jnp.bfloat16))


def norm_backward(total, y, copies):
    return pl.pallas_call(
        backward_kernel,
        out_shape=pltpu.HBM((copies,) + y.shape, jnp.bfloat16),
        compiler_params=pltpu.CompilerParams(vmem_limit_bytes=8 * MIB),
    )(total, hbm(y))


def local(hid_teacher, hid_student, proj_teacher, proj_student, proto_teacher, proto_student):
    bot = proj_teacher.shape[1]
    half = proto_teacher.shape[1] // lax.axis_size("yh")
    first = lax.axis_index("yh") * half
    columns, planes = lax.axis_size("z"), lax.axis_size(PLANE)

    gathered = lax.all_gather(proj_student, SHARD, axis=0, tiled=True)
    z_own = unit_split(hid_teacher, proj_teacher, planes)
    z_own, proto_teacher, proto_student = lax.optimization_barrier(
        (z_own, proto_teacher, proto_student)
    )
    z_t = exchange(z_own, PLANE).reshape(-1, bot)
    v_t, v_all, norm_all = unit_columns(
        lax.dynamic_slice_in_dim(proto_teacher, first, half, 1), proto_student
    )
    v_s = lax.dynamic_slice_in_dim(v_all, first, half, 1)
    last = bot // lax.axis_size(DP)
    v_last = lax.dynamic_slice_in_dim(v_all, lax.axis_index(DP) * last, last, 0).astype(jnp.float32)
    z_t, v_t, v_s, v_last = lax.optimization_barrier((z_t, v_t, v_s, v_last))
    y_s = project(hid_student, gathered)
    z_t, y_s, hid_student = lax.optimization_barrier((z_t, y_s, hid_student))
    wide_s = lax.all_gather(y_s, PLANE, axis=0, tiled=True)
    hid_group = lax.all_gather(hid_student, SHARD, axis=0, tiled=True)

    teacher_exp, mass = first_pass(z_t, v_t, columns)
    col_parts = exchange(mass, "z")
    for step in range(ITERS - 1):
        row_parts = exchange(row_pass(col_parts, teacher_exp, planes), PLANE)
        mass = column_pass(row_parts, teacher_exp, columns)
        if step == ITERS - 2:
            mass, wide_s = lax.optimization_barrier((mass, wide_s))
            z_s, z_s_t, scores, exps = student_pass(wide_s, v_s)
        col_parts = exchange(mass, "z")
    sums = exchange(last_pass(col_parts, exps, teacher_exp, scores, planes), PLANE)
    dy_part, dproto_part, dots = gradient_pass(
        sums, col_parts, teacher_exp, z_s, z_s_t, v_s, wide_s
    )

    dy_part, hid_group, sums = lax.optimization_barrier((dy_part, hid_group, sums))
    row_mass, expsum, cross = jnp.split(jnp.sum(sums, axis=0), 3, axis=0)
    row_count = y_s.shape[0] * lax.axis_size(DP + SHARD)
    loss_part = jnp.sum(jnp.log(expsum) - cross / row_mass / TAU_S) / row_count
    dproto = lax.psum_scatter(dproto_part, "z", scatter_dimension=0, tiled=True)

    parts = (dy_part * WIRE_SCALE).astype(jnp.float16).reshape((planes,) + y_s.shape)
    tangent = jnp.sum(exchange(parts, PLANE).astype(jnp.float32), axis=0) * (1.0 / WIRE_SCALE)
    dy_group = exchange(
        norm_backward(tangent, y_s, lax.axis_size(SHARD)), SHARD
    ).reshape(-1, bot)
    depth = proj_student.shape[0]
    hid_block = lax.dynamic_slice_in_dim(
        hid_group, lax.axis_index(SHARD) * depth, depth, 1
    )
    proj_term = lax.dot_general(hid_block, dy_group, ROW_DIMS, preferred_element_type=jnp.float32)
    proj_parts = exchange(proj_term.reshape(lax.axis_size(DP), -1, bot), DP)
    height = proj_parts.shape[1] + 8 * -(-(half + LANES) // (8 * bot))
    collected = pl.pallas_call(
        collect_kernel,
        out_shape=pltpu.HBM((proj_parts.shape[0], height, bot), jnp.float32),
        compiler_params=pltpu.CompilerParams(vmem_limit_bytes=8 * MIB),
    )(proj_parts, hbm(dots), loss_part.reshape(1, 1))
    swapped = swap(dproto)
    grad_proj, grad_proto, loss = pl.pallas_call(
        finish_kernel,
        out_shape=[f32(depth, bot), f32(last, 2 * half), f32(1, LANES)],
        compiler_params=pltpu.CompilerParams(vmem_limit_bytes=12 * MIB),
    )(exchange(collected, DP), hbm(swapped), hbm(v_last), hbm(norm_all))
    return (loss[0, 0], grad_proj, grad_proto)


def solution(mesh):
    fine = Mesh(mesh.devices.reshape(8, 2, 2, 4, 2), DP + SHARD)
    everything = DP + SHARD
    placed = (
        P(everything, None),
        P(everything, None),
        P(SHARD, None),
        P(SHARD, None),
        P(None, SHARD),
        P(None, SHARD),
    )
    return jax.shard_map(
        local,
        mesh=fine,
        in_specs=placed,
        out_specs=(P(), P(SHARD, None), P(DP, SHARD)),
        check_vma=False,
    )
```

```python
import functools

import jax
import jax.numpy as jnp
from jax import lax
from jax.experimental import pallas as pl
from jax.experimental.pallas import tpu as pltpu
from jax.sharding import Mesh, PartitionSpec as P

ITERS = 3
GRAD_SCALE = 256
TAU_T = 0.04
TAU_S = 0.1
EPS = 1e-06
LANES = 128
ROWS_BLOCK = 256
TALL_BLOCK = 512
GRAD_BLOCK = 1024
DEPTH_BLOCK = 1024
CHUNK = 512
MIB = 1024 * 1024
WIRE_SCALE = 4.0
ROW_DIMS = (((0,), (0,)), ((), ()))
COL_DIMS = (((1,), (1,)), ((), ()))

DP = ("z", "yh")
SHARD = ("yl", "x", "c")
PLANE = ("yh", "yl", "x", "c")


def exchange(blocks, axes):
    return lax.all_to_all(blocks, axes, 0, 0, tiled=True)


def over_cores(blocks):
    return lax.ppermute(blocks, "c", [(0, 1), (1, 0)])


def features_kernel(part_ref, got_ref, out_ref):
    y = part_ref[0 : got_ref.shape[0], :] + got_ref[...]
    unit = y / jnp.sqrt(jnp.sum(y * y, axis=1, keepdims=True) + EPS)
    repeat_out(out_ref, unit.astype(jnp.bfloat16))


def unit_split(hidden, weight, copies):
    rows, bot = hidden.shape[0], weight.shape[1]
    kept, sent, repeated = depth_halves(hidden, weight, lax.axis_size(("yl", "x")))
    share = exchange(repeated, ("yl", "x")).reshape(-1, bot)
    both = jnp.concatenate([kept, over_cores(sent)], axis=0)
    part = jnp.dot(both, share, preferred_element_type=jnp.float32)
    return pl.pallas_call(
        features_kernel,
        out_shape=pltpu.HBM((copies, rows, bot), jnp.bfloat16),
        compiler_params=pltpu.CompilerParams(vmem_limit_bytes=8 * MIB),
    )(part, over_cores(part[rows:]))


def swap(block):
    side = lax.axis_index("yh")
    rows = block.shape[0] // lax.axis_size("yh")
    kept = lax.dynamic_slice_in_dim(block, side * rows, rows, 0)
    sent = lax.dynamic_slice_in_dim(block, (1 - side) * rows, rows, 0)
    return kept, lax.ppermute(sent, "yh", [(0, 1), (1, 0)])


def lane_rows(row):
    return jnp.concatenate(
        [row[:, i * LANES : (i + 1) * LANES] for i in range(row.shape[1] // LANES)], axis=0
    )


def one_row(block):
    return jnp.concatenate([block[i : i + 1] for i in range(block.shape[0])], axis=1)


def down(block):
    return jnp.concatenate(
        [
            jnp.broadcast_to(block[i : i + 1], (LANES, LANES)).T
            for i in range(block.shape[0])
        ],
        axis=0,
    )


def lane_sums(wide):
    ones = jnp.ones((8, LANES), jnp.float32)
    row = lax.dot_general(
        ones, wide, COL_DIMS, precision=lax.Precision.HIGHEST, preferred_element_type=jnp.float32
    )
    return lane_rows(row[0:1])


def fold_lanes(wide):
    pieces = [wide[:, i * LANES : (i + 1) * LANES] for i in range(wide.shape[1] // LANES)]
    return functools.reduce(lambda a, b: a + b, pieces)


def fold_rows(tall):
    return jnp.sum(tall.reshape(-1, 8, tall.shape[1]), axis=0)


def repeat_out(out_ref, block):
    out_ref[...] = jnp.broadcast_to(block[None], out_ref.shape)


def unit_kernel(teacher_ref, student_ref, vt_ref, vs_ref, norm_ref):
    def unit(ref, out_ref):
        wide = ref[...].astype(jnp.float32)
        norm = jnp.sqrt(jnp.sum(wide * wide, axis=0, keepdims=True) + EPS)
        out_ref[...] = (wide / norm).astype(jnp.bfloat16)
        return norm

    unit(teacher_ref, vt_ref)
    norm_ref[...] = unit(student_ref, vs_ref)


def halves_kernel(core_ref, hidden_ref, weight_ref, kept_ref, sent_ref, out_ref):
    width = kept_ref.shape[1]
    repeat_out(out_ref, weight_ref[...])

    def split(even_ref, odd_ref):
        for start in range(0, width, LANES):
            cols = slice(start, start + LANES)
            even_ref[:, cols] = hidden_ref[:, 2 * start : 2 * start + LANES]
            odd_ref[:, cols] = hidden_ref[:, 2 * start + LANES : 2 * start + 2 * LANES]

    @pl.when(core_ref[0] == 0)
    def _():
        split(kept_ref, sent_ref)

    @pl.when(core_ref[0] != 0)
    def _():
        split(sent_ref, kept_ref)


def project_kernel(hidden_ref, weight_ref, out_ref):
    @pl.when(pl.program_id(0) == 0)
    def _():
        out_ref[...] = jnp.zeros_like(out_ref)

    out_ref[...] += jnp.dot(hidden_ref[...], weight_ref[...], preferred_element_type=jnp.float32)


def first_kernel(z_ref, v_ref, exp_ref, out_ref, acc):
    step = pl.program_id(0)
    width = v_ref.shape[1]

    @pl.when(step == 0)
    def _():
        acc[...] = jnp.zeros_like(acc)

    for start in range(0, width, CHUNK):
        cols = slice(start, start + CHUNK)
        product = jnp.dot(z_ref[...], v_ref[:, cols], preferred_element_type=jnp.float32)
        block = jnp.exp(product * (1.0 / TAU_T))
        exp_ref[:, cols] = block
        acc[:, cols] += fold_rows(block)

    @pl.when(step == pl.num_programs(0) - 1)
    def _():
        repeat_out(out_ref, lane_rows(jnp.sum(acc[...], axis=0, keepdims=True)))


def row_kernel(parts_ref, exp_ref, out_ref, scale, acc):
    step = pl.program_id(0)

    @pl.when(step == 0)
    def _():
        scale[...] = one_row(1.0 / jnp.sum(parts_ref[...], axis=0))

    rows, width = exp_ref.shape
    block = exp_ref[:, 0:LANES] * scale[:, 0:LANES]
    for start in range(LANES, width, LANES):
        cols = slice(start, start + LANES)
        block += exp_ref[:, cols] * scale[:, cols]
    acc[pl.ds(pl.multiple_of(step * rows, rows), rows), :] = block

    @pl.when(step == pl.num_programs(0) - 1)
    def _():
        repeat_out(out_ref, lane_sums(acc[...]))


def column_kernel(parts_ref, exp_ref, out_ref, scale, acc):
    step = pl.program_id(0)

    @pl.when(step == 0)
    def _():
        scale[...] = down(1.0 / jnp.sum(parts_ref[...], axis=0))
        acc[...] = jnp.zeros_like(acc)

    rows, width = exp_ref.shape
    factor = scale[pl.ds(pl.multiple_of(step * rows, rows), rows), :]
    for start in range(0, width, LANES):
        cols = slice(start, start + LANES)
        acc[:, cols] += fold_rows(exp_ref[:, cols] * factor)

    @pl.when(step == pl.num_programs(0) - 1)
    def _():
        repeat_out(out_ref, lane_rows(jnp.sum(acc[...], axis=0, keepdims=True)))


def student_kernel(parts_ref, exp_ref, y_ref, v_ref, out_ref, z_ref, zt_ref, scale, acc):
    step = pl.program_id(0)

    @pl.when(step == 0)
    def _():
        scale[...] = one_row(1.0 / jnp.sum(parts_ref[...], axis=0))

    rows, width = exp_ref.shape
    here = pl.ds(pl.multiple_of(step * rows, rows), rows)
    y = y_ref[...]
    z = y / jnp.sqrt(jnp.sum(y * y, axis=1, keepdims=True) + EPS)
    z_ref[...] = z.astype(jnp.bfloat16)
    zt_ref[...] = z.T.astype(jnp.bfloat16)
    mass = jnp.zeros((rows, LANES), jnp.float32)
    exps = jnp.zeros((rows, LANES), jnp.float32)
    cross = jnp.zeros((rows, LANES), jnp.float32)
    for start in range(0, width, CHUNK):
        cols = slice(start, start + CHUNK)
        scores = jnp.dot(z_ref[...], v_ref[:, cols], preferred_element_type=jnp.float32)
        weighted = exp_ref[:, cols] * scale[:, cols]
        mass += fold_lanes(weighted)
        exps += fold_lanes(jnp.exp(scores * (1.0 / TAU_S)))
        cross += fold_lanes(weighted * scores)
    acc[0, here, :] = mass
    acc[1, here, :] = exps
    acc[2, here, :] = cross

    @pl.when(step == pl.num_programs(0) - 1)
    def _():
        sums = [lane_sums(acc[i]) for i in range(3)]
        repeat_out(out_ref, jnp.concatenate(sums, axis=0))


def gradient_kernel(
    row_parts_ref, col_parts_ref, exp_ref, z_ref, zt_ref, v_ref, y_ref, dy_ref, dp_ref, dots_ref,
    scale, teacher, student, grad, dz,
):
    step = pl.program_id(0)
    rows, width = exp_ref.shape
    tall = rows // LANES

    @pl.when(step == 0)
    def _():
        sums = jnp.sum(row_parts_ref[...], axis=0)
        factor = GRAD_SCALE / TAU_S
        teacher[...] = down(factor / sums[0:tall])
        student[...] = down(factor / sums[tall : 2 * tall])
        scale[...] = 1.0 / jnp.sum(col_parts_ref[...], axis=0)
        dz[...] = jnp.zeros_like(dz)

    groups = width // LANES
    col = one_row(scale[pl.ds(pl.multiple_of(step * groups, groups), groups), :])
    for start in range(0, rows, GRAD_BLOCK):
        here = slice(start, start + GRAD_BLOCK)
        scores = jnp.dot(z_ref[here, :], v_ref[...], preferred_element_type=jnp.float32)
        prob = jnp.exp(scores * (1.0 / TAU_S))
        for piece in range(0, width, LANES):
            cols = slice(piece, piece + LANES)
            target = exp_ref[here, cols] * col[:, cols] * teacher[here, :]
            grad[here, cols] = (prob[:, cols] * student[here, :] - target).astype(jnp.bfloat16)
        dz[here, :] += lax.dot_general(
            grad[here, :], v_ref[...], COL_DIMS, preferred_element_type=jnp.float32
        )
    dproto = jnp.dot(zt_ref[...], grad[...], preferred_element_type=jnp.float32)
    dp_ref[...] = dproto
    dots_ref[...] = jnp.sum(v_ref[...].astype(jnp.float32) * dproto, axis=0, keepdims=True)

    @pl.when(step == pl.num_programs(0) - 1)
    def _():
        for start in range(0, rows, ROWS_BLOCK):
            here = slice(start, start + ROWS_BLOCK)
            y = y_ref[here, :]
            part = dz[here, :]
            square = jnp.sum(y * y, axis=1, keepdims=True) + EPS
            inner = jnp.sum(y * part, axis=1, keepdims=True)
            dy_ref[here, :] = part - y * (inner / square)


def collect_kernel(proj_ref, dots_ref, loss_ref, out_ref):
    own, bot = proj_ref.shape[1:]
    proj = jnp.sum(proj_ref[...], axis=0)
    dots = dots_ref[...]
    width = dots.shape[1]
    rows = -(-(width + LANES) // bot)
    loss = jnp.broadcast_to(loss_ref[...], (1, rows * bot - width))
    row = jnp.concatenate([dots, loss], axis=1)
    pieces = [row[:, i * bot : (i + 1) * bot] for i in range(rows)]
    pieces.append(jnp.zeros((out_ref.shape[1] - own - rows, bot), jnp.float32))
    repeat_out(out_ref, jnp.concatenate([proj] + pieces, axis=0))


def finish_kernel(
    side_ref, parts_ref, kept_ref, got_ref, v_ref, norm_ref, proj_ref, grad_ref, loss_ref
):
    copies, height, bot = parts_ref.shape
    own = proj_ref.shape[0] // copies
    width = kept_ref.shape[1]
    rows = -(-(width + LANES) // bot)
    for i in range(copies):
        proj_ref[i * own : (i + 1) * own, :] = parts_ref[i, 0:own, :]
    lines = []
    for side in range(2):
        block = parts_ref[side, own:height, :]
        for i in range(2 + side, copies, 2):
            block = block + parts_ref[i, own:height, :]
        lines.append(jnp.concatenate([block[i : i + 1] for i in range(rows)], axis=1))
    loss_ref[...] = lines[0][:, width : width + LANES]

    def write(halves):
        for side in range(2):
            cols = slice(side * width, (side + 1) * width)
            dots = lines[side][:, 0:width]
            grad_ref[:, cols] = (halves[side][...] - v_ref[:, cols] * dots) / norm_ref[:, cols]

    @pl.when(side_ref[0] == 0)
    def _():
        write((kept_ref, got_ref))

    @pl.when(side_ref[0] != 0)
    def _():
        write((got_ref, kept_ref))


def params(mib):
    return pltpu.CompilerParams(
        dimension_semantics=("arbitrary",), vmem_limit_bytes=mib * MIB
    )


def cost(flops, size, exps=0):
    return pl.CostEstimate(flops=flops, bytes_accessed=size, transcendentals=exps)


def whole(shape):
    return pl.BlockSpec(shape, lambda i: (0,) * len(shape))


def f32(*shape):
    return jax.ShapeDtypeStruct(shape, jnp.float32)


def hbm(array):
    return pltpu.with_memory_space_constraint(array, pltpu.HBM)


def unit_columns(teacher, student):
    bot, width = teacher.shape
    step = width // CHUNK
    wide = student.shape[1] // step
    return pl.pallas_call(
        unit_kernel,
        grid=(step,),
        in_specs=[
            pl.BlockSpec((bot, CHUNK), lambda i: (0, i)),
            pl.BlockSpec((bot, wide), lambda i: (0, i)),
        ],
        out_specs=[
            pl.BlockSpec((bot, CHUNK), lambda i: (0, i)),
            pl.BlockSpec((bot, wide), lambda i: (0, i)),
            pl.BlockSpec((1, wide), lambda i: (0, i)),
        ],
        out_shape=[
            jax.ShapeDtypeStruct(teacher.shape, jnp.bfloat16),
            jax.ShapeDtypeStruct(student.shape, jnp.bfloat16),
            f32(1, student.shape[1]),
        ],
        compiler_params=params(20),
        cost_estimate=cost(4 * (teacher.size + student.size), 4 * (teacher.size + student.size)),
    )(teacher, student)


def depth_halves(hidden, weight, copies):
    half = jax.ShapeDtypeStruct((hidden.shape[0], hidden.shape[1] // 2), hidden.dtype)
    return pl.pallas_call(
        halves_kernel,
        in_specs=[pl.BlockSpec(memory_space=pltpu.SMEM)]
        + [pl.BlockSpec(memory_space=pltpu.VMEM)] * 2,
        out_shape=[half, half, pltpu.HBM((copies,) + weight.shape, weight.dtype)],
        compiler_params=pltpu.CompilerParams(vmem_limit_bytes=8 * MIB),
        cost_estimate=cost(0, 4 * hidden.size + 2 * copies * weight.size),
    )(lax.axis_index("c").reshape(1), hbm(hidden), hbm(weight))


def project(hidden, weight):
    rows, depth = hidden.shape
    bot = weight.shape[1]
    return pl.pallas_call(
        project_kernel,
        grid=(depth // DEPTH_BLOCK,),
        in_specs=[
            pl.BlockSpec((rows, DEPTH_BLOCK), lambda i: (0, i)),
            pl.BlockSpec((DEPTH_BLOCK, bot), lambda i: (i, 0)),
        ],
        out_specs=whole((rows, bot)),
        out_shape=f32(rows, bot),
        compiler_params=params(8),
        cost_estimate=cost(2 * rows * weight.size, 2 * (hidden.size + weight.size)),
    )(hidden, hbm(weight))


def first_pass(z, v, copies):
    rows, bot = z.shape
    width = v.shape[1]
    out = (copies, width // LANES, LANES)
    return pl.pallas_call(
        first_kernel,
        grid=(rows // TALL_BLOCK,),
        in_specs=[pl.BlockSpec((TALL_BLOCK, bot), lambda i: (i, 0)), whole(v.shape)],
        out_specs=[pl.BlockSpec((TALL_BLOCK, width), lambda i: (i, 0)), whole(out)],
        out_shape=[f32(rows, width), f32(*out)],
        scratch_shapes=[pltpu.VMEM((8, width), jnp.float32)],
        compiler_params=params(20),
        cost_estimate=cost(2 * z.size * width, rows * width * 4, rows * width),
    )(z, hbm(v))


def row_pass(parts, exp, copies):
    rows, width = exp.shape
    out = (copies, rows // LANES, LANES)
    return pl.pallas_call(
        row_kernel,
        grid=(rows // ROWS_BLOCK,),
        in_specs=[whole(parts.shape), pl.BlockSpec((ROWS_BLOCK, width), lambda i: (i, 0))],
        out_specs=whole(out),
        out_shape=f32(*out),
        scratch_shapes=[pltpu.VMEM((1, width), jnp.float32), pltpu.VMEM((rows, LANES), jnp.float32)],
        compiler_params=params(20),
        cost_estimate=cost(2 * exp.size, exp.size * 4),
    )(parts, exp)


def column_pass(parts, exp, copies):
    rows, width = exp.shape
    out = (copies, width // LANES, LANES)
    return pl.pallas_call(
        column_kernel,
        grid=(rows // ROWS_BLOCK,),
        in_specs=[whole(parts.shape), pl.BlockSpec((ROWS_BLOCK, width), lambda i: (i, 0))],
        out_specs=whole(out),
        out_shape=f32(*out),
        scratch_shapes=[pltpu.VMEM((rows, LANES), jnp.float32), pltpu.VMEM((8, width), jnp.float32)],
        compiler_params=params(20),
        cost_estimate=cost(2 * exp.size, exp.size * 4),
    )(parts, exp)


def student_pass(parts, exp, y, v, copies):
    rows, width = exp.shape
    bot = y.shape[1]
    out = (copies, 3 * rows // LANES, LANES)
    return pl.pallas_call(
        student_kernel,
        grid=(rows // ROWS_BLOCK,),
        in_specs=[
            whole(parts.shape),
            pl.BlockSpec((ROWS_BLOCK, width), lambda i: (i, 0)),
            pl.BlockSpec((ROWS_BLOCK, bot), lambda i: (i, 0)),
            whole(v.shape),
        ],
        out_specs=[
            whole(out),
            pl.BlockSpec((ROWS_BLOCK, bot), lambda i: (i, 0)),
            pl.BlockSpec((bot, ROWS_BLOCK), lambda i: (0, i)),
        ],
        out_shape=[
            f32(*out),
            jax.ShapeDtypeStruct((rows, bot), jnp.bfloat16),
            jax.ShapeDtypeStruct((bot, rows), jnp.bfloat16),
        ],
        scratch_shapes=[
            pltpu.VMEM((1, width), jnp.float32),
            pltpu.VMEM((3, rows, LANES), jnp.float32),
        ],
        compiler_params=params(20),
        cost_estimate=cost(2 * y.size * width, exp.size * 4, exp.size),
    )(parts, hbm(exp), hbm(y), hbm(v))


def gradient_pass(row_parts, col_parts, exp, z, zt, v, y):
    rows, width = exp.shape
    bot = z.shape[1]
    return pl.pallas_call(
        gradient_kernel,
        grid=(width // CHUNK,),
        in_specs=[
            whole(row_parts.shape),
            whole(col_parts.shape),
            pl.BlockSpec((rows, CHUNK), lambda i: (0, i)),
            whole(z.shape),
            whole(zt.shape),
            pl.BlockSpec((bot, CHUNK), lambda i: (0, i)),
            whole(y.shape),
        ],
        out_specs=[
            whole((rows, bot)),
            pl.BlockSpec((bot, CHUNK), lambda i: (0, i)),
            pl.BlockSpec((1, CHUNK), lambda i: (0, i)),
        ],
        out_shape=[
            pltpu.HBM((rows, bot), jnp.float32),
            pltpu.HBM((bot, width), jnp.float32),
            pltpu.HBM((1, width), jnp.float32),
        ],
        scratch_shapes=[
            pltpu.VMEM((width // LANES, LANES), jnp.float32),
            pltpu.VMEM((rows, LANES), jnp.float32),
            pltpu.VMEM((rows, LANES), jnp.float32),
            pltpu.VMEM((rows, CHUNK), jnp.bfloat16),
            pltpu.VMEM((rows, bot), jnp.float32),
        ],
        compiler_params=params(28),
        cost_estimate=cost(6 * z.size * width, exp.size * 4, exp.size),
    )(row_parts, col_parts, exp, z, zt, v, y)


def backward_kernel(sum_ref, y_ref, out_ref):
    y = y_ref[...]
    norm = jnp.sqrt(jnp.sum(y * y, axis=1, keepdims=True) + EPS)
    repeat_out(out_ref, (sum_ref[...] / norm).astype(jnp.bfloat16))


def norm_backward(total, y, copies):
    return pl.pallas_call(
        backward_kernel,
        out_shape=pltpu.HBM((copies,) + y.shape, jnp.bfloat16),
        compiler_params=pltpu.CompilerParams(vmem_limit_bytes=8 * MIB),
    )(total, hbm(y))


def local(hid_teacher, hid_student, proj_teacher, proj_student, proto_teacher, proto_student):
    bot = proj_teacher.shape[1]
    half = proto_teacher.shape[1] // lax.axis_size("yh")
    first = lax.axis_index("yh") * half
    columns, planes = lax.axis_size("z"), lax.axis_size(PLANE)

    gathered = lax.all_gather(proj_student, SHARD, axis=0, tiled=True)
    z_own = unit_split(hid_teacher, proj_teacher, planes)
    z_own, proto_teacher, proto_student = lax.optimization_barrier(
        (z_own, proto_teacher, proto_student)
    )
    z_t = exchange(z_own, PLANE).reshape(-1, bot)
    v_t, v_all, norm_all = unit_columns(
        lax.dynamic_slice_in_dim(proto_teacher, first, half, 1), proto_student
    )
    v_s = lax.dynamic_slice_in_dim(v_all, first, half, 1)
    last = bot // lax.axis_size(DP)
    v_last = lax.dynamic_slice_in_dim(v_all, lax.axis_index(DP) * last, last, 0).astype(jnp.float32)
    z_t, v_t, v_s, v_last = lax.optimization_barrier((z_t, v_t, v_s, v_last))
    y_s = project(hid_student, gathered)
    z_t, y_s, hid_student = lax.optimization_barrier((z_t, y_s, hid_student))
    wide_s = lax.all_gather(y_s, PLANE, axis=0, tiled=True)
    hid_group = lax.all_gather(hid_student, SHARD, axis=0, tiled=True)

    teacher_exp, mass = first_pass(z_t, v_t, columns)
    col_parts = exchange(mass, "z")
    for step in range(ITERS - 1):
        row_parts = exchange(row_pass(col_parts, teacher_exp, planes), PLANE)
        mass = column_pass(row_parts, teacher_exp, columns)
        if step == ITERS - 2:
            mass, wide_s = lax.optimization_barrier((mass, wide_s))
        col_parts = exchange(mass, "z")
    sums, z_s, z_s_t = student_pass(col_parts, teacher_exp, wide_s, v_s, planes)
    sums = exchange(sums, PLANE)
    dy_part, dproto_part, dots = gradient_pass(
        sums, col_parts, teacher_exp, z_s, z_s_t, v_s, wide_s
    )

    dy_part, hid_group, sums = lax.optimization_barrier((dy_part, hid_group, sums))
    row_mass, expsum, cross = jnp.split(jnp.sum(sums, axis=0), 3, axis=0)
    row_count = y_s.shape[0] * lax.axis_size(DP + SHARD)
    loss_part = jnp.sum(jnp.log(expsum) - cross / row_mass / TAU_S) / row_count
    dproto = lax.psum_scatter(dproto_part, "z", scatter_dimension=0, tiled=True)
    kept, got = swap(dproto)

    parts = (dy_part * WIRE_SCALE).astype(jnp.float16).reshape((planes,) + y_s.shape)
    tangent = jnp.sum(exchange(parts, PLANE).astype(jnp.float32), axis=0) * (1.0 / WIRE_SCALE)
    dy_group = exchange(
        norm_backward(tangent, y_s, lax.axis_size(SHARD)), SHARD
    ).reshape(-1, bot)
    depth = proj_student.shape[0]
    hid_block = lax.dynamic_slice_in_dim(
        hid_group, lax.axis_index(SHARD) * depth, depth, 1
    )
    proj_term = lax.dot_general(hid_block, dy_group, ROW_DIMS, preferred_element_type=jnp.float32)
    proj_parts = exchange(proj_term.reshape(lax.axis_size(DP), -1, bot), DP)
    height = proj_parts.shape[1] + 8 * -(-(half + LANES) // (8 * bot))
    collected = pl.pallas_call(
        collect_kernel,
        out_shape=pltpu.HBM((proj_parts.shape[0], height, bot), jnp.float32),
        compiler_params=pltpu.CompilerParams(vmem_limit_bytes=8 * MIB),
    )(proj_parts, hbm(dots), loss_part.reshape(1, 1))
    grad_proj, grad_proto, loss = pl.pallas_call(
        finish_kernel,
        in_specs=[pl.BlockSpec(memory_space=pltpu.SMEM)]
        + [pl.BlockSpec(memory_space=pltpu.VMEM)] * 5,
        out_shape=[f32(depth, bot), f32(last, 2 * half), f32(1, LANES)],
        compiler_params=pltpu.CompilerParams(vmem_limit_bytes=12 * MIB),
    )(
        lax.axis_index("yh").reshape(1),
        exchange(collected, DP),
        hbm(kept),
        hbm(got),
        hbm(v_last),
        hbm(norm_all),
    )
    return (loss[0, 0], grad_proj, grad_proto)


def solution(mesh):
    fine = Mesh(mesh.devices.reshape(8, 2, 2, 4, 2), DP + SHARD)
    everything = DP + SHARD
    placed = (
        P(everything, None),
        P(everything, None),
        P(SHARD, None),
        P(SHARD, None),
        P(None, SHARD),
        P(None, SHARD),
    )
    return jax.shard_map(
        local,
        mesh=fine,
        in_specs=placed,
        out_specs=(P(), P(SHARD, None), P(DP, SHARD)),
        check_vma=False,
    )
```

```python
import functools

import jax
import jax.numpy as jnp
from jax import lax
from jax.experimental import pallas as pl
from jax.experimental.pallas import tpu as pltpu
from jax.sharding import Mesh, PartitionSpec as P

ITERS = 3
GRAD_SCALE = 256
TAU_T = 0.04
TAU_S = 0.1
EPS = 1e-06
LANES = 128
ROWS_BLOCK = 256
TALL_BLOCK = 512
GRAD_BLOCK = 1024
DEPTH_BLOCK = 1024
CHUNK = 512
MIB = 1024 * 1024
WIRE_SCALE = 4.0
ROW_DIMS = (((0,), (0,)), ((), ()))
COL_DIMS = (((1,), (1,)), ((), ()))

DP = ("z", "yh")
SHARD = ("yl", "x", "c")
PLANE = ("yh", "yl", "x", "c")


def exchange(blocks, axes):
    return lax.all_to_all(blocks, axes, 0, 0, tiled=True)


def over_cores(blocks):
    return lax.ppermute(blocks, "c", [(0, 1), (1, 0)])


def features_kernel(part_ref, got_ref, out_ref):
    y = part_ref[0 : got_ref.shape[0], :] + got_ref[...]
    unit = y / jnp.sqrt(jnp.sum(y * y, axis=1, keepdims=True) + EPS)
    repeat_out(out_ref, unit.astype(jnp.bfloat16))


def unit_split(hidden, weight, copies):
    rows, bot = hidden.shape[0], weight.shape[1]
    kept, sent, repeated = depth_halves(hidden, weight, lax.axis_size(("yl", "x")))
    share = exchange(repeated, ("yl", "x")).reshape(-1, bot)
    both = jnp.concatenate([kept, over_cores(sent)], axis=0)
    part = jnp.dot(both, share, preferred_element_type=jnp.float32)
    return pl.pallas_call(
        features_kernel,
        out_shape=pltpu.HBM((copies, rows, bot), jnp.bfloat16),
        compiler_params=pltpu.CompilerParams(vmem_limit_bytes=8 * MIB),
    )(part, over_cores(part[rows:]))


def swap(block):
    side = lax.axis_index("yh")
    rows = block.shape[0] // lax.axis_size("yh")
    kept = lax.dynamic_slice_in_dim(block, side * rows, rows, 0)
    sent = lax.dynamic_slice_in_dim(block, (1 - side) * rows, rows, 0)
    return kept, lax.ppermute(sent, "yh", [(0, 1), (1, 0)])


def lane_rows(row):
    return jnp.concatenate(
        [row[:, i * LANES : (i + 1) * LANES] for i in range(row.shape[1] // LANES)], axis=0
    )


def one_row(block):
    return jnp.concatenate([block[i : i + 1] for i in range(block.shape[0])], axis=1)


def down(block):
    return jnp.concatenate(
        [
            jnp.broadcast_to(block[i : i + 1], (LANES, LANES)).T
            for i in range(block.shape[0])
        ],
        axis=0,
    )


def lane_sums(wide):
    ones = jnp.ones((8, LANES), jnp.float32)
    row = lax.dot_general(
        ones, wide, COL_DIMS, precision=lax.Precision.HIGHEST, preferred_element_type=jnp.float32
    )
    return lane_rows(row[0:1])


def fold_lanes(wide):
    pieces = [wide[:, i * LANES : (i + 1) * LANES] for i in range(wide.shape[1] // LANES)]
    return functools.reduce(lambda a, b: a + b, pieces)


def fold_rows(tall):
    return jnp.sum(tall.reshape(-1, 8, tall.shape[1]), axis=0)


def repeat_out(out_ref, block):
    out_ref[...] = jnp.broadcast_to(block[None], out_ref.shape)


def unit_kernel(teacher_ref, student_ref, vt_ref, vs_ref, norm_ref):
    def unit(ref, out_ref):
        wide = ref[...].astype(jnp.float32)
        norm = jnp.sqrt(jnp.sum(wide * wide, axis=0, keepdims=True) + EPS)
        out_ref[...] = (wide / norm).astype(jnp.bfloat16)
        return norm

    unit(teacher_ref, vt_ref)
    norm_ref[...] = unit(student_ref, vs_ref)


def halves_kernel(core_ref, hidden_ref, weight_ref, kept_ref, sent_ref, out_ref):
    width = kept_ref.shape[1]
    repeat_out(out_ref, weight_ref[...])

    def split(even_ref, odd_ref):
        for start in range(0, width, LANES):
            cols = slice(start, start + LANES)
            even_ref[:, cols] = hidden_ref[:, 2 * start : 2 * start + LANES]
            odd_ref[:, cols] = hidden_ref[:, 2 * start + LANES : 2 * start + 2 * LANES]

    @pl.when(core_ref[0] == 0)
    def _():
        split(kept_ref, sent_ref)

    @pl.when(core_ref[0] != 0)
    def _():
        split(sent_ref, kept_ref)


def project_kernel(hidden_ref, weight_ref, out_ref):
    @pl.when(pl.program_id(0) == 0)
    def _():
        out_ref[...] = jnp.zeros_like(out_ref)

    out_ref[...] += jnp.dot(hidden_ref[...], weight_ref[...], preferred_element_type=jnp.float32)


def first_kernel(z_ref, v_ref, exp_ref, out_ref, acc):
    step = pl.program_id(0)
    width = v_ref.shape[1]

    @pl.when(step == 0)
    def _():
        acc[...] = jnp.zeros_like(acc)

    for start in range(0, width, CHUNK):
        cols = slice(start, start + CHUNK)
        product = jnp.dot(z_ref[...], v_ref[:, cols], preferred_element_type=jnp.float32)
        block = jnp.exp(product * (1.0 / TAU_T))
        exp_ref[:, cols] = block
        acc[:, cols] += fold_rows(block)

    @pl.when(step == pl.num_programs(0) - 1)
    def _():
        repeat_out(out_ref, lane_rows(jnp.sum(acc[...], axis=0, keepdims=True)))


def row_kernel(parts_ref, exp_ref, out_ref, scale, acc):
    step = pl.program_id(0)

    @pl.when(step == 0)
    def _():
        scale[...] = one_row(1.0 / jnp.sum(parts_ref[...], axis=0))

    rows, width = exp_ref.shape
    block = exp_ref[:, 0:LANES] * scale[:, 0:LANES]
    for start in range(LANES, width, LANES):
        cols = slice(start, start + LANES)
        block += exp_ref[:, cols] * scale[:, cols]
    acc[pl.ds(pl.multiple_of(step * rows, rows), rows), :] = block

    @pl.when(step == pl.num_programs(0) - 1)
    def _():
        repeat_out(out_ref, lane_sums(acc[...]))


def column_kernel(parts_ref, exp_ref, out_ref, scale, acc):
    step = pl.program_id(0)

    @pl.when(step == 0)
    def _():
        scale[...] = down(1.0 / jnp.sum(parts_ref[...], axis=0))
        acc[...] = jnp.zeros_like(acc)

    rows, width = exp_ref.shape
    factor = scale[pl.ds(pl.multiple_of(step * rows, rows), rows), :]
    for start in range(0, width, LANES):
        cols = slice(start, start + LANES)
        acc[:, cols] += fold_rows(exp_ref[:, cols] * factor)

    @pl.when(step == pl.num_programs(0) - 1)
    def _():
        repeat_out(out_ref, lane_rows(jnp.sum(acc[...], axis=0, keepdims=True)))


def student_kernel(parts_ref, exp_ref, y_ref, v_ref, out_ref, z_ref, zt_ref, scale, acc):
    step = pl.program_id(0)

    @pl.when(step == 0)
    def _():
        scale[...] = one_row(1.0 / jnp.sum(parts_ref[...], axis=0))

    rows, width = exp_ref.shape
    here = pl.ds(pl.multiple_of(step * rows, rows), rows)
    y = y_ref[...]
    z = y / jnp.sqrt(jnp.sum(y * y, axis=1, keepdims=True) + EPS)
    z_ref[...] = z.astype(jnp.bfloat16)
    zt_ref[...] = z.T.astype(jnp.bfloat16)
    mass = jnp.zeros((rows, LANES), jnp.float32)
    exps = jnp.zeros((rows, LANES), jnp.float32)
    cross = jnp.zeros((rows, LANES), jnp.float32)
    for start in range(0, width, CHUNK):
        cols = slice(start, start + CHUNK)
        scores = jnp.dot(z_ref[...], v_ref[:, cols], preferred_element_type=jnp.float32)
        weighted = exp_ref[:, cols] * scale[:, cols]
        mass += fold_lanes(weighted)
        exps += fold_lanes(jnp.exp(scores * (1.0 / TAU_S)))
        cross += fold_lanes(weighted * scores)
    acc[0, here, :] = mass
    acc[1, here, :] = exps
    acc[2, here, :] = cross

    @pl.when(step == pl.num_programs(0) - 1)
    def _():
        sums = [lane_sums(acc[i]) for i in range(3)]
        repeat_out(out_ref, jnp.concatenate(sums, axis=0))


def gradient_kernel(
    row_parts_ref, col_parts_ref, exp_ref, z_ref, zt_ref, v_ref, y_ref, dy_ref, dp_ref, dots_ref,
    scale, teacher, student, grad, dz,
):
    step = pl.program_id(0)
    rows, width = exp_ref.shape
    tall = rows // LANES

    @pl.when(step == 0)
    def _():
        sums = jnp.sum(row_parts_ref[...], axis=0)
        factor = GRAD_SCALE / TAU_S
        teacher[...] = down(factor / sums[0:tall])
        student[...] = down(factor / sums[tall : 2 * tall])
        scale[...] = 1.0 / jnp.sum(col_parts_ref[...], axis=0)
        dz[...] = jnp.zeros_like(dz)

    groups = width // LANES
    col = one_row(scale[pl.ds(pl.multiple_of(step * groups, groups), groups), :])
    for start in range(0, rows, GRAD_BLOCK):
        here = slice(start, start + GRAD_BLOCK)
        scores = jnp.dot(z_ref[here, :], v_ref[...], preferred_element_type=jnp.float32)
        prob = jnp.exp(scores * (1.0 / TAU_S))
        for piece in range(0, width, LANES):
            cols = slice(piece, piece + LANES)
            target = exp_ref[here, cols] * col[:, cols] * teacher[here, :]
            grad[here, cols] = (prob[:, cols] * student[here, :] - target).astype(jnp.bfloat16)
        dz[here, :] += lax.dot_general(
            grad[here, :], v_ref[...], COL_DIMS, preferred_element_type=jnp.float32
        )
    dproto = jnp.dot(zt_ref[...], grad[...], preferred_element_type=jnp.float32)
    dp_ref[...] = dproto
    dots_ref[...] = jnp.sum(v_ref[...].astype(jnp.float32) * dproto, axis=0, keepdims=True)

    @pl.when(step == pl.num_programs(0) - 1)
    def _():
        for start in range(0, rows, ROWS_BLOCK):
            here = slice(start, start + ROWS_BLOCK)
            y = y_ref[here, :]
            part = dz[here, :]
            square = jnp.sum(y * y, axis=1, keepdims=True) + EPS
            inner = jnp.sum(y * part, axis=1, keepdims=True)
            dy_ref[here, :] = part - y * (inner / square)


def rows_kernel(hidden_ref, dy_ref, dots_ref, out_ref):
    copies, height = out_ref.shape[:2]
    product = lax.dot_general(
        hidden_ref[...], dy_ref[...], ROW_DIMS, preferred_element_type=jnp.float32
    )
    own, bot = product.shape[0] // copies, product.shape[1]
    for i in range(copies):
        for piece in range(0, bot, LANES):
            row = piece // LANES * own
            out_ref[i, row : row + own, :] = product[
                i * own : (i + 1) * own, piece : piece + LANES
            ]
        dots = dots_ref[:, i * LANES : (i + 1) * LANES]
        tail = height - own * bot // LANES
        out_ref[i, height - tail : height, :] = jnp.broadcast_to(dots, (tail, LANES))


def collect_kernel(parts_ref, loss_ref, out_ref):
    copies, height = parts_ref.shape[:2]
    sides = []
    for side in range(2):
        block = parts_ref[side]
        for i in range(2 + side, copies, 2):
            block = block + parts_ref[i]
        sides.append(block)
    head = height - 8
    loss = jnp.broadcast_to(loss_ref[...], (6, LANES))
    tail = [sides[0][head : head + 1], sides[1][head : head + 1], loss]
    repeat_out(
        out_ref, jnp.concatenate([sides[0][0:head] + sides[1][0:head]] + tail, axis=0)
    )


def finish_kernel(
    side_ref, parts_ref, kept_ref, got_ref, v_ref, norm_ref, proj_ref, grad_ref, loss_ref
):
    copies, height = parts_ref.shape[:2]
    rows, bot = proj_ref.shape
    own, width, head = rows // copies, kept_ref.shape[1], height - 8
    for i in range(copies):
        for piece in range(0, bot, LANES):
            row = piece // LANES * own
            proj_ref[i * own : (i + 1) * own, piece : piece + LANES] = parts_ref[
                i, row : row + own, :
            ]
    lines = [
        jnp.concatenate(
            [parts_ref[i, head + side : head + side + 1, :] for i in range(copies)], axis=1
        )
        for side in range(2)
    ]
    loss = parts_ref[0, head + 2 : head + 3, :]
    for i in range(2, copies, 2):
        loss = loss + parts_ref[i, head + 2 : head + 3, :]
    loss_ref[...] = loss

    def write(halves):
        for side in range(2):
            cols = slice(side * width, (side + 1) * width)
            dots = lines[side][:, 0:width]
            grad_ref[:, cols] = (halves[side][...] - v_ref[:, cols] * dots) / norm_ref[:, cols]

    @pl.when(side_ref[0] == 0)
    def _():
        write((kept_ref, got_ref))

    @pl.when(side_ref[0] != 0)
    def _():
        write((got_ref, kept_ref))


def params(mib):
    return pltpu.CompilerParams(
        dimension_semantics=("arbitrary",), vmem_limit_bytes=mib * MIB
    )


def cost(flops, size, exps=0):
    return pl.CostEstimate(flops=flops, bytes_accessed=size, transcendentals=exps)


def whole(shape):
    return pl.BlockSpec(shape, lambda i: (0,) * len(shape))


def f32(*shape):
    return jax.ShapeDtypeStruct(shape, jnp.float32)


def hbm(array):
    return pltpu.with_memory_space_constraint(array, pltpu.HBM)


def unit_columns(teacher, student):
    bot, width = teacher.shape
    step = width // CHUNK
    wide = student.shape[1] // step
    return pl.pallas_call(
        unit_kernel,
        grid=(step,),
        in_specs=[
            pl.BlockSpec((bot, CHUNK), lambda i: (0, i)),
            pl.BlockSpec((bot, wide), lambda i: (0, i)),
        ],
        out_specs=[
            pl.BlockSpec((bot, CHUNK), lambda i: (0, i)),
            pl.BlockSpec((bot, wide), lambda i: (0, i)),
            pl.BlockSpec((1, wide), lambda i: (0, i)),
        ],
        out_shape=[
            jax.ShapeDtypeStruct(teacher.shape, jnp.bfloat16),
            jax.ShapeDtypeStruct(student.shape, jnp.bfloat16),
            f32(1, student.shape[1]),
        ],
        compiler_params=params(20),
        cost_estimate=cost(4 * (teacher.size + student.size), 4 * (teacher.size + student.size)),
    )(teacher, student)


def depth_halves(hidden, weight, copies):
    half = jax.ShapeDtypeStruct((hidden.shape[0], hidden.shape[1] // 2), hidden.dtype)
    return pl.pallas_call(
        halves_kernel,
        in_specs=[pl.BlockSpec(memory_space=pltpu.SMEM)]
        + [pl.BlockSpec(memory_space=pltpu.VMEM)] * 2,
        out_shape=[half, half, pltpu.HBM((copies,) + weight.shape, weight.dtype)],
        compiler_params=pltpu.CompilerParams(vmem_limit_bytes=8 * MIB),
        cost_estimate=cost(0, 4 * hidden.size + 2 * copies * weight.size),
    )(lax.axis_index("c").reshape(1), hbm(hidden), hbm(weight))


def project(hidden, weight):
    rows, depth = hidden.shape
    bot = weight.shape[1]
    return pl.pallas_call(
        project_kernel,
        grid=(depth // DEPTH_BLOCK,),
        in_specs=[
            pl.BlockSpec((rows, DEPTH_BLOCK), lambda i: (0, i)),
            pl.BlockSpec((DEPTH_BLOCK, bot), lambda i: (i, 0)),
        ],
        out_specs=whole((rows, bot)),
        out_shape=f32(rows, bot),
        compiler_params=params(8),
        cost_estimate=cost(2 * rows * weight.size, 2 * (hidden.size + weight.size)),
    )(hidden, hbm(weight))


def first_pass(z, v, copies):
    rows, bot = z.shape
    width = v.shape[1]
    out = (copies, width // LANES, LANES)
    return pl.pallas_call(
        first_kernel,
        grid=(rows // TALL_BLOCK,),
        in_specs=[pl.BlockSpec((TALL_BLOCK, bot), lambda i: (i, 0)), whole(v.shape)],
        out_specs=[pl.BlockSpec((TALL_BLOCK, width), lambda i: (i, 0)), whole(out)],
        out_shape=[f32(rows, width), f32(*out)],
        scratch_shapes=[pltpu.VMEM((8, width), jnp.float32)],
        compiler_params=params(20),
        cost_estimate=cost(2 * z.size * width, rows * width * 4, rows * width),
    )(z, hbm(v))


def row_pass(parts, exp, copies):
    rows, width = exp.shape
    out = (copies, rows // LANES, LANES)
    return pl.pallas_call(
        row_kernel,
        grid=(rows // ROWS_BLOCK,),
        in_specs=[whole(parts.shape), pl.BlockSpec((ROWS_BLOCK, width), lambda i: (i, 0))],
        out_specs=whole(out),
        out_shape=f32(*out),
        scratch_shapes=[pltpu.VMEM((1, width), jnp.float32), pltpu.VMEM((rows, LANES), jnp.float32)],
        compiler_params=params(20),
        cost_estimate=cost(2 * exp.size, exp.size * 4),
    )(parts, exp)


def column_pass(parts, exp, copies):
    rows, width = exp.shape
    out = (copies, width // LANES, LANES)
    return pl.pallas_call(
        column_kernel,
        grid=(rows // ROWS_BLOCK,),
        in_specs=[whole(parts.shape), pl.BlockSpec((ROWS_BLOCK, width), lambda i: (i, 0))],
        out_specs=whole(out),
        out_shape=f32(*out),
        scratch_shapes=[pltpu.VMEM((rows, LANES), jnp.float32), pltpu.VMEM((8, width), jnp.float32)],
        compiler_params=params(20),
        cost_estimate=cost(2 * exp.size, exp.size * 4),
    )(parts, exp)


def student_pass(parts, exp, y, v, copies):
    rows, width = exp.shape
    bot = y.shape[1]
    out = (copies, 3 * rows // LANES, LANES)
    return pl.pallas_call(
        student_kernel,
        grid=(rows // TALL_BLOCK,),
        in_specs=[
            whole(parts.shape),
            pl.BlockSpec((TALL_BLOCK, width), lambda i: (i, 0)),
            pl.BlockSpec((TALL_BLOCK, bot), lambda i: (i, 0)),
            whole(v.shape),
        ],
        out_specs=[
            whole(out),
            pl.BlockSpec((TALL_BLOCK, bot), lambda i: (i, 0)),
            pl.BlockSpec((bot, TALL_BLOCK), lambda i: (0, i)),
        ],
        out_shape=[
            f32(*out),
            jax.ShapeDtypeStruct((rows, bot), jnp.bfloat16),
            jax.ShapeDtypeStruct((bot, rows), jnp.bfloat16),
        ],
        scratch_shapes=[
            pltpu.VMEM((1, width), jnp.float32),
            pltpu.VMEM((3, rows, LANES), jnp.float32),
        ],
        compiler_params=params(28),
        cost_estimate=cost(2 * y.size * width, exp.size * 4, exp.size),
    )(parts, hbm(exp), hbm(y), hbm(v))


def gradient_pass(row_parts, col_parts, exp, z, zt, v, y):
    rows, width = exp.shape
    bot = z.shape[1]
    return pl.pallas_call(
        gradient_kernel,
        grid=(width // CHUNK,),
        in_specs=[
            whole(row_parts.shape),
            whole(col_parts.shape),
            pl.BlockSpec((rows, CHUNK), lambda i: (0, i)),
            whole(z.shape),
            whole(zt.shape),
            pl.BlockSpec((bot, CHUNK), lambda i: (0, i)),
            whole(y.shape),
        ],
        out_specs=[
            whole((rows, bot)),
            pl.BlockSpec((bot, CHUNK), lambda i: (0, i)),
            pl.BlockSpec((1, CHUNK), lambda i: (0, i)),
        ],
        out_shape=[
            pltpu.HBM((rows, bot), jnp.float32),
            pltpu.HBM((bot, width), jnp.float32),
            pltpu.HBM((1, width), jnp.float32),
        ],
        scratch_shapes=[
            pltpu.VMEM((width // LANES, LANES), jnp.float32),
            pltpu.VMEM((rows, LANES), jnp.float32),
            pltpu.VMEM((rows, LANES), jnp.float32),
            pltpu.VMEM((rows, CHUNK), jnp.bfloat16),
            pltpu.VMEM((rows, bot), jnp.float32),
        ],
        compiler_params=params(28),
        cost_estimate=cost(6 * z.size * width, exp.size * 4, exp.size),
    )(row_parts, col_parts, exp, z, zt, v, y)


def backward_kernel(sum_ref, y_ref, out_ref):
    y = y_ref[...]
    norm = jnp.sqrt(jnp.sum(y * y, axis=1, keepdims=True) + EPS)
    repeat_out(out_ref, (sum_ref[...] / norm).astype(jnp.bfloat16))


def norm_backward(total, y, copies):
    return pl.pallas_call(
        backward_kernel,
        out_shape=pltpu.HBM((copies,) + y.shape, jnp.bfloat16),
        compiler_params=pltpu.CompilerParams(vmem_limit_bytes=8 * MIB),
    )(total, hbm(y))


def local(hid_teacher, hid_student, proj_teacher, proj_student, proto_teacher, proto_student):
    bot = proj_teacher.shape[1]
    half = proto_teacher.shape[1] // lax.axis_size("yh")
    first = lax.axis_index("yh") * half
    columns, planes = lax.axis_size("z"), lax.axis_size(PLANE)

    gathered = lax.all_gather(proj_student, SHARD, axis=0, tiled=True)
    z_own = unit_split(hid_teacher, proj_teacher, planes)
    z_own, proto_teacher, proto_student = lax.optimization_barrier(
        (z_own, proto_teacher, proto_student)
    )
    z_t = exchange(z_own, PLANE).reshape(-1, bot)
    v_t, v_all, norm_all = unit_columns(
        lax.dynamic_slice_in_dim(proto_teacher, first, half, 1), proto_student
    )
    v_s = lax.dynamic_slice_in_dim(v_all, first, half, 1)
    last = bot // lax.axis_size(DP)
    v_last = lax.dynamic_slice_in_dim(v_all, lax.axis_index(DP) * last, last, 0).astype(jnp.float32)
    z_t, v_t, v_s, v_last = lax.optimization_barrier((z_t, v_t, v_s, v_last))
    y_s = project(hid_student, gathered)
    z_t, y_s, hid_student = lax.optimization_barrier((z_t, y_s, hid_student))
    wide_s = lax.all_gather(y_s, PLANE, axis=0, tiled=True)
    hid_group = lax.all_gather(hid_student, SHARD, axis=0, tiled=True)

    teacher_exp, mass = first_pass(z_t, v_t, columns)
    col_parts = exchange(mass, "z")
    for step in range(ITERS - 1):
        row_parts = exchange(row_pass(col_parts, teacher_exp, planes), PLANE)
        mass = column_pass(row_parts, teacher_exp, columns)
        if step == ITERS - 2:
            mass, wide_s = lax.optimization_barrier((mass, wide_s))
        col_parts = exchange(mass, "z")
    sums, z_s, z_s_t = student_pass(col_parts, teacher_exp, wide_s, v_s, planes)
    sums = exchange(sums, PLANE)
    dy_part, dproto_part, dots = gradient_pass(
        sums, col_parts, teacher_exp, z_s, z_s_t, v_s, wide_s
    )

    dy_part, hid_group, sums = lax.optimization_barrier((dy_part, hid_group, sums))
    row_mass, expsum, cross = jnp.split(jnp.sum(sums, axis=0), 3, axis=0)
    row_count = y_s.shape[0] * lax.axis_size(DP + SHARD)
    loss_part = jnp.sum(jnp.log(expsum) - cross / row_mass / TAU_S) / row_count
    dproto = lax.psum_scatter(dproto_part, "z", scatter_dimension=0, tiled=True)

    parts = (dy_part * WIRE_SCALE).astype(jnp.float16).reshape((planes,) + y_s.shape)
    tangent = jnp.sum(exchange(parts, PLANE).astype(jnp.float32), axis=0) * (1.0 / WIRE_SCALE)
    dy_group = exchange(
        norm_backward(tangent, y_s, lax.axis_size(SHARD)), SHARD
    ).reshape(-1, bot)
    depth = proj_student.shape[0]
    hid_block = lax.dynamic_slice_in_dim(
        hid_group, lax.axis_index(SHARD) * depth, depth, 1
    )
    copies = lax.axis_size(DP)
    height = depth // copies * bot // LANES + 8
    proj_rows = pl.pallas_call(
        rows_kernel,
        out_shape=pltpu.HBM((copies, height, LANES), jnp.float32),
        compiler_params=pltpu.CompilerParams(vmem_limit_bytes=8 * MIB),
    )(hbm(hid_block), hbm(dy_group), hbm(dots))
    collected = pl.pallas_call(
        collect_kernel,
        out_shape=pltpu.HBM((copies, height, LANES), jnp.float32),
        compiler_params=pltpu.CompilerParams(vmem_limit_bytes=8 * MIB),
    )(exchange(proj_rows, DP), loss_part.reshape(1, 1))
    kept, got = swap(dproto)
    grad_proj, grad_proto, loss = pl.pallas_call(
        finish_kernel,
        in_specs=[pl.BlockSpec(memory_space=pltpu.SMEM)]
        + [pl.BlockSpec(memory_space=pltpu.VMEM)] * 5,
        out_shape=[f32(depth, bot), f32(last, 2 * half), f32(1, LANES)],
        compiler_params=pltpu.CompilerParams(vmem_limit_bytes=12 * MIB),
    )(
        lax.axis_index("yh").reshape(1),
        exchange(collected, DP),
        hbm(kept),
        hbm(got),
        hbm(v_last),
        hbm(norm_all),
    )
    return (loss[0, 0], grad_proj, grad_proto)


def solution(mesh):
    fine = Mesh(mesh.devices.reshape(8, 2, 2, 4, 2), DP + SHARD)
    everything = DP + SHARD
    placed = (
        P(everything, None),
        P(everything, None),
        P(SHARD, None),
        P(SHARD, None),
        P(None, SHARD),
        P(None, SHARD),
    )
    return jax.shard_map(
        local,
        mesh=fine,
        in_specs=placed,
        out_specs=(P(), P(SHARD, None), P(DP, SHARD)),
        check_vma=False,
    )
```

```python
import functools

import jax
import jax.numpy as jnp
from jax import lax
from jax.experimental import pallas as pl
from jax.experimental.pallas import tpu as pltpu
from jax.sharding import Mesh, PartitionSpec as P

ITERS = 3
GRAD_SCALE = 256
TAU_T = 0.04
TAU_S = 0.1
EPS = 1e-06
LANES = 128
ROWS_BLOCK = 256
TALL_BLOCK = 512
GRAD_BLOCK = 1024
DEPTH_BLOCK = 1024
CHUNK = 512
MIB = 1024 * 1024
WIRE_SCALE = 4.0
ROW_DIMS = (((0,), (0,)), ((), ()))
COL_DIMS = (((1,), (1,)), ((), ()))

DP = ("z", "yh")
SHARD = ("yl", "x", "c")
PLANE = ("yh", "yl", "x", "c")


def exchange(blocks, axes):
    return lax.all_to_all(blocks, axes, 0, 0, tiled=True)


def over_cores(blocks):
    return lax.ppermute(blocks, "c", [(0, 1), (1, 0)])


def features_kernel(part_ref, got_ref, out_ref):
    y = part_ref[0 : got_ref.shape[0], :] + got_ref[...]
    unit = y / jnp.sqrt(jnp.sum(y * y, axis=1, keepdims=True) + EPS)
    repeat_out(out_ref, unit.astype(jnp.bfloat16))


def unit_split(hidden, weight, copies):
    rows, bot = hidden.shape[0], weight.shape[1]
    kept, sent, repeated = depth_halves(hidden, weight, lax.axis_size(("yl", "x")))
    share = exchange(repeated, ("yl", "x")).reshape(-1, bot)
    both = jnp.concatenate([kept, over_cores(sent)], axis=0)
    part = jnp.dot(both, share, preferred_element_type=jnp.float32)
    return pl.pallas_call(
        features_kernel,
        out_shape=pltpu.HBM((copies, rows, bot), jnp.bfloat16),
        compiler_params=pltpu.CompilerParams(vmem_limit_bytes=8 * MIB),
    )(part, over_cores(part[rows:]))


def shares_kernel(side_ref, block_ref, ready_ref, kept_ref, sent_ref):
    del ready_ref
    rows = kept_ref.shape[0]

    @pl.when(side_ref[0] == 0)
    def _():
        kept_ref[...] = block_ref[0:rows, :]
        sent_ref[...] = block_ref[rows:, :]

    @pl.when(side_ref[0] != 0)
    def _():
        kept_ref[...] = block_ref[rows:, :]
        sent_ref[...] = block_ref[0:rows, :]


def swap(block, ready):
    rows = block.shape[0] // lax.axis_size("yh")
    share = pltpu.HBM((rows, block.shape[1]), jnp.float32)
    kept, sent = pl.pallas_call(
        shares_kernel,
        in_specs=[
            pl.BlockSpec(memory_space=pltpu.SMEM),
            pl.BlockSpec(memory_space=pltpu.VMEM),
            pl.BlockSpec(memory_space=pl.ANY),
        ],
        out_shape=[share, share],
        compiler_params=pltpu.CompilerParams(vmem_limit_bytes=8 * MIB),
    )(lax.axis_index("yh").reshape(1), hbm(block), hbm(ready))
    return kept, lax.ppermute(sent, "yh", [(0, 1), (1, 0)])


def lane_rows(row):
    return jnp.concatenate(
        [row[:, i * LANES : (i + 1) * LANES] for i in range(row.shape[1] // LANES)], axis=0
    )


def one_row(block):
    return jnp.concatenate([block[i : i + 1] for i in range(block.shape[0])], axis=1)


def down(block):
    return jnp.concatenate(
        [
            jnp.broadcast_to(block[i : i + 1], (LANES, LANES)).T
            for i in range(block.shape[0])
        ],
        axis=0,
    )


def lane_sums(wide):
    ones = jnp.ones((8, LANES), jnp.float32)
    row = lax.dot_general(
        ones, wide, COL_DIMS, precision=lax.Precision.HIGHEST, preferred_element_type=jnp.float32
    )
    return lane_rows(row[0:1])


def fold_lanes(wide):
    pieces = [wide[:, i * LANES : (i + 1) * LANES] for i in range(wide.shape[1] // LANES)]
    return functools.reduce(lambda a, b: a + b, pieces)


def fold_rows(tall):
    return jnp.sum(tall.reshape(-1, 8, tall.shape[1]), axis=0)


def repeat_out(out_ref, block):
    out_ref[...] = jnp.broadcast_to(block[None], out_ref.shape)


def unit_kernel(teacher_ref, student_ref, vt_ref, vs_ref, norm_ref):
    def unit(ref, out_ref):
        wide = ref[...].astype(jnp.float32)
        norm = jnp.sqrt(jnp.sum(wide * wide, axis=0, keepdims=True) + EPS)
        out_ref[...] = (wide / norm).astype(jnp.bfloat16)
        return norm

    unit(teacher_ref, vt_ref)
    norm_ref[...] = unit(student_ref, vs_ref)


def halves_kernel(core_ref, hidden_ref, weight_ref, kept_ref, sent_ref, out_ref):
    width = kept_ref.shape[1]
    repeat_out(out_ref, weight_ref[...])

    def split(even_ref, odd_ref):
        for start in range(0, width, LANES):
            cols = slice(start, start + LANES)
            even_ref[:, cols] = hidden_ref[:, 2 * start : 2 * start + LANES]
            odd_ref[:, cols] = hidden_ref[:, 2 * start + LANES : 2 * start + 2 * LANES]

    @pl.when(core_ref[0] == 0)
    def _():
        split(kept_ref, sent_ref)

    @pl.when(core_ref[0] != 0)
    def _():
        split(sent_ref, kept_ref)


def project_kernel(hidden_ref, weight_ref, out_ref):
    @pl.when(pl.program_id(0) == 0)
    def _():
        out_ref[...] = jnp.zeros_like(out_ref)

    out_ref[...] += jnp.dot(hidden_ref[...], weight_ref[...], preferred_element_type=jnp.float32)


def first_kernel(z_ref, v_ref, exp_ref, out_ref, acc):
    step = pl.program_id(0)
    width = v_ref.shape[1]

    @pl.when(step == 0)
    def _():
        acc[...] = jnp.zeros_like(acc)

    for start in range(0, width, CHUNK):
        cols = slice(start, start + CHUNK)
        product = jnp.dot(z_ref[...], v_ref[:, cols], preferred_element_type=jnp.float32)
        block = jnp.exp(product * (1.0 / TAU_T))
        exp_ref[:, cols] = block
        acc[:, cols] += fold_rows(block)

    @pl.when(step == pl.num_programs(0) - 1)
    def _():
        repeat_out(out_ref, lane_rows(jnp.sum(acc[...], axis=0, keepdims=True)))


def row_kernel(parts_ref, exp_ref, out_ref, scale, acc):
    step = pl.program_id(0)

    @pl.when(step == 0)
    def _():
        scale[...] = one_row(1.0 / jnp.sum(parts_ref[...], axis=0))

    rows, width = exp_ref.shape
    block = exp_ref[:, 0:LANES] * scale[:, 0:LANES]
    for start in range(LANES, width, LANES):
        cols = slice(start, start + LANES)
        block += exp_ref[:, cols] * scale[:, cols]
    acc[pl.ds(pl.multiple_of(step * rows, rows), rows), :] = block

    @pl.when(step == pl.num_programs(0) - 1)
    def _():
        repeat_out(out_ref, lane_sums(acc[...]))


def column_kernel(parts_ref, exp_ref, out_ref, scale, acc):
    step = pl.program_id(0)

    @pl.when(step == 0)
    def _():
        scale[...] = down(1.0 / jnp.sum(parts_ref[...], axis=0))
        acc[...] = jnp.zeros_like(acc)

    rows, width = exp_ref.shape
    factor = scale[pl.ds(pl.multiple_of(step * rows, rows), rows), :]
    for start in range(0, width, LANES):
        cols = slice(start, start + LANES)
        acc[:, cols] += fold_rows(exp_ref[:, cols] * factor)

    @pl.when(step == pl.num_programs(0) - 1)
    def _():
        repeat_out(out_ref, lane_rows(jnp.sum(acc[...], axis=0, keepdims=True)))


def student_kernel(parts_ref, exp_ref, y_ref, v_ref, out_ref, z_ref, zt_ref, scale, acc):
    step = pl.program_id(0)

    @pl.when(step == 0)
    def _():
        scale[...] = one_row(1.0 / jnp.sum(parts_ref[...], axis=0))

    rows, width = exp_ref.shape
    here = pl.ds(pl.multiple_of(step * rows, rows), rows)
    y = y_ref[...]
    z = y / jnp.sqrt(jnp.sum(y * y, axis=1, keepdims=True) + EPS)
    z_ref[...] = z.astype(jnp.bfloat16)
    zt_ref[...] = z.T.astype(jnp.bfloat16)
    mass = jnp.zeros((rows, LANES), jnp.float32)
    exps = jnp.zeros((rows, LANES), jnp.float32)
    cross = jnp.zeros((rows, LANES), jnp.float32)
    for start in range(0, width, CHUNK):
        cols = slice(start, start + CHUNK)
        scores = jnp.dot(z_ref[...], v_ref[:, cols], preferred_element_type=jnp.float32)
        weighted = exp_ref[:, cols] * scale[:, cols]
        mass += fold_lanes(weighted)
        exps += fold_lanes(jnp.exp(scores * (1.0 / TAU_S)))
        cross += fold_lanes(weighted * scores)
    acc[0, here, :] = mass
    acc[1, here, :] = exps
    acc[2, here, :] = cross

    @pl.when(step == pl.num_programs(0) - 1)
    def _():
        sums = [lane_sums(acc[i]) for i in range(3)]
        repeat_out(out_ref, jnp.concatenate(sums, axis=0))


def gradient_kernel(
    row_parts_ref, col_parts_ref, exp_ref, z_ref, zt_ref, v_ref, y_ref, dy_ref, dp_ref, dots_ref,
    scale, teacher, student, grad, dz,
):
    step = pl.program_id(0)
    rows, width = exp_ref.shape
    tall = rows // LANES

    @pl.when(step == 0)
    def _():
        sums = jnp.sum(row_parts_ref[...], axis=0)
        factor = GRAD_SCALE / TAU_S
        teacher[...] = down(factor / sums[0:tall])
        student[...] = down(factor / sums[tall : 2 * tall])
        scale[...] = 1.0 / jnp.sum(col_parts_ref[...], axis=0)
        dz[...] = jnp.zeros_like(dz)

    groups = width // LANES
    col = one_row(scale[pl.ds(pl.multiple_of(step * groups, groups), groups), :])
    for start in range(0, rows, GRAD_BLOCK):
        here = slice(start, start + GRAD_BLOCK)
        scores = jnp.dot(z_ref[here, :], v_ref[...], preferred_element_type=jnp.float32)
        prob = jnp.exp(scores * (1.0 / TAU_S))
        for piece in range(0, width, LANES):
            cols = slice(piece, piece + LANES)
            target = exp_ref[here, cols] * col[:, cols] * teacher[here, :]
            grad[here, cols] = (prob[:, cols] * student[here, :] - target).astype(jnp.bfloat16)
        dz[here, :] += lax.dot_general(
            grad[here, :], v_ref[...], COL_DIMS, preferred_element_type=jnp.float32
        )
    dproto = jnp.dot(zt_ref[...], grad[...], preferred_element_type=jnp.float32)
    dp_ref[...] = dproto
    dots_ref[...] = jnp.sum(v_ref[...].astype(jnp.float32) * dproto, axis=0, keepdims=True)

    @pl.when(step == pl.num_programs(0) - 1)
    def _():
        for start in range(0, rows, ROWS_BLOCK):
            here = slice(start, start + ROWS_BLOCK)
            y = y_ref[here, :]
            part = dz[here, :]
            square = jnp.sum(y * y, axis=1, keepdims=True) + EPS
            inner = jnp.sum(y * part, axis=1, keepdims=True)
            dy_ref[here, :] = part - y * (inner / square)


def rows_kernel(hidden_ref, dy_ref, dots_ref, out_ref):
    copies, height = out_ref.shape[:2]
    product = lax.dot_general(
        hidden_ref[...], dy_ref[...], ROW_DIMS, preferred_element_type=jnp.float32
    )
    own, bot = product.shape[0] // copies, product.shape[1]
    for i in range(copies):
        for piece in range(0, bot, LANES):
            row = piece // LANES * own
            out_ref[i, row : row + own, :] = product[
                i * own : (i + 1) * own, piece : piece + LANES
            ]
        dots = dots_ref[:, i * LANES : (i + 1) * LANES]
        tail = height - own * bot // LANES
        out_ref[i, height - tail : height, :] = jnp.broadcast_to(dots, (tail, LANES))


def collect_kernel(parts_ref, loss_ref, ready_ref, out_ref):
    del ready_ref
    copies, height = parts_ref.shape[:2]
    sides = []
    for side in range(2):
        block = parts_ref[side]
        for i in range(2 + side, copies, 2):
            block = block + parts_ref[i]
        sides.append(block)
    head = height - 8
    loss = jnp.broadcast_to(loss_ref[...], (6, LANES))
    tail = [sides[0][head : head + 1], sides[1][head : head + 1], loss]
    repeat_out(
        out_ref, jnp.concatenate([sides[0][0:head] + sides[1][0:head]] + tail, axis=0)
    )


def finish_kernel(
    side_ref, parts_ref, kept_ref, got_ref, v_ref, norm_ref, proj_ref, grad_ref, loss_ref
):
    copies, height = parts_ref.shape[:2]
    rows, bot = proj_ref.shape
    own, width, head = rows // copies, kept_ref.shape[1], height - 8
    for i in range(copies):
        for piece in range(0, bot, LANES):
            row = piece // LANES * own
            proj_ref[i * own : (i + 1) * own, piece : piece + LANES] = parts_ref[
                i, row : row + own, :
            ]
    lines = [
        jnp.concatenate(
            [parts_ref[i, head + side : head + side + 1, :] for i in range(copies)], axis=1
        )
        for side in range(2)
    ]
    loss = parts_ref[0, head + 2 : head + 3, :]
    for i in range(2, copies, 2):
        loss = loss + parts_ref[i, head + 2 : head + 3, :]
    loss_ref[...] = loss

    def write(halves):
        for side in range(2):
            cols = slice(side * width, (side + 1) * width)
            dots = lines[side][:, 0:width]
            grad_ref[:, cols] = (halves[side][...] - v_ref[:, cols] * dots) / norm_ref[:, cols]

    @pl.when(side_ref[0] == 0)
    def _():
        write((kept_ref, got_ref))

    @pl.when(side_ref[0] != 0)
    def _():
        write((got_ref, kept_ref))


def params(mib):
    return pltpu.CompilerParams(
        dimension_semantics=("arbitrary",), vmem_limit_bytes=mib * MIB
    )


def cost(flops, size, exps=0):
    return pl.CostEstimate(flops=flops, bytes_accessed=size, transcendentals=exps)


def whole(shape):
    return pl.BlockSpec(shape, lambda i: (0,) * len(shape))


def f32(*shape):
    return jax.ShapeDtypeStruct(shape, jnp.float32)


def hbm(array):
    return pltpu.with_memory_space_constraint(array, pltpu.HBM)


def unit_columns(teacher, student):
    bot, width = teacher.shape
    step = width // CHUNK
    wide = student.shape[1] // step
    return pl.pallas_call(
        unit_kernel,
        grid=(step,),
        in_specs=[
            pl.BlockSpec((bot, CHUNK), lambda i: (0, i)),
            pl.BlockSpec((bot, wide), lambda i: (0, i)),
        ],
        out_specs=[
            pl.BlockSpec((bot, CHUNK), lambda i: (0, i)),
            pl.BlockSpec((bot, wide), lambda i: (0, i)),
            pl.BlockSpec((1, wide), lambda i: (0, i)),
        ],
        out_shape=[
            jax.ShapeDtypeStruct(teacher.shape, jnp.bfloat16),
            jax.ShapeDtypeStruct(student.shape, jnp.bfloat16),
            f32(1, student.shape[1]),
        ],
        compiler_params=params(20),
        cost_estimate=cost(4 * (teacher.size + student.size), 4 * (teacher.size + student.size)),
    )(teacher, student)


def depth_halves(hidden, weight, copies):
    half = jax.ShapeDtypeStruct((hidden.shape[0], hidden.shape[1] // 2), hidden.dtype)
    return pl.pallas_call(
        halves_kernel,
        in_specs=[pl.BlockSpec(memory_space=pltpu.SMEM)]
        + [pl.BlockSpec(memory_space=pltpu.VMEM)] * 2,
        out_shape=[half, half, pltpu.HBM((copies,) + weight.shape, weight.dtype)],
        compiler_params=pltpu.CompilerParams(vmem_limit_bytes=8 * MIB),
        cost_estimate=cost(0, 4 * hidden.size + 2 * copies * weight.size),
    )(lax.axis_index("c").reshape(1), hbm(hidden), hbm(weight))


def project(hidden, weight):
    rows, depth = hidden.shape
    bot = weight.shape[1]
    return pl.pallas_call(
        project_kernel,
        grid=(depth // DEPTH_BLOCK,),
        in_specs=[
            pl.BlockSpec((rows, DEPTH_BLOCK), lambda i: (0, i)),
            pl.BlockSpec((DEPTH_BLOCK, bot), lambda i: (i, 0)),
        ],
        out_specs=whole((rows, bot)),
        out_shape=f32(rows, bot),
        compiler_params=params(8),
        cost_estimate=cost(2 * rows * weight.size, 2 * (hidden.size + weight.size)),
    )(hidden, hbm(weight))


def first_pass(z, v, copies):
    rows, bot = z.shape
    width = v.shape[1]
    out = (copies, width // LANES, LANES)
    return pl.pallas_call(
        first_kernel,
        grid=(rows // TALL_BLOCK,),
        in_specs=[pl.BlockSpec((TALL_BLOCK, bot), lambda i: (i, 0)), whole(v.shape)],
        out_specs=[pl.BlockSpec((TALL_BLOCK, width), lambda i: (i, 0)), whole(out)],
        out_shape=[f32(rows, width), f32(*out)],
        scratch_shapes=[pltpu.VMEM((8, width), jnp.float32)],
        compiler_params=params(20),
        cost_estimate=cost(2 * z.size * width, rows * width * 4, rows * width),
    )(z, hbm(v))


def row_pass(parts, exp, copies):
    rows, width = exp.shape
    out = (copies, rows // LANES, LANES)
    return pl.pallas_call(
        row_kernel,
        grid=(rows // ROWS_BLOCK,),
        in_specs=[whole(parts.shape), pl.BlockSpec((ROWS_BLOCK, width), lambda i: (i, 0))],
        out_specs=whole(out),
        out_shape=f32(*out),
        scratch_shapes=[pltpu.VMEM((1, width), jnp.float32), pltpu.VMEM((rows, LANES), jnp.float32)],
        compiler_params=params(20),
        cost_estimate=cost(2 * exp.size, exp.size * 4),
    )(parts, exp)


def column_pass(parts, exp, copies):
    rows, width = exp.shape
    out = (copies, width // LANES, LANES)
    return pl.pallas_call(
        column_kernel,
        grid=(rows // ROWS_BLOCK,),
        in_specs=[whole(parts.shape), pl.BlockSpec((ROWS_BLOCK, width), lambda i: (i, 0))],
        out_specs=whole(out),
        out_shape=f32(*out),
        scratch_shapes=[pltpu.VMEM((rows, LANES), jnp.float32), pltpu.VMEM((8, width), jnp.float32)],
        compiler_params=params(20),
        cost_estimate=cost(2 * exp.size, exp.size * 4),
    )(parts, exp)


def student_pass(parts, exp, y, v, copies):
    rows, width = exp.shape
    bot = y.shape[1]
    out = (copies, 3 * rows // LANES, LANES)
    return pl.pallas_call(
        student_kernel,
        grid=(rows // TALL_BLOCK,),
        in_specs=[
            whole(parts.shape),
            pl.BlockSpec((TALL_BLOCK, width), lambda i: (i, 0)),
            pl.BlockSpec((TALL_BLOCK, bot), lambda i: (i, 0)),
            whole(v.shape),
        ],
        out_specs=[
            whole(out),
            pl.BlockSpec((TALL_BLOCK, bot), lambda i: (i, 0)),
            pl.BlockSpec((bot, TALL_BLOCK), lambda i: (0, i)),
        ],
        out_shape=[
            f32(*out),
            jax.ShapeDtypeStruct((rows, bot), jnp.bfloat16),
            jax.ShapeDtypeStruct((bot, rows), jnp.bfloat16),
        ],
        scratch_shapes=[
            pltpu.VMEM((1, width), jnp.float32),
            pltpu.VMEM((3, rows, LANES), jnp.float32),
        ],
        compiler_params=params(28),
        cost_estimate=cost(2 * y.size * width, exp.size * 4, exp.size),
    )(parts, hbm(exp), hbm(y), hbm(v))


def gradient_pass(row_parts, col_parts, exp, z, zt, v, y):
    rows, width = exp.shape
    bot = z.shape[1]
    return pl.pallas_call(
        gradient_kernel,
        grid=(width // CHUNK,),
        in_specs=[
            whole(row_parts.shape),
            whole(col_parts.shape),
            pl.BlockSpec((rows, CHUNK), lambda i: (0, i)),
            whole(z.shape),
            whole(zt.shape),
            pl.BlockSpec((bot, CHUNK), lambda i: (0, i)),
            whole(y.shape),
        ],
        out_specs=[
            whole((rows, bot)),
            pl.BlockSpec((bot, CHUNK), lambda i: (0, i)),
            pl.BlockSpec((1, CHUNK), lambda i: (0, i)),
        ],
        out_shape=[
            pltpu.HBM((rows, bot), jnp.float32),
            pltpu.HBM((bot, width), jnp.float32),
            pltpu.HBM((1, width), jnp.float32),
        ],
        scratch_shapes=[
            pltpu.VMEM((width // LANES, LANES), jnp.float32),
            pltpu.VMEM((rows, LANES), jnp.float32),
            pltpu.VMEM((rows, LANES), jnp.float32),
            pltpu.VMEM((rows, CHUNK), jnp.bfloat16),
            pltpu.VMEM((rows, bot), jnp.float32),
        ],
        compiler_params=params(28),
        cost_estimate=cost(6 * z.size * width, exp.size * 4, exp.size),
    )(row_parts, col_parts, exp, z, zt, v, y)


def backward_kernel(sum_ref, y_ref, out_ref):
    y = y_ref[...]
    norm = jnp.sqrt(jnp.sum(y * y, axis=1, keepdims=True) + EPS)
    repeat_out(out_ref, (sum_ref[...] / norm).astype(jnp.bfloat16))


def norm_backward(total, y, copies):
    return pl.pallas_call(
        backward_kernel,
        out_shape=pltpu.HBM((copies,) + y.shape, jnp.bfloat16),
        compiler_params=pltpu.CompilerParams(vmem_limit_bytes=8 * MIB),
    )(total, hbm(y))


def local(hid_teacher, hid_student, proj_teacher, proj_student, proto_teacher, proto_student):
    bot = proj_teacher.shape[1]
    half = proto_teacher.shape[1] // lax.axis_size("yh")
    first = lax.axis_index("yh") * half
    columns, planes = lax.axis_size("z"), lax.axis_size(PLANE)

    gathered = lax.all_gather(proj_student, SHARD, axis=0, tiled=True)
    z_own = unit_split(hid_teacher, proj_teacher, planes)
    z_own, proto_teacher, proto_student = lax.optimization_barrier(
        (z_own, proto_teacher, proto_student)
    )
    z_t = exchange(z_own, PLANE).reshape(-1, bot)
    v_t, v_all, norm_all = unit_columns(
        lax.dynamic_slice_in_dim(proto_teacher, first, half, 1), proto_student
    )
    v_s = lax.dynamic_slice_in_dim(v_all, first, half, 1)
    last = bot // lax.axis_size(DP)
    v_last = lax.dynamic_slice_in_dim(v_all, lax.axis_index(DP) * last, last, 0).astype(jnp.float32)
    z_t, v_t, v_s, v_last = lax.optimization_barrier((z_t, v_t, v_s, v_last))
    y_s = project(hid_student, gathered)
    z_t, y_s, hid_student = lax.optimization_barrier((z_t, y_s, hid_student))
    wide_s = lax.all_gather(y_s, PLANE, axis=0, tiled=True)
    hid_group = lax.all_gather(hid_student, SHARD, axis=0, tiled=True)

    teacher_exp, mass = first_pass(z_t, v_t, columns)
    col_parts = exchange(mass, "z")
    for step in range(ITERS - 1):
        row_parts = exchange(row_pass(col_parts, teacher_exp, planes), PLANE)
        mass = column_pass(row_parts, teacher_exp, columns)
        if step == ITERS - 2:
            mass, wide_s = lax.optimization_barrier((mass, wide_s))
        col_parts = exchange(mass, "z")
    sums, z_s, z_s_t = student_pass(col_parts, teacher_exp, wide_s, v_s, planes)
    sums = exchange(sums, PLANE)
    dy_part, dproto_part, dots = gradient_pass(
        sums, col_parts, teacher_exp, z_s, z_s_t, v_s, wide_s
    )

    dy_part, hid_group, sums = lax.optimization_barrier((dy_part, hid_group, sums))
    row_mass, expsum, cross = jnp.split(jnp.sum(sums, axis=0), 3, axis=0)
    row_count = y_s.shape[0] * lax.axis_size(DP + SHARD)
    loss_part = jnp.sum(jnp.log(expsum) - cross / row_mass / TAU_S) / row_count
    dproto = lax.psum_scatter(dproto_part, "z", scatter_dimension=0, tiled=True)

    parts = (dy_part * WIRE_SCALE).astype(jnp.float16).reshape((planes,) + y_s.shape)
    tangent = jnp.sum(exchange(parts, PLANE).astype(jnp.float32), axis=0) * (1.0 / WIRE_SCALE)
    dy_group = exchange(
        norm_backward(tangent, y_s, lax.axis_size(SHARD)), SHARD
    ).reshape(-1, bot)
    depth = proj_student.shape[0]
    hid_block = lax.dynamic_slice_in_dim(
        hid_group, lax.axis_index(SHARD) * depth, depth, 1
    )
    copies = lax.axis_size(DP)
    height = depth // copies * bot // LANES + 8
    proj_rows = pl.pallas_call(
        rows_kernel,
        out_shape=pltpu.HBM((copies, height, LANES), jnp.float32),
        compiler_params=pltpu.CompilerParams(vmem_limit_bytes=8 * MIB),
    )(hbm(hid_block), hbm(dy_group), hbm(dots))
    kept, got = swap(dproto, proj_rows)
    collected = pl.pallas_call(
        collect_kernel,
        in_specs=[pl.BlockSpec(memory_space=pltpu.VMEM)] * 2
        + [pl.BlockSpec(memory_space=pl.ANY)],
        out_shape=f32(copies, height, LANES),
        compiler_params=pltpu.CompilerParams(vmem_limit_bytes=8 * MIB),
    )(exchange(proj_rows, DP), loss_part.reshape(1, 1), hbm(got))
    grad_proj, grad_proto, loss = pl.pallas_call(
        finish_kernel,
        in_specs=[pl.BlockSpec(memory_space=pltpu.SMEM)]
        + [pl.BlockSpec(memory_space=pltpu.VMEM)] * 5,
        out_shape=[f32(depth, bot), f32(last, 2 * half), f32(1, LANES)],
        compiler_params=pltpu.CompilerParams(vmem_limit_bytes=12 * MIB),
    )(
        lax.axis_index("yh").reshape(1),
        exchange(collected, DP),
        hbm(kept),
        hbm(got),
        hbm(v_last),
        hbm(norm_all),
    )
    return (loss[0, 0], grad_proj, grad_proto)


def solution(mesh):
    fine = Mesh(mesh.devices.reshape(8, 2, 2, 4, 2), DP + SHARD)
    everything = DP + SHARD
    placed = (
        P(everything, None),
        P(everything, None),
        P(SHARD, None),
        P(SHARD, None),
        P(None, SHARD),
        P(None, SHARD),
    )
    return jax.shard_map(
        local,
        mesh=fine,
        in_specs=placed,
        out_specs=(P(), P(SHARD, None), P(DP, SHARD)),
        check_vma=False,
    )
```

```python
import functools

import jax
import jax.numpy as jnp
from jax import lax
from jax.experimental import pallas as pl
from jax.experimental.pallas import tpu as pltpu
from jax.sharding import Mesh, PartitionSpec as P

ITERS = 3
GRAD_SCALE = 256
TAU_T = 0.04
TAU_S = 0.1
EPS = 1e-06
LANES = 128
ROWS_BLOCK = 256
TALL_BLOCK = 512
GRAD_BLOCK = 1024
DEPTH_BLOCK = 1024
CHUNK = 512
MIB = 1024 * 1024
WIRE_SCALE = 4.0
ROW_DIMS = (((0,), (0,)), ((), ()))
COL_DIMS = (((1,), (1,)), ((), ()))

DP = ("z", "yh")
SHARD = ("yl", "x", "c")
PLANE = ("yh", "yl", "x", "c")


def exchange(blocks, axes):
    return lax.all_to_all(blocks, axes, 0, 0, tiled=True)


def over_cores(blocks):
    return lax.ppermute(blocks, "c", [(0, 1), (1, 0)])


def features_kernel(part_ref, got_ref, out_ref):
    y = part_ref[0 : got_ref.shape[0], :] + got_ref[...]
    unit = y / jnp.sqrt(jnp.sum(y * y, axis=1, keepdims=True) + EPS)
    repeat_out(out_ref, unit.astype(jnp.bfloat16))


def unit_split(hidden, weight, copies):
    rows, bot = hidden.shape[0], weight.shape[1]
    kept, sent, repeated = depth_halves(hidden, weight, lax.axis_size(("yl", "x")))
    share = exchange(repeated, ("yl", "x")).reshape(-1, bot)
    both = jnp.concatenate([kept, over_cores(sent)], axis=0)
    part = jnp.dot(both, share, preferred_element_type=jnp.float32)
    return pl.pallas_call(
        features_kernel,
        out_shape=pltpu.HBM((copies, rows, bot), jnp.bfloat16),
        compiler_params=pltpu.CompilerParams(vmem_limit_bytes=8 * MIB),
    )(part, over_cores(part[rows:]))


def swap(block):
    side = lax.axis_index("yh")
    rows = block.shape[0] // lax.axis_size("yh")
    kept = lax.dynamic_slice_in_dim(block, side * rows, rows, 0)
    sent = lax.dynamic_slice_in_dim(block, (1 - side) * rows, rows, 0)
    return kept, lax.ppermute(sent, "yh", [(0, 1), (1, 0)])


def lane_rows(row):
    return jnp.concatenate(
        [row[:, i * LANES : (i + 1) * LANES] for i in range(row.shape[1] // LANES)], axis=0
    )


def one_row(block):
    return jnp.concatenate([block[i : i + 1] for i in range(block.shape[0])], axis=1)


def down(block):
    return jnp.concatenate(
        [
            jnp.broadcast_to(block[i : i + 1], (LANES, LANES)).T
            for i in range(block.shape[0])
        ],
        axis=0,
    )


def lane_sums(wide):
    ones = jnp.ones((8, LANES), jnp.float32)
    row = lax.dot_general(
        ones, wide, COL_DIMS, precision=lax.Precision.HIGHEST, preferred_element_type=jnp.float32
    )
    return lane_rows(row[0:1])


def fold_lanes(wide):
    pieces = [wide[:, i * LANES : (i + 1) * LANES] for i in range(wide.shape[1] // LANES)]
    return functools.reduce(lambda a, b: a + b, pieces)


def fold_rows(tall):
    return jnp.sum(tall.reshape(-1, 8, tall.shape[1]), axis=0)


def repeat_out(out_ref, block):
    out_ref[...] = jnp.broadcast_to(block[None], out_ref.shape)


def unit_kernel(teacher_ref, student_ref, vt_ref, vs_ref, norm_ref):
    def unit(ref, out_ref):
        wide = ref[...].astype(jnp.float32)
        norm = jnp.sqrt(jnp.sum(wide * wide, axis=0, keepdims=True) + EPS)
        out_ref[...] = (wide / norm).astype(jnp.bfloat16)
        return norm

    unit(teacher_ref, vt_ref)
    norm_ref[...] = unit(student_ref, vs_ref)


def halves_kernel(core_ref, hidden_ref, weight_ref, kept_ref, sent_ref, out_ref):
    width = kept_ref.shape[1]
    repeat_out(out_ref, weight_ref[...])

    def split(even_ref, odd_ref):
        for start in range(0, width, LANES):
            cols = slice(start, start + LANES)
            even_ref[:, cols] = hidden_ref[:, 2 * start : 2 * start + LANES]
            odd_ref[:, cols] = hidden_ref[:, 2 * start + LANES : 2 * start + 2 * LANES]

    @pl.when(core_ref[0] == 0)
    def _():
        split(kept_ref, sent_ref)

    @pl.when(core_ref[0] != 0)
    def _():
        split(sent_ref, kept_ref)


def project_kernel(hidden_ref, weight_ref, out_ref):
    @pl.when(pl.program_id(0) == 0)
    def _():
        out_ref[...] = jnp.zeros_like(out_ref)

    out_ref[...] += jnp.dot(hidden_ref[...], weight_ref[...], preferred_element_type=jnp.float32)


def first_kernel(z_ref, v_ref, exp_ref, out_ref, acc):
    step = pl.program_id(0)
    width = v_ref.shape[1]

    @pl.when(step == 0)
    def _():
        acc[...] = jnp.zeros_like(acc)

    for start in range(0, width, CHUNK):
        cols = slice(start, start + CHUNK)
        product = jnp.dot(z_ref[...], v_ref[:, cols], preferred_element_type=jnp.float32)
        block = jnp.exp(product * (1.0 / TAU_T))
        exp_ref[:, cols] = block
        acc[:, cols] += fold_rows(block)

    @pl.when(step == pl.num_programs(0) - 1)
    def _():
        repeat_out(out_ref, lane_rows(jnp.sum(acc[...], axis=0, keepdims=True)))


def row_kernel(parts_ref, exp_ref, out_ref, scale, acc):
    step = pl.program_id(0)

    @pl.when(step == 0)
    def _():
        scale[...] = one_row(1.0 / jnp.sum(parts_ref[...], axis=0))

    rows, width = exp_ref.shape
    block = exp_ref[:, 0:LANES] * scale[:, 0:LANES]
    for start in range(LANES, width, LANES):
        cols = slice(start, start + LANES)
        block += exp_ref[:, cols] * scale[:, cols]
    acc[pl.ds(pl.multiple_of(step * rows, rows), rows), :] = block

    @pl.when(step == pl.num_programs(0) - 1)
    def _():
        repeat_out(out_ref, lane_sums(acc[...]))


def column_kernel(parts_ref, exp_ref, out_ref, scale, acc):
    step = pl.program_id(0)

    @pl.when(step == 0)
    def _():
        scale[...] = down(1.0 / jnp.sum(parts_ref[...], axis=0))
        acc[...] = jnp.zeros_like(acc)

    rows, width = exp_ref.shape
    factor = scale[pl.ds(pl.multiple_of(step * rows, rows), rows), :]
    for start in range(0, width, LANES):
        cols = slice(start, start + LANES)
        acc[:, cols] += fold_rows(exp_ref[:, cols] * factor)

    @pl.when(step == pl.num_programs(0) - 1)
    def _():
        repeat_out(out_ref, lane_rows(jnp.sum(acc[...], axis=0, keepdims=True)))


def student_kernel(parts_ref, exp_ref, y_ref, v_ref, out_ref, z_ref, zt_ref, scale, acc):
    step = pl.program_id(0)

    @pl.when(step == 0)
    def _():
        scale[...] = one_row(1.0 / jnp.sum(parts_ref[...], axis=0))

    rows, width = exp_ref.shape
    here = pl.ds(pl.multiple_of(step * rows, rows), rows)
    y = y_ref[...]
    z = y / jnp.sqrt(jnp.sum(y * y, axis=1, keepdims=True) + EPS)
    z_ref[...] = z.astype(jnp.bfloat16)
    zt_ref[...] = z.T.astype(jnp.bfloat16)
    mass = jnp.zeros((rows, LANES), jnp.float32)
    exps = jnp.zeros((rows, LANES), jnp.float32)
    cross = jnp.zeros((rows, LANES), jnp.float32)
    for start in range(0, width, CHUNK):
        cols = slice(start, start + CHUNK)
        scores = jnp.dot(z_ref[...], v_ref[:, cols], preferred_element_type=jnp.float32)
        weighted = exp_ref[:, cols] * scale[:, cols]
        mass += fold_lanes(weighted)
        exps += fold_lanes(jnp.exp(scores * (1.0 / TAU_S)))
        cross += fold_lanes(weighted * scores)
    acc[0, here, :] = mass
    acc[1, here, :] = exps
    acc[2, here, :] = cross

    @pl.when(step == pl.num_programs(0) - 1)
    def _():
        sums = [lane_sums(acc[i]) for i in range(3)]
        repeat_out(out_ref, jnp.concatenate(sums, axis=0))


def gradient_kernel(
    row_parts_ref, col_parts_ref, exp_ref, z_ref, zt_ref, v_ref, y_ref, dy_ref, dp_ref, dots_ref,
    scale, teacher, student, grad, dz,
):
    step = pl.program_id(0)
    rows, width = exp_ref.shape
    tall = rows // LANES

    @pl.when(step == 0)
    def _():
        sums = jnp.sum(row_parts_ref[...], axis=0)
        factor = GRAD_SCALE / TAU_S
        teacher[...] = down(factor / sums[0:tall])
        student[...] = down(factor / sums[tall : 2 * tall])
        scale[...] = 1.0 / jnp.sum(col_parts_ref[...], axis=0)
        dz[...] = jnp.zeros_like(dz)

    groups = width // LANES
    col = one_row(scale[pl.ds(pl.multiple_of(step * groups, groups), groups), :])
    for start in range(0, rows, GRAD_BLOCK):
        here = slice(start, start + GRAD_BLOCK)
        scores = jnp.dot(z_ref[here, :], v_ref[...], preferred_element_type=jnp.float32)
        prob = jnp.exp(scores * (1.0 / TAU_S))
        for piece in range(0, width, LANES):
            cols = slice(piece, piece + LANES)
            target = exp_ref[here, cols] * col[:, cols] * teacher[here, :]
            grad[here, cols] = (prob[:, cols] * student[here, :] - target).astype(jnp.bfloat16)
        dz[here, :] += lax.dot_general(
            grad[here, :], v_ref[...], COL_DIMS, preferred_element_type=jnp.float32
        )
    dproto = jnp.dot(zt_ref[...], grad[...], preferred_element_type=jnp.float32)
    dp_ref[...] = dproto
    dots_ref[...] = jnp.sum(v_ref[...].astype(jnp.float32) * dproto, axis=0, keepdims=True)

    @pl.when(step == pl.num_programs(0) - 1)
    def _():
        for start in range(0, rows, ROWS_BLOCK):
            here = slice(start, start + ROWS_BLOCK)
            y = y_ref[here, :]
            part = dz[here, :]
            square = jnp.sum(y * y, axis=1, keepdims=True) + EPS
            inner = jnp.sum(y * part, axis=1, keepdims=True)
            dy_ref[here, :] = part - y * (inner / square)


def rows_kernel(hidden_ref, dy_ref, dots_ref, out_ref):
    copies, height = out_ref.shape[:2]
    product = lax.dot_general(
        hidden_ref[...], dy_ref[...], ROW_DIMS, preferred_element_type=jnp.float32
    )
    own, bot = product.shape[0] // copies, product.shape[1]
    for i in range(copies):
        for piece in range(0, bot, LANES):
            row = piece // LANES * own
            out_ref[i, row : row + own, :] = product[
                i * own : (i + 1) * own, piece : piece + LANES
            ]
        dots = dots_ref[:, i * LANES : (i + 1) * LANES]
        tail = height - own * bot // LANES
        out_ref[i, height - tail : height, :] = jnp.broadcast_to(dots, (tail, LANES))


def collect_kernel(parts_ref, loss_ref, out_ref):
    copies, height = parts_ref.shape[:2]
    sides = []
    for side in range(2):
        block = parts_ref[side]
        for i in range(2 + side, copies, 2):
            block = block + parts_ref[i]
        sides.append(block)
    head = height - 8
    loss = jnp.broadcast_to(loss_ref[...], (6, LANES))
    tail = [sides[0][head : head + 1], sides[1][head : head + 1], loss]
    repeat_out(
        out_ref, jnp.concatenate([sides[0][0:head] + sides[1][0:head]] + tail, axis=0)
    )


def finish_kernel(
    side_ref, parts_ref, kept_ref, got_ref, v_ref, norm_ref, proj_ref, grad_ref, loss_ref
):
    copies, height = parts_ref.shape[:2]
    rows, bot = proj_ref.shape
    own, width, head = rows // copies, kept_ref.shape[1], height - 8
    for i in range(copies):
        for piece in range(0, bot, LANES):
            row = piece // LANES * own
            proj_ref[i * own : (i + 1) * own, piece : piece + LANES] = parts_ref[
                i, row : row + own, :
            ]
    lines = [
        jnp.concatenate(
            [parts_ref[i, head + side : head + side + 1, :] for i in range(copies)], axis=1
        )
        for side in range(2)
    ]
    loss = parts_ref[0, head + 2 : head + 3, :]
    for i in range(2, copies, 2):
        loss = loss + parts_ref[i, head + 2 : head + 3, :]
    loss_ref[...] = loss

    def write(halves):
        for side in range(2):
            cols = slice(side * width, (side + 1) * width)
            dots = lines[side][:, 0:width]
            grad_ref[:, cols] = (halves[side][...] - v_ref[:, cols] * dots) / norm_ref[:, cols]

    @pl.when(side_ref[0] == 0)
    def _():
        write((kept_ref, got_ref))

    @pl.when(side_ref[0] != 0)
    def _():
        write((got_ref, kept_ref))


def params(mib):
    return pltpu.CompilerParams(
        dimension_semantics=("arbitrary",), vmem_limit_bytes=mib * MIB
    )


def cost(flops, size, exps=0):
    return pl.CostEstimate(flops=flops, bytes_accessed=size, transcendentals=exps)


def whole(shape):
    return pl.BlockSpec(shape, lambda i: (0,) * len(shape))


def f32(*shape):
    return jax.ShapeDtypeStruct(shape, jnp.float32)


def hbm(array):
    return pltpu.with_memory_space_constraint(array, pltpu.HBM)


def unit_columns(teacher, student):
    bot, width = teacher.shape
    step = width // CHUNK
    wide = student.shape[1] // step
    return pl.pallas_call(
        unit_kernel,
        grid=(step,),
        in_specs=[
            pl.BlockSpec((bot, CHUNK), lambda i: (0, i)),
            pl.BlockSpec((bot, wide), lambda i: (0, i)),
        ],
        out_specs=[
            pl.BlockSpec((bot, CHUNK), lambda i: (0, i)),
            pl.BlockSpec((bot, wide), lambda i: (0, i)),
            pl.BlockSpec((1, wide), lambda i: (0, i)),
        ],
        out_shape=[
            jax.ShapeDtypeStruct(teacher.shape, jnp.bfloat16),
            jax.ShapeDtypeStruct(student.shape, jnp.bfloat16),
            f32(1, student.shape[1]),
        ],
        compiler_params=params(20),
        cost_estimate=cost(4 * (teacher.size + student.size), 4 * (teacher.size + student.size)),
    )(teacher, student)


def depth_halves(hidden, weight, copies):
    half = jax.ShapeDtypeStruct((hidden.shape[0], hidden.shape[1] // 2), hidden.dtype)
    return pl.pallas_call(
        halves_kernel,
        in_specs=[pl.BlockSpec(memory_space=pltpu.SMEM)]
        + [pl.BlockSpec(memory_space=pltpu.VMEM)] * 2,
        out_shape=[half, half, pltpu.HBM((copies,) + weight.shape, weight.dtype)],
        compiler_params=pltpu.CompilerParams(vmem_limit_bytes=8 * MIB),
        cost_estimate=cost(0, 4 * hidden.size + 2 * copies * weight.size),
    )(lax.axis_index("c").reshape(1), hbm(hidden), hbm(weight))


def project(hidden, weight):
    rows, depth = hidden.shape
    bot = weight.shape[1]
    return pl.pallas_call(
        project_kernel,
        grid=(depth // DEPTH_BLOCK,),
        in_specs=[
            pl.BlockSpec((rows, DEPTH_BLOCK), lambda i: (0, i)),
            pl.BlockSpec((DEPTH_BLOCK, bot), lambda i: (i, 0)),
        ],
        out_specs=whole((rows, bot)),
        out_shape=f32(rows, bot),
        compiler_params=params(8),
        cost_estimate=cost(2 * rows * weight.size, 2 * (hidden.size + weight.size)),
    )(hidden, hbm(weight))


def first_pass(z, v, copies):
    rows, bot = z.shape
    width = v.shape[1]
    out = (copies, width // LANES, LANES)
    return pl.pallas_call(
        first_kernel,
        grid=(rows // TALL_BLOCK,),
        in_specs=[pl.BlockSpec((TALL_BLOCK, bot), lambda i: (i, 0)), whole(v.shape)],
        out_specs=[pl.BlockSpec((TALL_BLOCK, width), lambda i: (i, 0)), whole(out)],
        out_shape=[f32(rows, width), f32(*out)],
        scratch_shapes=[pltpu.VMEM((8, width), jnp.float32)],
        compiler_params=params(20),
        cost_estimate=cost(2 * z.size * width, rows * width * 4, rows * width),
    )(z, hbm(v))


def row_pass(parts, exp, copies):
    rows, width = exp.shape
    out = (copies, rows // LANES, LANES)
    return pl.pallas_call(
        row_kernel,
        grid=(rows // ROWS_BLOCK,),
        in_specs=[whole(parts.shape), pl.BlockSpec((ROWS_BLOCK, width), lambda i: (i, 0))],
        out_specs=whole(out),
        out_shape=f32(*out),
        scratch_shapes=[pltpu.VMEM((1, width), jnp.float32), pltpu.VMEM((rows, LANES), jnp.float32)],
        compiler_params=params(20),
        cost_estimate=cost(2 * exp.size, exp.size * 4),
    )(parts, exp)


def column_pass(parts, exp, copies):
    rows, width = exp.shape
    out = (copies, width // LANES, LANES)
    return pl.pallas_call(
        column_kernel,
        grid=(rows // ROWS_BLOCK,),
        in_specs=[whole(parts.shape), pl.BlockSpec((ROWS_BLOCK, width), lambda i: (i, 0))],
        out_specs=whole(out),
        out_shape=f32(*out),
        scratch_shapes=[pltpu.VMEM((rows, LANES), jnp.float32), pltpu.VMEM((8, width), jnp.float32)],
        compiler_params=params(20),
        cost_estimate=cost(2 * exp.size, exp.size * 4),
    )(parts, exp)


def student_pass(parts, exp, y, v, copies):
    rows, width = exp.shape
    bot = y.shape[1]
    out = (copies, 3 * rows // LANES, LANES)
    return pl.pallas_call(
        student_kernel,
        grid=(rows // TALL_BLOCK,),
        in_specs=[
            whole(parts.shape),
            pl.BlockSpec((TALL_BLOCK, width), lambda i: (i, 0)),
            pl.BlockSpec((TALL_BLOCK, bot), lambda i: (i, 0)),
            whole(v.shape),
        ],
        out_specs=[
            whole(out),
            pl.BlockSpec((TALL_BLOCK, bot), lambda i: (i, 0)),
            pl.BlockSpec((bot, TALL_BLOCK), lambda i: (0, i)),
        ],
        out_shape=[
            f32(*out),
            jax.ShapeDtypeStruct((rows, bot), jnp.bfloat16),
            jax.ShapeDtypeStruct((bot, rows), jnp.bfloat16),
        ],
        scratch_shapes=[
            pltpu.VMEM((1, width), jnp.float32),
            pltpu.VMEM((3, rows, LANES), jnp.float32),
        ],
        compiler_params=params(28),
        cost_estimate=cost(2 * y.size * width, exp.size * 4, exp.size),
    )(parts, hbm(exp), hbm(y), hbm(v))


def gradient_pass(row_parts, col_parts, exp, z, zt, v, y):
    rows, width = exp.shape
    bot = z.shape[1]
    return pl.pallas_call(
        gradient_kernel,
        grid=(width // CHUNK,),
        in_specs=[
            whole(row_parts.shape),
            whole(col_parts.shape),
            pl.BlockSpec((rows, CHUNK), lambda i: (0, i)),
            whole(z.shape),
            whole(zt.shape),
            pl.BlockSpec((bot, CHUNK), lambda i: (0, i)),
            whole(y.shape),
        ],
        out_specs=[
            whole((rows, bot)),
            pl.BlockSpec((bot, CHUNK), lambda i: (0, i)),
            pl.BlockSpec((1, CHUNK), lambda i: (0, i)),
        ],
        out_shape=[
            pltpu.HBM((rows, bot), jnp.float32),
            pltpu.HBM((bot, width), jnp.float32),
            pltpu.HBM((1, width), jnp.float32),
        ],
        scratch_shapes=[
            pltpu.VMEM((width // LANES, LANES), jnp.float32),
            pltpu.VMEM((rows, LANES), jnp.float32),
            pltpu.VMEM((rows, LANES), jnp.float32),
            pltpu.VMEM((rows, CHUNK), jnp.bfloat16),
            pltpu.VMEM((rows, bot), jnp.float32),
        ],
        compiler_params=params(28),
        cost_estimate=cost(6 * z.size * width, exp.size * 4, exp.size),
    )(row_parts, col_parts, hbm(exp), z, zt, v, y)


def backward_kernel(sum_ref, y_ref, out_ref):
    y = y_ref[...]
    norm = jnp.sqrt(jnp.sum(y * y, axis=1, keepdims=True) + EPS)
    repeat_out(out_ref, (sum_ref[...] / norm).astype(jnp.bfloat16))


def norm_backward(total, y, copies):
    return pl.pallas_call(
        backward_kernel,
        out_shape=pltpu.HBM((copies,) + y.shape, jnp.bfloat16),
        compiler_params=pltpu.CompilerParams(vmem_limit_bytes=8 * MIB),
    )(total, hbm(y))


def local(hid_teacher, hid_student, proj_teacher, proj_student, proto_teacher, proto_student):
    bot = proj_teacher.shape[1]
    half = proto_teacher.shape[1] // lax.axis_size("yh")
    first = lax.axis_index("yh") * half
    columns, planes = lax.axis_size("z"), lax.axis_size(PLANE)

    gathered = lax.all_gather(proj_student, SHARD, axis=0, tiled=True)
    z_own = unit_split(hid_teacher, proj_teacher, planes)
    z_own, proto_teacher, proto_student = lax.optimization_barrier(
        (z_own, proto_teacher, proto_student)
    )
    z_t = exchange(z_own, PLANE).reshape(-1, bot)
    v_t, v_all, norm_all = unit_columns(
        lax.dynamic_slice_in_dim(proto_teacher, first, half, 1), proto_student
    )
    v_s = lax.dynamic_slice_in_dim(v_all, first, half, 1)
    last = bot // lax.axis_size(DP)
    v_last = lax.dynamic_slice_in_dim(v_all, lax.axis_index(DP) * last, last, 0).astype(jnp.float32)
    z_t, v_t, v_s, v_last = lax.optimization_barrier((z_t, v_t, v_s, v_last))
    y_s = project(hid_student, gathered)
    z_t, y_s, hid_student = lax.optimization_barrier((z_t, y_s, hid_student))
    wide_s = lax.all_gather(y_s, PLANE, axis=0, tiled=True)
    hid_group = lax.all_gather(hid_student, SHARD, axis=0, tiled=True)

    teacher_exp, mass = first_pass(z_t, v_t, columns)
    col_parts = exchange(mass, "z")
    for step in range(ITERS - 1):
        row_parts = exchange(row_pass(col_parts, teacher_exp, planes), PLANE)
        mass = column_pass(row_parts, teacher_exp, columns)
        if step == ITERS - 2:
            mass, wide_s = lax.optimization_barrier((mass, wide_s))
        col_parts = exchange(mass, "z")
    sums, z_s, z_s_t = student_pass(col_parts, teacher_exp, wide_s, v_s, planes)
    sums = exchange(sums, PLANE)
    dy_part, dproto_part, dots = gradient_pass(
        sums, col_parts, teacher_exp, z_s, z_s_t, v_s, wide_s
    )

    dy_part, hid_group, sums = lax.optimization_barrier((dy_part, hid_group, sums))
    row_mass, expsum, cross = jnp.split(jnp.sum(sums, axis=0), 3, axis=0)
    row_count = y_s.shape[0] * lax.axis_size(DP + SHARD)
    loss_part = jnp.sum(jnp.log(expsum) - cross / row_mass / TAU_S) / row_count
    dproto = lax.psum_scatter(dproto_part, "z", scatter_dimension=0, tiled=True)

    parts = (dy_part * WIRE_SCALE).astype(jnp.float16).reshape((planes,) + y_s.shape)
    tangent = jnp.sum(exchange(parts, PLANE).astype(jnp.float32), axis=0) * (1.0 / WIRE_SCALE)
    dy_group = exchange(
        norm_backward(tangent, y_s, lax.axis_size(SHARD)), SHARD
    ).reshape(-1, bot)
    depth = proj_student.shape[0]
    hid_block = lax.dynamic_slice_in_dim(
        hid_group, lax.axis_index(SHARD) * depth, depth, 1
    )
    copies = lax.axis_size(DP)
    height = depth // copies * bot // LANES + 8
    proj_rows = pl.pallas_call(
        rows_kernel,
        out_shape=pltpu.HBM((copies, height, LANES), jnp.float32),
        compiler_params=pltpu.CompilerParams(vmem_limit_bytes=8 * MIB),
    )(hbm(hid_block), hbm(dy_group), hbm(dots))
    collected = pl.pallas_call(
        collect_kernel,
        out_shape=pltpu.HBM((copies, height, LANES), jnp.float32),
        compiler_params=pltpu.CompilerParams(vmem_limit_bytes=8 * MIB),
    )(exchange(proj_rows, DP), loss_part.reshape(1, 1))
    kept, got = swap(dproto)
    grad_proj, grad_proto, loss = pl.pallas_call(
        finish_kernel,
        in_specs=[pl.BlockSpec(memory_space=pltpu.SMEM)]
        + [pl.BlockSpec(memory_space=pltpu.VMEM)] * 5,
        out_shape=[f32(depth, bot), f32(last, 2 * half), f32(1, LANES)],
        compiler_params=pltpu.CompilerParams(vmem_limit_bytes=12 * MIB),
    )(
        lax.axis_index("yh").reshape(1),
        exchange(collected, DP),
        hbm(kept),
        hbm(got),
        hbm(v_last),
        hbm(norm_all),
    )
    return (loss[0, 0], grad_proj, grad_proto)


def solution(mesh):
    fine = Mesh(mesh.devices.reshape(8, 2, 2, 4, 2), DP + SHARD)
    everything = DP + SHARD
    placed = (
        P(everything, None),
        P(everything, None),
        P(SHARD, None),
        P(SHARD, None),
        P(None, SHARD),
        P(None, SHARD),
    )
    return jax.shard_map(
        local,
        mesh=fine,
        in_specs=placed,
        out_specs=(P(), P(SHARD, None), P(DP, SHARD)),
        check_vma=False,
    )
```
